256 devices in a mesh: exp: 16 (over z, core), trow: 4 (over y), tcol: 4 (over x).
Axes of the slice: x: 4, y: 4, z: 8, core: 2. Of those that a mesh axis runs over, the one named last changes fastest.
Arguments:
- stamps: bfloat16 [32, 1536, 1536], P('exp', 'trow', 'tcol'), may hold values from -6 to 6
- footprint: int32 [32, 4], P('exp'), may hold values from 0 to 4, as said below
- psf_anchor: int32 [32, 2], P('exp'), may hold values from 0 to 1535
- psf_degree: int32 [32], P('exp'), may hold values from 1 to 3
- psf_powers: int32 [32, 10, 2], P('exp'), may hold values from 0 to 3, as said below
- psf_basis: float32 [32, 10, 1024], P('exp'), may hold values from -0.1875 to 0.1875
- flux: float32 [32], P('exp'), may hold values from 0.1 to 0.4
- variance: float32 [32], P('exp'), may hold values from 0.5 to 2
Outputs:
- coadd: float32 [4, 384, 1536], P('trow', 'exp', 'tcol')
The draws below stay inside these ranges and needn't reach their ends.
Inputs may be any that keep to these rules, and one draw needn't show every extreme that they name: `footprint`: each row is a rectangle of tiles with row_lo < row_hi and col_lo < col_hi; for each g, exposures 2g and 2g + 1 (the two held by one device along `exp`) both cover at least one common tile. `psf_powers`: each exposure's rows are the ten pairs (p, q) with p + q <= 3, each once.
All inputs are finite; a program needn't handle non-finite values.
Results may differ from the reference program's by a relative error of at most 0.0068.
Values may be sent and summed in bfloat16 or wider, within the bound.
A program may use at most 192 MiB of HBM per device.

```python
import math
import jax
import jax.numpy as jnp
from jax import lax

TILE = 512
HALO = 64
PS = 32
NBASIS = 10
EXP_DEV = 2
CORE = 384
EXPOSURES = 32
N_TROW = 4
N_TCOL = 4


def draw_footprint(key, part):
    key = jax.random.fold_in(key, 11)
    keys = jax.random.split(key, 6)
    groups = EXPOSURES // EXP_DEV
    centre_row = jnp.repeat(jax.random.randint(keys[0], (groups,), 0, N_TROW), EXP_DEV)
    centre_col = jnp.repeat(jax.random.randint(keys[1], (groups,), 0, N_TCOL), EXP_DEV)
    row_lo = jax.random.randint(keys[2], (EXPOSURES,), 0, centre_row + 1)
    row_hi = jax.random.randint(keys[3], (EXPOSURES,), centre_row + 1, N_TROW + 1)
    col_lo = jax.random.randint(keys[4], (EXPOSURES,), 0, centre_col + 1)
    col_hi = jax.random.randint(keys[5], (EXPOSURES,), centre_col + 1, N_TCOL + 1)
    return jnp.stack([row_lo, row_hi, col_lo, col_hi], axis=1).astype(jnp.int32)


def draw_psf_powers(key, part):
    key = jax.random.fold_in(key, 23)
    table = jnp.array([[0, 0], [1, 0], [0, 1], [2, 0], [1, 1], [0, 2], [3, 0], [2, 1], [1, 2], [0, 3]], jnp.int32)
    keys = jax.random.split(key, EXPOSURES)
    orders = jax.vmap(lambda k: jax.random.permutation(k, NBASIS))(keys)
    return table[orders].astype(jnp.int32)


def touch_ends(values, rng, smallest, largest):
    longest = values.shape.index(max(values.shape))
    spots = []
    for shift in (0, 1):
        where = [jax.random.randint(jax.random.fold_in(rng, axis), (), 0, length) for axis, length in enumerate(values.shape)]
        where[longest] = (where[longest] + shift) % values.shape[longest]
        spots.append(tuple(where))
    return values.at[spots[0]].set(smallest).at[spots[1]].set(largest)


def shard_levels(rng, shape, cuts, smallest, high):
    loudness = 1.0
    for position, blocks in cuts:
        draws = jax.random.uniform(jax.random.fold_in(jax.random.fold_in(rng, 6), position), (blocks,), jnp.float32, smallest / len(cuts), high / len(cuts))
        loudness = loudness * jnp.repeat(jnp.exp(draws), shape[position] // blocks).reshape((-1,) + (1,) * (len(shape) - 1 - position))
    return loudness


def scatter_about(rng, dims, width, reach, pieces=(), kind=jnp.bfloat16):
    loudness = shard_levels(rng, dims, pieces, -0.22, 0.18) if pieces else 1.0
    entries = jax.random.normal(rng, dims, jnp.float32) * width * loudness
    return jnp.minimum(jnp.maximum(entries, -reach), reach).astype(kind)


def setup_inputs(seed: int = 0) -> dict:
    streams_of = jax.random.split(jax.random.key(seed), 9)
    stamps = scatter_about(streams_of[0], (EXPOSURES, N_TROW * CORE, N_TCOL * CORE), 1.0, 6.0, ((0, 16), (1, 4), (2, 4)))
    footprint = draw_footprint(jax.random.fold_in(streams_of[8], 71), 0)
    psf_anchor = touch_ends(jax.random.randint(streams_of[2], (EXPOSURES, 2), 0, N_TCOL * CORE), jax.random.fold_in(streams_of[2], 1), 0, (N_TCOL * CORE) - 1).astype(jnp.int32)
    psf_degree = touch_ends(jax.random.randint(streams_of[3], (EXPOSURES,), 1, 4), jax.random.fold_in(streams_of[3], 1), 1, 3).astype(jnp.int32)
    psf_powers = draw_psf_powers(jax.random.fold_in(streams_of[8], 71), 0)
    psf_basis = scatter_about(streams_of[5], (EXPOSURES, NBASIS, PS * PS), (1.0 / PS), 0.1875, ((0, 16),), jnp.float32)
    flux = jnp.clip(jnp.exp(math.log(0.4) - 1.3862944 * jax.random.uniform(streams_of[6], (EXPOSURES,), jnp.float32) ** shard_levels(streams_of[6], (EXPOSURES,), ((0, 16),), -0.2, 0.2)), 0.1, 0.4)
    variance = jnp.clip(jnp.exp(math.log(2.0) - 1.3862944 * jax.random.uniform(streams_of[7], (EXPOSURES,), jnp.float32) ** shard_levels(streams_of[7], (EXPOSURES,), ((0, 16),), -0.2, 0.2)), 0.5, 2.0)
    return {"stamps": stamps, "footprint": footprint, "psf_anchor": psf_anchor, "psf_degree": psf_degree, "psf_powers": psf_powers, "psf_basis": psf_basis, "flux": flux, "variance": variance}


def spectral_tables():
    idx = jnp.arange(TILE, dtype=jnp.int32)
    prod = idx[:, None] * idx[None, :] % TILE
    angle = prod.astype(jnp.float32) * (2.0 * math.pi / TILE)
    scale = 1.0 / math.sqrt(TILE)
    cosine = jnp.cos(angle) * scale
    sine = jnp.sin(angle) * scale
    return (cosine.astype(jnp.bfloat16), (-sine).astype(jnp.bfloat16), cosine, sine)

def psf_tables():
    idx = jnp.arange(TILE, dtype=jnp.int32)
    offsets = jnp.arange(PS, dtype=jnp.int32) - PS // 2
    prod = idx[:, None] * offsets[None, :] % TILE
    angle = prod.astype(jnp.float32) * (2.0 * math.pi / TILE)
    return (jnp.cos(angle).astype(jnp.bfloat16), (-jnp.sin(angle)).astype(jnp.bfloat16))

def taper_plane():
    idx = jnp.arange(TILE, dtype=jnp.int32)
    dist = jnp.minimum(idx, TILE - 1 - idx).astype(jnp.float32)
    ramp = jnp.sin(0.5 * math.pi * (dist + 0.5) / HALO) ** 2
    line = jnp.where(dist >= HALO, jnp.float32(1.0), ramp)
    return line[:, None] * line[None, :]

def monomial(value, power):
    return jnp.where(power == 0, 1.0, jnp.where(power == 1, value, jnp.where(power == 2, value * value, value * value * value)))

def render(basis, powers, degree, anchor, row_tile, col_tile, sky_half):
    ux = (col_tile * CORE + CORE // 2 - anchor[..., 1]).astype(jnp.float32) / sky_half
    uy = (row_tile * CORE + CORE // 2 - anchor[..., 0]).astype(jnp.float32) / sky_half
    px = powers[..., 0]
    qy = powers[..., 1]
    keep = (px + qy <= degree[..., None]).astype(jnp.float32)
    term = monomial(ux[..., None], px) * monomial(uy[..., None], qy) * keep
    return lax.optimization_barrier(jnp.sum(term[..., None] * basis, axis=-2)).astype(jnp.bfloat16)

def image_spectrum(plane, fwd_re, fwd_im):
    half_re = jnp.dot(fwd_re, plane, preferred_element_type=jnp.float32).astype(jnp.bfloat16)
    half_im = jnp.dot(fwd_im, plane, preferred_element_type=jnp.float32).astype(jnp.bfloat16)
    spec_re = jnp.dot(half_re, fwd_re.T, preferred_element_type=jnp.float32) - jnp.dot(half_im, fwd_im.T, preferred_element_type=jnp.float32)
    spec_im = jnp.dot(half_re, fwd_im.T, preferred_element_type=jnp.float32) + jnp.dot(half_im, fwd_re.T, preferred_element_type=jnp.float32)
    return (spec_re, spec_im)

def psf_spectrum(stamp, pg_re, pg_im):
    lift_re = jnp.dot(pg_re, stamp, preferred_element_type=jnp.float32).astype(jnp.bfloat16)
    lift_im = jnp.dot(pg_im, stamp, preferred_element_type=jnp.float32).astype(jnp.bfloat16)
    otf_re = jnp.dot(lift_re, pg_re.T, preferred_element_type=jnp.float32) - jnp.dot(lift_im, pg_im.T, preferred_element_type=jnp.float32)
    otf_im = jnp.dot(lift_re, pg_im.T, preferred_element_type=jnp.float32) + jnp.dot(lift_im, pg_re.T, preferred_element_type=jnp.float32)
    return (otf_re, otf_im)

def reference(stamps, footprint, psf_anchor, psf_degree, psf_powers, psf_basis, flux, variance):
    fwd_re, fwd_im, inv_re, inv_im = spectral_tables()
    pg_re, pg_im = psf_tables()
    taper = taper_plane()
    tiles = N_TROW * N_TCOL
    sky_half = 0.5 * CORE * N_TCOL
    rows_tile = jnp.arange(N_TROW, dtype=jnp.int32)[:, None]
    cols_tile = jnp.arange(N_TCOL, dtype=jnp.int32)[None, :]
    zero_plane = jnp.zeros((TILE, TILE), jnp.float32)

    def per_exposure(carry, j):
        frame = footprint[j]
        cover = (frame[0] <= rows_tile) & (rows_tile < frame[1]) & (frame[2] <= cols_tile) & (cols_tile < frame[3])
        pixels = jnp.repeat(jnp.repeat(cover, CORE, axis=0), CORE, axis=1)
        masked = jnp.where(pixels, stamps[j], jnp.zeros((), jnp.bfloat16))
        padded = jnp.pad(masked, HALO)
        wnum = flux[j] / variance[j]
        wden = flux[j] * flux[j] / variance[j]

        def compute(tile):
            row_tile = (tile // N_TCOL).astype(jnp.int32)
            col_tile = (tile % N_TCOL).astype(jnp.int32)
            ext = lax.dynamic_slice(padded, (row_tile * CORE, col_tile * CORE), (TILE, TILE))
            apodized = (ext.astype(jnp.float32) * taper).astype(jnp.bfloat16)
            spec_re, spec_im = image_spectrum(apodized, fwd_re, fwd_im)
            stamp = render(psf_basis[j], psf_powers[j], psf_degree[j], psf_anchor[j], row_tile, col_tile, sky_half).reshape(PS, PS)
            otf_re, otf_im = psf_spectrum(stamp, pg_re, pg_im)
            part_re = wnum * (otf_re * spec_re + otf_im * spec_im)
            part_im = wnum * (otf_re * spec_im - otf_im * spec_re)
            part_den = wden * (otf_re * otf_re + otf_im * otf_im)
            return (part_re, part_im, part_den)

        def one_tile(tile):
            row_tile = tile // N_TCOL
            col_tile = tile % N_TCOL
            active = (frame[0] <= row_tile) & (row_tile < frame[1]) & (frame[2] <= col_tile) & (col_tile < frame[3])
            return lax.cond(active, compute, lambda t: (zero_plane, zero_plane, zero_plane), tile)
        part_re, part_im, part_den = lax.map(one_tile, jnp.arange(tiles, dtype=jnp.int32))
        return ((carry[0] + part_re, carry[1] + part_im, carry[2] + part_den), None)
    start = jnp.zeros((tiles, TILE, TILE), jnp.float32)
    (num_re, num_im, den), _ = lax.scan(per_exposure, (start, start, start), jnp.arange(EXPOSURES, dtype=jnp.int32))
    high = lax.Precision.HIGHEST
    core_re = inv_re[:, HALO:HALO + CORE]
    core_im = inv_im[:, HALO:HALO + CORE]

    def finish(tile):
        norm = jnp.sqrt(den[tile] + 1.0)
        spec_re = num_re[tile] / norm
        spec_im = num_im[tile] / norm
        temp_re = jnp.dot(spec_re, core_re, precision=high) - jnp.dot(spec_im, core_im, precision=high)
        temp_im = jnp.dot(spec_re, core_im, precision=high) + jnp.dot(spec_im, core_re, precision=high)
        return jnp.dot(core_re.T, temp_re, precision=high) - jnp.dot(core_im.T, temp_im, precision=high)
    images = lax.map(finish, jnp.arange(tiles, dtype=jnp.int32))
    images = images.reshape(N_TROW, N_TCOL, CORE, CORE).transpose(0, 2, 1, 3)
    return images.reshape(N_TROW, CORE, N_TCOL * CORE)
```

```python
import functools
import math

import jax
import jax.numpy as jnp
import ml_dtypes
import numpy as np
from jax import lax
from jax.experimental import pallas as pl
from jax.experimental.pallas import tpu as pltpu
from jax.sharding import PartitionSpec as P

TILE = 512
HALO = 64
PS = 32
NBASIS = 10
CORE = 384
CHIPS = 8
BLK = 16
HALF = CHIPS * BLK
ROWS = HALF + BLK
OUT = CORE // (2 * CHIPS)
PACK = 80
MESH = pl.DeviceIdType.MESH
F32 = jnp.float32
BF16 = jnp.bfloat16


def angles(a, b):
    return (a[:, None] * b[None, :] % TILE) * (2.0 * math.pi / TILE)


@functools.cache
def tables():
    freq = np.arange(TILE)
    pixel = (freq + HALO) % TILE
    offset = np.arange(PS) - PS // 2
    scale = 1.0 / math.sqrt(TILE)

    def bf(x):
        return np.asarray(x, np.float32).astype(ml_dtypes.bfloat16)

    rows = [np.arange(HALF * q, HALF * q + ROWS) for q in range(2)]
    live = [(u <= TILE // 2)[:, None] for u in rows]
    ftab = np.stack(
        [
            np.concatenate([np.cos(angles(u, pixel)) * k, -np.sin(angles(u, pixel)) * k]) * scale
            for u, k in zip(rows, live)
        ]
    )
    wtab = np.concatenate([np.cos(angles(pixel, freq)), -np.sin(angles(pixel, freq))], 1) * scale
    pgt = np.stack(
        [np.concatenate([np.cos(angles(u, offset)) * k, -np.sin(angles(u, offset)) * k]) for u, k in zip(rows, live)]
    )
    cos, sin = np.cos(angles(offset, freq)), np.sin(angles(offset, freq))
    cos, sin = np.tile(cos, (4, 1)), np.tile(sin, (4, 1))
    pgw = np.block([[cos, -sin], [sin, cos]])
    core = np.arange(CORE) + HALO
    cos, sin = np.cos(angles(freq, core)) * scale, np.sin(angles(freq, core)) * scale
    ytab = np.block([[cos, sin], [-sin, cos]])
    xtab = np.zeros((2 * CHIPS, 2, CHIPS * OUT, 4 * BLK))
    for z in range(CHIPS):
        for p in range(2):
            x = np.concatenate([OUT * (2 * t + p) + np.arange(OUT) for t in range(CHIPS)]) + HALO
            for side in range(2):
                q = p ^ side
                u = np.concatenate([q * HALF + BLK * z + np.arange(BLK), TILE // 2 + np.arange(BLK)])
                count = np.where((u == 0) | (u == TILE // 2), 1.0, 2.0)
                count[BLK:] = 0.0
                if z == CHIPS - 1 and q == 1:
                    count[BLK] = 1.0
                xtab[2 * z + p, side, :, : 2 * BLK] = np.cos(angles(x, u)) * scale * count
                xtab[2 * z + p, side, :, 2 * BLK :] = -np.sin(angles(x, u)) * scale * count
    edge = np.arange(HALO)
    dist = np.concatenate([HALO - 1 - edge, edge])
    line = np.sin(0.5 * math.pi * (dist + 0.5) / HALO) ** 2
    taper = np.stack([np.tile(line[:, None], (1, 128)), np.tile(line[None, :], (128, 1))]).astype(np.float32)
    return bf(ftab), bf(wtab), bf(pgt), bf(pgw), bf(ytab), bf(xtab), taper


def monomial(value, power):
    return jnp.where(
        power == 0,
        1.0,
        jnp.where(power == 1, value, jnp.where(power == 2, value * value, value * value * value)),
    )


def dot(a, b):
    return jnp.dot(a, b, preferred_element_type=F32)


def kernel(
    foot, anchor, degree, powers, flux, variance, basis, pgt, taper, stamps, ftab_h, wtab_h, pgw_h, ytab_h, xtab_h,
    out,
    core, rowh, first, last, right, left, ap, ftab, wtab, pgw, ytab, xtab,
    psf_own, psf_sib, psf_all, num_sib_out, num_sib_in, num_own, num_out, num_in, ex_in, ex_sum,
    t_own, t_sib, part_out, part_in,
    load_sem, halo_send, halo_recv, sib_send, sib_recv, psf_send, psf_recv, num_send, num_recv,
    ex_send, ex_recv, part_send, part_recv,
):
    group = lax.axis_index("exp")
    r = lax.axis_index("trow")
    c = lax.axis_index("tcol")
    z = group // 2
    p = group % 2
    sib = {"exp": group + 1 - 2 * p}

    def along(k):
        return 2 * ((z + k) % CHIPS) + p

    def near(dr, dc):
        return {"trow": (r + dr + 4) % 4, "tcol": (c + dc + 4) % 4}

    around = [(-1, 0), (1, 0), (0, -1), (0, 1), (-1, -1), (-1, 1), (1, -1), (1, 1)]
    loads = []
    for i, (src, dst) in enumerate(
        [(stamps, core), (ftab_h, ftab), (wtab_h, wtab), (pgw_h, pgw), (ytab_h, ytab), (xtab_h.at[group], xtab)]
    ):
        load = pltpu.make_async_copy(src, dst, load_sem.at[i])
        load.start()
        loads.append(load)
    barrier = pltpu.get_barrier_semaphore()
    for dr, dc in around:
        pl.semaphore_signal(barrier, inc=1, device_id=near(dr, dc), device_id_type=MESH)
    pl.semaphore_signal(barrier, inc=1, device_id=sib, device_id_type=MESH)
    for k in range(1, CHIPS):
        pl.semaphore_signal(barrier, inc=1, device_id={"exp": along(k)}, device_id_type=MESH)

    def remote(src, dst, send, recv, where):
        copy = pltpu.make_async_remote_copy(
            src_ref=src, dst_ref=dst, send_sem=send, recv_sem=recv, device_id=where, device_id_type=MESH
        )
        copy.start()
        return copy

    loads[0].wait()
    lane = lax.broadcasted_iota(jnp.int32, (CORE, 128), 1)
    low = lane < HALO
    first[...] = jnp.where(
        low, core[0, :, 0:128].astype(F32), pltpu.roll(core[1, :, 0:128].astype(F32), HALO, 1)
    ).astype(BF16)
    last[...] = jnp.where(
        low, pltpu.roll(core[0, :, 256:384].astype(F32), HALO, 1), core[1, :, 256:384].astype(F32)
    ).astype(BF16)
    pl.semaphore_wait(barrier, len(around) + CHIPS)
    top, low_rows = pl.ds(0, HALO), pl.ds(CORE - HALO, HALO)
    at_next, at_prev = pl.ds(CORE, HALO), pl.ds(CORE + HALO, HALO)
    pieces = [
        (core.at[:, top, :], rowh.at[:, pl.ds(0, HALO), :]),
        (core.at[:, low_rows, :], rowh.at[:, pl.ds(HALO, HALO), :]),
        (first, right.at[pl.ds(0, CORE), :]),
        (last, left.at[pl.ds(0, CORE), :]),
        (first.at[top, :], right.at[at_next, :]),
        (last.at[top, :], left.at[at_next, :]),
        (first.at[low_rows, :], right.at[at_prev, :]),
        (last.at[low_rows, :], left.at[at_prev, :]),
    ]
    halos = [
        remote(src, dst, halo_send.at[i], halo_recv.at[i], near(*around[i])) for i, (src, dst) in enumerate(pieces)
    ]

    lane32 = lax.broadcasted_iota(jnp.int32, (PS, 128), 1)
    row32 = lax.broadcasted_iota(jnp.int32, (PS, 128), 0)
    slot32 = lane32 // PS
    fold = jnp.where(
        lax.broadcasted_iota(jnp.int32, (128, 128), 0) % PS == lax.broadcasted_iota(jnp.int32, (128, 128), 1) % PS,
        1.0,
        0.0,
    ).astype(BF16)
    lane16 = lax.broadcasted_iota(jnp.int32, (BLK, 128), 1) // PS
    row16 = lax.broadcasted_iota(jnp.int32, (BLK, 128), 0)
    psf = jnp.zeros((PS, 128), F32)
    wrow = jnp.zeros((BLK, 128), F32)
    wnum = []
    for e in range(2):
        ux = (c * CORE + CORE // 2 - anchor[e, 1]).astype(F32) / (2.0 * CORE)
        uy = (r * CORE + CORE // 2 - anchor[e, 0]).astype(F32) / (2.0 * CORE)
        flat = jnp.zeros((1, PS * PS), F32)
        for k in range(NBASIS):
            px, qy = powers[e, k, 0], powers[e, k, 1]
            term = jnp.where(px + qy <= degree[e], monomial(ux, px) * monomial(uy, qy), 0.0)
            flat = flat + term * basis[e, k : k + 1, :]
        spread = jnp.zeros((PS, 128), F32)
        for t in range(PS * PS // 128):
            spread = jnp.where(
                (row32 // 4 == t) & (slot32 == row32 % 4),
                jnp.broadcast_to(flat[:, 128 * t : 128 * t + 128], (PS, 128)),
                spread,
            )
        mine = 2 * p + e
        psf = jnp.where(slot32 == mine, dot(spread.astype(BF16), fold), psf)
        active = (foot[e, 0] <= r) & (r < foot[e, 1]) & (foot[e, 2] <= c) & (c < foot[e, 3])
        gain = jnp.where(active, flux[e], 0.0)
        wnum.append(jnp.full((8, 128), gain, F32) / jnp.full((8, 128), variance[e], F32))
        wden = jnp.full((BLK, 128), gain * flux[e], F32) / jnp.full((BLK, 128), variance[e], F32)
        wrow = jnp.where(lane16 == mine, wden, wrow)
    high = wrow.astype(BF16).astype(F32)
    rest = wrow - high
    mid = rest.astype(BF16).astype(F32)
    wrow = jnp.where(row16 == 0, high, jnp.where(row16 == 1, mid, jnp.where(row16 == 2, rest - mid, 0.0)))
    psf_own[0:PS, :] = psf.astype(BF16)
    psf_own[PS : PS + BLK, :] = wrow.astype(BF16)
    psf_pair = remote(psf_own, psf_sib, sib_send.at[0], sib_recv.at[0], sib)

    for load in loads[1:4]:
        load.wait()
    psf_pair.wait()
    psf_all[0] = (psf_own[...].astype(F32) + psf_sib[...].astype(F32)).astype(BF16)
    psf_copies = [
        remote(psf_all.at[0], psf_all.at[k], psf_send.at[k], psf_recv.at[k], {"exp": along(k)})
        for k in range(1, CHIPS)
    ]

    for copy in halos:
        copy.wait()
    cover = []
    for e in range(2):
        cover.append(
            [
                jnp.where((foot[e, lo] <= at) & (at < foot[e, lo + 1]), 1.0, 0.0)
                for lo, at in ((0, r + 1), (0, r - 1), (2, c + 1), (2, c - 1))
            ]
        )
    lane_s = lax.broadcasted_iota(jnp.int32, (TILE, 128), 1) < HALO
    line_r = taper[0]
    line_c = taper[1]
    right_v, left_v = right[...].astype(F32), left[...].astype(F32)
    right_t, left_t = pltpu.roll(right_v, HALO, 1), pltpu.roll(left_v, HALO, 1)
    for e in range(2):
        ap[e, 0:CORE, 0:CORE] = core[e]
        up, down, after, before = cover[e]
        wide = jnp.concatenate([line_r] * 3, axis=1)
        ap[e, CORE : CORE + HALO, 0:CORE] = (rowh[e, 0:HALO, :].astype(F32) * (wide[0:HALO] * up)).astype(BF16)
        ap[e, CORE + HALO : TILE, 0:CORE] = (rowh[e, HALO:, :].astype(F32) * (wide[HALO:] * down)).astype(BF16)
        side = jnp.where(lane_s, right_v, left_t) if e == 0 else jnp.where(lane_s, right_t, left_v)
        keep = jnp.where(lane_s[0:128], after, before) * line_c
        for t in range(3):
            ap[e, 128 * t : 128 * t + 128, CORE:TILE] = (side[128 * t : 128 * t + 128] * keep).astype(BF16)
        corner = side[CORE:TILE]
        taper2 = line_r * line_c * jnp.where(lane_s[0:128], after, before)
        ap[e, CORE : CORE + HALO, CORE:TILE] = (corner[0:HALO] * (taper2[0:HALO] * up)).astype(BF16)
        ap[e, CORE + HALO : TILE, CORE:TILE] = (corner[HALO:] * (taper2[HALO:] * down)).astype(BF16)

    lane_r = lax.broadcasted_iota(jnp.int32, (2 * ROWS, 128), 1) // PS
    stamp = psf_own[0:PS, :]

    def numerator(q):
        f = ftab[q]
        lift = dot(pgt[q], stamp)
        total_re = total_im = None
        for e in range(2):
            half = dot(f, ap[e]).astype(BF16)
            prod = dot(half, wtab[...])
            spec_re = prod[:ROWS, :TILE] - prod[ROWS:, TILE:]
            spec_im = prod[:ROWS, TILE:] + prod[ROWS:, :TILE]
            one = jnp.where(lane_r == 2 * p + e, lift, 0.0).astype(BF16)
            otf = dot(jnp.concatenate([one[:ROWS], one[ROWS:]], axis=1), pgw[...])
            otf_re, otf_im = otf[:, :TILE], otf[:, TILE:]
            w = wnum[e][0:1, 0:1]
            part_re = w * (otf_re * spec_re + otf_im * spec_im)
            part_im = w * (otf_re * spec_im - otf_im * spec_re)
            total_re = part_re if e == 0 else total_re + part_re
            total_im = part_im if e == 0 else total_im + part_im
        return total_re, total_im

    num_re, num_im = numerator(1 - p)
    num_sib_out[0] = num_re.astype(BF16)
    num_sib_out[1] = num_im.astype(BF16)
    num_pair = remote(num_sib_out, num_sib_in, sib_send.at[1], sib_recv.at[1], sib)
    num_re, num_im = numerator(p)
    num_pair.wait()
    num_re = num_re + num_sib_in[0].astype(F32)
    num_im = num_im + num_sib_in[1].astype(F32)
    num_own[0] = num_re
    num_own[1] = num_im
    num_out[0] = num_re.astype(BF16)
    num_out[1] = num_im.astype(BF16)
    num_copies = [
        remote(
            num_out.at[:, pl.ds(pl.multiple_of(BLK * ((z + k) % CHIPS), BLK), BLK), :],
            num_in.at[k],
            num_send.at[k],
            num_recv.at[k],
            {"exp": along(k)},
        )
        for k in range(1, CHIPS)
    ]

    def extra(at):
        return pltpu.make_async_remote_copy(
            src_ref=num_out.at[:, pl.ds(HALF, BLK), :],
            dst_ref=ex_in.at[at],
            send_sem=ex_send,
            recv_sem=ex_recv.at[at],
            device_id={"exp": 2 * CHIPS - 1},
            device_id_type=MESH,
        )

    @pl.when((p == 1) & (z < CHIPS - 1))
    def _():
        extra(z).start()

    for copy in psf_copies:
        copy.wait()
    start = pl.multiple_of(BLK * z, BLK)
    pgz = jnp.concatenate(
        [
            pgt[p, pl.ds(start, BLK), :],
            pgt[p, HALF:ROWS, :],
            pgt[p, pl.ds(pl.multiple_of(start + ROWS, BLK), BLK), :],
            pgt[p, ROWS + HALF :, :],
        ],
        axis=0,
    )
    lane_d = lax.broadcasted_iota(jnp.int32, (4 * BLK, 128), 1) // PS

    def add_den(g, den):
        lift = dot(pgz, psf_all[g, 0:PS, :])
        weights = jnp.sum(psf_all[g, PS : PS + BLK, :].astype(F32), axis=0, keepdims=True)
        ones = [jnp.where(lane_d == t, lift, 0.0).astype(BF16) for t in range(4)]
        lhs = jnp.concatenate(
            [jnp.concatenate([one[: 2 * BLK], one[2 * BLK :]], axis=1) for one in ones], axis=0
        )
        otf = dot(lhs, pgw[...])
        power = otf[:, :TILE] * otf[:, :TILE] + otf[:, TILE:] * otf[:, TILE:]
        for t in range(4):
            den = den + weights[:, PS * t : PS * t + 1] * power[2 * BLK * t : 2 * BLK * (t + 1)]
        return den

    den = lax.fori_loop(0, CHIPS, add_den, jnp.zeros((2 * BLK, TILE), F32))

    ex_sum[...] = jnp.zeros_like(ex_sum)

    @pl.when(group == 2 * CHIPS - 1)
    def _():
        for t in range(CHIPS - 1):
            extra(t).wait_recv()
        total = num_own[:, HALF:ROWS, :]
        for t in range(CHIPS - 1):
            total = total + ex_in[t].astype(F32)
        ex_sum[...] = total

    sums = num_own[:, pl.ds(start, BLK), :]
    for k in range(1, CHIPS):
        num_copies[k - 1].wait_recv()
        sums = sums + num_in[k].astype(F32)
    norm = lax.rsqrt(den + 1.0)
    s_re = jnp.concatenate([sums[0], ex_sum[0]], axis=0) * norm
    s_im = jnp.concatenate([sums[1], ex_sum[1]], axis=0) * norm
    loads[4].wait()
    loads[5].wait()
    t_all = dot(jnp.concatenate([s_re, s_im], axis=1).astype(BF16), ytab[...])
    t_own[0 : 2 * BLK, :] = t_all[:, :CORE].astype(BF16)
    t_own[2 * BLK :, :] = t_all[:, CORE:].astype(BF16)
    t_pair = remote(t_own, t_sib, sib_send.at[2], sib_recv.at[2], sib)
    image = dot(xtab[0], t_own[...])
    t_pair.wait()
    image = image + dot(xtab[1], t_sib[...])
    for t in range(CHIPS):
        block = image[OUT * t : OUT * (t + 1)]
        part_out[t] = jnp.concatenate(
            [block[:, 128 * i : 128 * i + 128] for i in range(3)] + [jnp.zeros((PACK - 3 * OUT, 128), F32)], axis=0
        ).astype(BF16)
    parts = [
        remote(
            part_out.at[(z + k) % CHIPS], part_in.at[k], part_send.at[k], part_recv.at[k], {"exp": along(k)}
        )
        for k in range(1, CHIPS)
    ]
    total = part_out[z].astype(F32)
    for k in range(1, CHIPS):
        parts[k - 1].wait_recv()
        total = total + part_in[k].astype(F32)
    for i in range(3):
        out[0, :, 128 * i : 128 * i + 128] = total[OUT * i : OUT * (i + 1)]
    for copy in num_copies + parts:
        copy.wait_send()

    @pl.when((p == 1) & (z < CHIPS - 1))
    def _():
        extra(z).wait_send()


def body(stamps, footprint, psf_anchor, psf_degree, psf_powers, psf_basis, flux, variance):
    ftab, wtab, pgt, pgw, ytab, xtab, taper = (jnp.asarray(t) for t in tables())
    smem = pl.BlockSpec(memory_space=pltpu.SMEM)
    vmem = pl.BlockSpec(memory_space=pltpu.VMEM)
    hbm = pl.BlockSpec(memory_space=pl.ANY)
    dma = pltpu.SemaphoreType.DMA
    return pl.pallas_call(
        kernel,
        out_shape=jax.ShapeDtypeStruct((1, OUT, CORE), F32),
        in_specs=[smem] * 6 + [vmem] * 3 + [hbm] * 6,
        out_specs=vmem,
        scratch_shapes=[
            pltpu.VMEM((2, CORE, CORE), BF16),
            pltpu.VMEM((2, 2 * HALO, CORE), BF16),
            pltpu.VMEM((CORE, 128), BF16),
            pltpu.VMEM((CORE, 128), BF16),
            pltpu.VMEM((TILE, 128), BF16),
            pltpu.VMEM((TILE, 128), BF16),
            pltpu.VMEM((2, TILE, TILE), BF16),
            pltpu.VMEM(ftab.shape, BF16),
            pltpu.VMEM(wtab.shape, BF16),
            pltpu.VMEM(pgw.shape, BF16),
            pltpu.VMEM(ytab.shape, BF16),
            pltpu.VMEM(xtab.shape[1:], BF16),
            pltpu.VMEM((PS + BLK, 128), BF16),
            pltpu.VMEM((PS + BLK, 128), BF16),
            pltpu.VMEM((CHIPS, PS + BLK, 128), BF16),
            pltpu.VMEM((2, ROWS, TILE), BF16),
            pltpu.VMEM((2, ROWS, TILE), BF16),
            pltpu.VMEM((2, ROWS, TILE), F32),
            pltpu.VMEM((2, ROWS, TILE), BF16),
            pltpu.VMEM((CHIPS, 2, BLK, TILE), BF16),
            pltpu.VMEM((CHIPS - 1, 2, BLK, TILE), BF16),
            pltpu.VMEM((2, BLK, TILE), F32),
            pltpu.VMEM((4 * BLK, CORE), BF16),
            pltpu.VMEM((4 * BLK, CORE), BF16),
            pltpu.VMEM((CHIPS, PACK, 128), BF16),
            pltpu.VMEM((CHIPS, PACK, 128), BF16),
            dma((6,)),
            dma((8,)),
            dma((8,)),
            dma((3,)),
            dma((3,)),
            dma((CHIPS,)),
            dma((CHIPS,)),
            dma((CHIPS,)),
            dma((CHIPS,)),
            dma,
            dma((CHIPS - 1,)),
            dma((CHIPS,)),
            dma((CHIPS,)),
        ],
        compiler_params=pltpu.CompilerParams(
            collective_id=0, has_side_effects=True, vmem_limit_bytes=48 * 1024 * 1024
        ),
    )(
        footprint, psf_anchor, psf_degree, psf_powers, flux, variance, psf_basis, pgt, taper,
        stamps, ftab, wtab, pgw, ytab, xtab,
    )


def solution(mesh):
    in_specs = (
        P("exp", "trow", "tcol"),
        P("exp", None),
        P("exp", None),
        P("exp"),
        P("exp", None, None),
        P("exp", None, None),
        P("exp"),
        P("exp"),
    )
    out_specs = P("trow", "exp", "tcol")
    return jax.shard_map(body, mesh=mesh, in_specs=in_specs, out_specs=out_specs, check_vma=False)
```

```python
import functools
import math

import jax
import jax.numpy as jnp
import ml_dtypes
import numpy as np
from jax import lax
from jax.experimental import pallas as pl
from jax.experimental.pallas import tpu as pltpu
from jax.sharding import PartitionSpec as P

TILE = 512
HALO = 64
PS = 32
NBASIS = 10
CORE = 384
CHIPS = 8
SIDE = TILE // 2
FAR = (4, 3, 5, 2, 6, 1, 7)
BLK = 16
HALF = CHIPS * BLK
ROWS = HALF + BLK
OUT = CORE // (2 * CHIPS)
PACK = 80
MESH = pl.DeviceIdType.MESH
F32 = jnp.float32
BF16 = jnp.bfloat16


def angles(a, b):
    return (a[:, None] * b[None, :] % TILE) * (2.0 * math.pi / TILE)


@functools.cache
def tables():
    freq = np.arange(TILE)
    pixel = (freq + HALO) % TILE
    offset = np.arange(PS) - PS // 2
    scale = 1.0 / math.sqrt(TILE)

    def bf(x):
        return np.asarray(x, np.float32).astype(ml_dtypes.bfloat16)

    rows = [np.arange(HALF * q, HALF * q + ROWS) for q in range(2)]
    live = [(u <= TILE // 2)[:, None] for u in rows]
    ftab = np.stack(
        [
            np.concatenate([np.cos(angles(u, pixel)) * k, -np.sin(angles(u, pixel)) * k]) * scale
            for u, k in zip(rows, live)
        ]
    )
    wtab = np.concatenate([np.cos(angles(pixel, freq[:SIDE])), -np.sin(angles(pixel, freq[:SIDE]))], 1) * scale
    wtab[:, SIDE] = np.cos(angles(pixel, freq[SIDE : SIDE + 1]))[:, 0] * scale
    pgt = np.stack(
        [np.concatenate([np.cos(angles(u, offset)) * k, -np.sin(angles(u, offset)) * k]) for u, k in zip(rows, live)]
    )
    order = np.concatenate([freq[:SIDE], freq[SIDE : SIDE + 1], freq[:SIDE:-1]])
    cos, sin = np.cos(angles(offset, order)), np.sin(angles(offset, order))
    cos, sin = np.tile(cos, (4, 1)), np.tile(sin, (4, 1))
    pgw = np.block([[cos, -sin], [sin, cos]])
    core = np.arange(CORE) + HALO
    ytab = np.concatenate([np.cos(angles(freq[:SIDE], core)), np.sin(angles(freq[:SIDE], core))]) * scale
    ytab[SIDE] = np.cos(angles(freq[SIDE : SIDE + 1], core))[0] * scale
    xtab = np.zeros((2 * CHIPS, 2, CHIPS * OUT, 4 * BLK))
    for z in range(CHIPS):
        for p in range(2):
            x = np.concatenate([OUT * (2 * t + p) + np.arange(OUT) for t in range(CHIPS)]) + HALO
            for side in range(2):
                q = p ^ side
                u = np.concatenate([q * HALF + BLK * z + np.arange(BLK), TILE // 2 + np.arange(BLK)])
                count = np.where((u == 0) | (u == TILE // 2), 1.0, 2.0)
                count[BLK:] = 0.0
                if z == CHIPS - 1 and q == 1:
                    count[BLK] = 1.0
                xtab[2 * z + p, side, :, : 2 * BLK] = np.cos(angles(x, u)) * scale * count
                xtab[2 * z + p, side, :, 2 * BLK :] = -np.sin(angles(x, u)) * scale * count
    edge = np.arange(HALO)
    dist = np.concatenate([HALO - 1 - edge, edge])
    line = np.sin(0.5 * math.pi * (dist + 0.5) / HALO) ** 2
    taper = np.stack([np.tile(line[:, None], (1, 128)), np.tile(line[None, :], (128, 1))]).astype(np.float32)
    return bf(ftab), bf(wtab), bf(pgt), bf(pgw), bf(ytab), bf(xtab), taper


def monomial(value, power):
    return jnp.where(
        power == 0,
        1.0,
        jnp.where(power == 1, value, jnp.where(power == 2, value * value, value * value * value)),
    )


def dot(a, b):
    return jnp.dot(a, b, preferred_element_type=F32)


def kernel(
    foot_h, anchor_h, degree_h, powers_h, flux_h, variance_h, basis_h, pgt_h, taper_h, stamps, ftab_h, wtab_h, pgw_h,
    ytab_h, xtab_h,
    out,
    foot, anchor, degree, powers, flux, variance, basis, pgt, taper, strip, otf_all, rowh, first, last, right, left, ap, ftab, wtab, pgw, ytab, xtab,
    psf_own, psf_sib, psf_all, num_sib_out, num_sib_in, num_own, num_out, num_in, ex_in, ex_sum,
    t_own, t_sib, part_out, part_in,
    load_sem, halo_send, halo_recv, sib_send, sib_recv, psf_send, psf_recv, num_send, num_recv,
    ex_send, ex_recv, part_send, part_recv,
):
    group = lax.axis_index("exp")
    r = lax.axis_index("trow")
    c = lax.axis_index("tcol")
    z = group // 2
    p = group % 2
    sib = {"exp": group + 1 - 2 * p}

    def along(k):
        return 2 * ((z + k) % CHIPS) + p

    def near(dr, dc):
        return {"trow": (r + dr + 4) % 4, "tcol": (c + dc + 4) % 4}

    around = [(-1, -1), (-1, 1), (1, -1), (1, 1), (0, -1), (0, 1), (-1, 0), (1, 0)]
    barrier = pltpu.get_barrier_semaphore()
    for dr, dc in around:
        pl.semaphore_signal(barrier, inc=1, device_id=near(dr, dc), device_id_type=MESH)
    for k in FAR:
        pl.semaphore_signal(barrier, inc=1, device_id={"exp": along(k)}, device_id_type=MESH)
    pl.semaphore_signal(barrier, inc=1, device_id=sib, device_id_type=MESH)
    loads = []
    for i, (src, dst) in enumerate(
        [
            (stamps.at[:, :, pl.ds(0, 128)], strip.at[0]), (stamps.at[:, :, pl.ds(CORE - 128, 128)], strip.at[1]),
            (foot_h, foot), (anchor_h, anchor), (degree_h, degree), (powers_h, powers),
            (flux_h, flux), (variance_h, variance), (basis_h, basis), (pgt_h, pgt), (pgw_h, pgw),
            (stamps, ap.at[:, pl.ds(0, CORE), pl.ds(0, CORE)]), (taper_h, taper), (ftab_h, ftab), (wtab_h, wtab),
            (ytab_h, ytab), (xtab_h.at[group], xtab),
        ]
    ):
        load = pltpu.make_async_copy(src, dst, load_sem.at[i])
        load.start()
        loads.append(load)

    def remote(src, dst, send, recv, where):
        copy = pltpu.make_async_remote_copy(
            src_ref=src, dst_ref=dst, send_sem=send, recv_sem=recv, device_id=where, device_id_type=MESH
        )
        copy.start()
        return copy

    loads[0].wait()
    loads[1].wait()
    low = lax.broadcasted_iota(jnp.int32, (CORE, 128), 1) < HALO
    first[...] = jnp.where(low, strip[0, 0].astype(F32), pltpu.roll(strip[0, 1].astype(F32), HALO, 1)).astype(BF16)
    last[...] = jnp.where(low, pltpu.roll(strip[1, 0].astype(F32), HALO, 1), strip[1, 1].astype(F32)).astype(BF16)
    pl.semaphore_wait(barrier, len(around) + CHIPS)
    top, low_rows = pl.ds(0, HALO), pl.ds(CORE - HALO, HALO)
    at_next, at_prev = pl.ds(CORE, HALO), pl.ds(CORE + HALO, HALO)
    pieces = [
        (first.at[top, :], right.at[at_next, :]),
        (last.at[top, :], left.at[at_next, :]),
        (first.at[low_rows, :], right.at[at_prev, :]),
        (last.at[low_rows, :], left.at[at_prev, :]),
        (first, right.at[pl.ds(0, CORE), :]),
        (last, left.at[pl.ds(0, CORE), :]),
        (stamps.at[:, top, :], rowh.at[:, pl.ds(0, HALO), :]),
        (stamps.at[:, low_rows, :], rowh.at[:, pl.ds(HALO, HALO), :]),
    ]
    halos = [
        remote(src, dst, halo_send.at[i], halo_recv.at[i], near(*around[i])) for i, (src, dst) in enumerate(pieces)
    ]

    for load in loads[2:9]:
        load.wait()

    lane32 = lax.broadcasted_iota(jnp.int32, (PS, 128), 1)
    row32 = lax.broadcasted_iota(jnp.int32, (PS, 128), 0)
    slot32 = lane32 // PS
    fold = jnp.where(
        lax.broadcasted_iota(jnp.int32, (128, 128), 0) % PS == lax.broadcasted_iota(jnp.int32, (128, 128), 1) % PS,
        1.0,
        0.0,
    ).astype(BF16)
    lane16 = lax.broadcasted_iota(jnp.int32, (BLK, 128), 1) // PS
    row16 = lax.broadcasted_iota(jnp.int32, (BLK, 128), 0)
    psf = jnp.zeros((PS, 128), F32)
    wrow = jnp.zeros((BLK, 128), F32)
    wnum = []
    for e in range(2):
        ux = (c * CORE + CORE // 2 - anchor[e, 1]).astype(F32) / (2.0 * CORE)
        uy = (r * CORE + CORE // 2 - anchor[e, 0]).astype(F32) / (2.0 * CORE)
        flat = jnp.zeros((1, PS * PS), F32)
        for k in range(NBASIS):
            px, qy = powers[e, 0, k], powers[e, 1, k]
            term = jnp.where(px + qy <= degree[e], monomial(ux, px) * monomial(uy, qy), 0.0)
            flat = flat + term * basis[k, e : e + 1, :]
        spread = jnp.zeros((PS, 128), F32)
        for t in range(PS * PS // 128):
            spread = jnp.where(
                (row32 // 4 == t) & (slot32 == row32 % 4),
                jnp.broadcast_to(flat[:, 128 * t : 128 * t + 128], (PS, 128)),
                spread,
            )
        mine = 2 * p + e
        psf = jnp.where(slot32 == mine, dot(spread.astype(BF16), fold), psf)
        active = (foot[e, 0] <= r) & (r < foot[e, 1]) & (foot[e, 2] <= c) & (c < foot[e, 3])
        gain = jnp.where(active, flux[e], 0.0)
        wnum.append(jnp.full((8, 128), gain, F32) / jnp.full((8, 128), variance[e], F32))
        wden = jnp.full((BLK, 128), gain * flux[e], F32) / jnp.full((BLK, 128), variance[e], F32)
        wrow = jnp.where(lane16 == mine, wden, wrow)
    high = wrow.astype(BF16).astype(F32)
    rest = wrow - high
    mid = rest.astype(BF16).astype(F32)
    wrow = jnp.where(row16 == 0, high, jnp.where(row16 == 1, mid, jnp.where(row16 == 2, rest - mid, 0.0)))
    psf_own[0:PS, :] = psf.astype(BF16)
    psf_own[PS : PS + BLK, :] = wrow.astype(BF16)
    psf_pair = remote(psf_own, psf_sib, sib_send.at[0], sib_recv.at[0], sib)


    loads[9].wait()
    loads[10].wait()
    stamp = psf_own[0:PS, :]
    lane_r = lax.broadcasted_iota(jnp.int32, (2 * ROWS, 128), 1) // PS
    for side in range(2):
        lift = dot(pgt[1 - p if side == 0 else p], stamp)
        for e in range(2):
            one = jnp.where(lane_r == 2 * p + e, lift, 0.0).astype(BF16)
            otf_all[side, e] = dot(jnp.concatenate([one[:ROWS], one[ROWS:]], axis=1), pgw[...])
        if side == 0:
            psf_pair.wait_recv()
            psf_all[0] = (psf_own[...].astype(F32) + psf_sib[...].astype(F32)).astype(BF16)
            psf_copies = [
                remote(psf_all.at[0], psf_all.at[k], psf_send.at[k], psf_recv.at[k], {"exp": along(k)}) for k in FAR
            ]

    for load in loads[11:15]:
        load.wait()
    for copy in halos:
        copy.wait_recv()
    cover = []
    for e in range(2):
        cover.append(
            [
                jnp.where((foot[e, lo] <= at) & (at < foot[e, lo + 1]), 1.0, 0.0)
                for lo, at in ((0, r + 1), (0, r - 1), (2, c + 1), (2, c - 1))
            ]
        )
    lane_s = lax.broadcasted_iota(jnp.int32, (TILE, 128), 1) < HALO
    line_r = taper[0]
    line_c = taper[1]
    right_v, left_v = right[...].astype(F32), left[...].astype(F32)
    right_t, left_t = pltpu.roll(right_v, HALO, 1), pltpu.roll(left_v, HALO, 1)
    for e in range(2):
        up, down, after, before = cover[e]
        wide = jnp.concatenate([line_r] * 3, axis=1)
        ap[e, CORE : CORE + HALO, 0:CORE] = (rowh[e, 0:HALO, :].astype(F32) * (wide[0:HALO] * up)).astype(BF16)
        ap[e, CORE + HALO : TILE, 0:CORE] = (rowh[e, HALO:, :].astype(F32) * (wide[HALO:] * down)).astype(BF16)
        side = jnp.where(lane_s, right_v, left_t) if e == 0 else jnp.where(lane_s, right_t, left_v)
        keep = jnp.where(lane_s[0:128], after, before) * line_c
        for t in range(3):
            ap[e, 128 * t : 128 * t + 128, CORE:TILE] = (side[128 * t : 128 * t + 128] * keep).astype(BF16)
        corner = side[CORE:TILE]
        taper2 = line_r * line_c * jnp.where(lane_s[0:128], after, before)
        ap[e, CORE : CORE + HALO, CORE:TILE] = (corner[0:HALO] * (taper2[0:HALO] * up)).astype(BF16)
        ap[e, CORE + HALO : TILE, CORE:TILE] = (corner[HALO:] * (taper2[HALO:] * down)).astype(BF16)

    lane0 = lax.broadcasted_iota(jnp.int32, (ROWS, SIDE), 1) == 0

    def numerator(q, side):
        total_re = total_im = None
        for e in range(2):
            half = dot(ftab[q], ap[e]).astype(BF16)
            prod = dot(half, wtab[...])
            re_cos, re_sin = prod[:ROWS, :SIDE], prod[:ROWS, SIDE:]
            im_cos, im_sin = prod[ROWS:, :SIDE], prod[ROWS:, SIDE:]
            spec_re = jnp.concatenate(
                [re_cos - jnp.where(lane0, 0.0, im_sin), jnp.where(lane0, re_sin, re_cos + im_sin)], axis=1
            )
            spec_im = jnp.concatenate(
                [im_cos + jnp.where(lane0, 0.0, re_sin), jnp.where(lane0, im_sin, im_cos - re_sin)], axis=1
            )
            otf_re, otf_im = otf_all[side, e, :, :TILE], otf_all[side, e, :, TILE:]
            w = wnum[e][0:1, 0:1]
            part_re = w * (otf_re * spec_re + otf_im * spec_im)
            part_im = w * (otf_re * spec_im - otf_im * spec_re)
            total_re = part_re if e == 0 else total_re + part_re
            total_im = part_im if e == 0 else total_im + part_im
        return total_re, total_im

    num_re, num_im = numerator(1 - p, 0)
    num_sib_out[0] = num_re.astype(BF16)
    num_sib_out[1] = num_im.astype(BF16)
    num_pair = remote(num_sib_out, num_sib_in, sib_send.at[1], sib_recv.at[1], sib)
    num_re, num_im = numerator(p, 1)
    num_pair.wait_recv()
    num_re = num_re + num_sib_in[0].astype(F32)
    num_im = num_im + num_sib_in[1].astype(F32)
    num_own[0] = num_re
    num_own[1] = num_im
    num_out[0] = num_re.astype(BF16)
    num_out[1] = num_im.astype(BF16)
    num_copies = [
        remote(
            num_out.at[:, pl.ds(pl.multiple_of(BLK * ((z + k) % CHIPS), BLK), BLK), :],
            num_in.at[k],
            num_send.at[k],
            num_recv.at[k],
            {"exp": along(k)},
        )
        for k in FAR
    ]

    def extra(at):
        return pltpu.make_async_remote_copy(
            src_ref=num_out.at[:, pl.ds(HALF, BLK), :],
            dst_ref=ex_in.at[at],
            send_sem=ex_send,
            recv_sem=ex_recv.at[at],
            device_id={"exp": 2 * CHIPS - 1},
            device_id_type=MESH,
        )

    @pl.when((p == 1) & (z < CHIPS - 1))
    def _():
        extra(z).start()

    for copy in psf_copies:
        copy.wait_recv()
    start = pl.multiple_of(BLK * z, BLK)
    pgz = jnp.concatenate(
        [
            pgt[p, pl.ds(start, BLK), :],
            pgt[p, HALF:ROWS, :],
            pgt[p, pl.ds(pl.multiple_of(start + ROWS, BLK), BLK), :],
            pgt[p, ROWS + HALF :, :],
        ],
        axis=0,
    )
    lane_d = lax.broadcasted_iota(jnp.int32, (4 * BLK, 128), 1) // PS

    def add_den(g, den):
        lift = dot(pgz, psf_all[g, 0:PS, :])
        weights = jnp.sum(psf_all[g, PS : PS + BLK, :].astype(F32), axis=0, keepdims=True)
        ones = [jnp.where(lane_d == t, lift, 0.0).astype(BF16) for t in range(4)]
        lhs = jnp.concatenate(
            [jnp.concatenate([one[: 2 * BLK], one[2 * BLK :]], axis=1) for one in ones], axis=0
        )
        otf = dot(lhs, pgw[...])
        power = otf[:, :TILE] * otf[:, :TILE] + otf[:, TILE:] * otf[:, TILE:]
        for t in range(4):
            den = den + weights[:, PS * t : PS * t + 1] * power[2 * BLK * t : 2 * BLK * (t + 1)]
        return den

    den = lax.fori_loop(0, CHIPS, add_den, jnp.zeros((2 * BLK, TILE), F32))

    ex_sum[...] = jnp.zeros_like(ex_sum)

    @pl.when(group == 2 * CHIPS - 1)
    def _():
        for t in range(CHIPS - 1):
            extra(t).wait_recv()
        total = num_own[:, HALF:ROWS, :]
        for t in range(CHIPS - 1):
            total = total + ex_in[t].astype(F32)
        ex_sum[...] = total

    sums = num_own[:, pl.ds(start, BLK), :]
    for k, copy in reversed(list(zip(FAR, num_copies))):
        copy.wait_recv()
        sums = sums + num_in[k].astype(F32)
    norm = lax.rsqrt(den + 1.0)
    s_re = jnp.concatenate([sums[0], ex_sum[0]], axis=0) * norm
    s_im = jnp.concatenate([sums[1], ex_sum[1]], axis=0) * norm
    loads[15].wait()
    loads[16].wait()
    lane0 = lax.broadcasted_iota(jnp.int32, (2 * BLK, SIDE), 1) == 0
    (re_p, re_m), (im_p, im_m) = ((x[:, :SIDE], x[:, SIDE:]) for x in (s_re, s_im))
    top_rows = [jnp.where(lane0, re_p, re_p + re_m), jnp.where(lane0, re_m, im_m - im_p)]
    low_rows = [jnp.where(lane0, im_p, im_p + im_m), jnp.where(lane0, im_m, re_p - re_m)]
    folded = jnp.concatenate([jnp.concatenate(top_rows, axis=1), jnp.concatenate(low_rows, axis=1)], axis=0)
    t_own[...] = dot(folded.astype(BF16), ytab[...]).astype(BF16)
    t_pair = remote(t_own, t_sib, sib_send.at[2], sib_recv.at[2], sib)
    image = dot(xtab[0], t_own[...])
    t_pair.wait_recv()
    image = image + dot(xtab[1], t_sib[...])
    for t in range(CHIPS):
        block = image[OUT * t : OUT * (t + 1)]
        part_out[t] = jnp.concatenate(
            [block[:, 128 * i : 128 * i + 128] for i in range(3)] + [jnp.zeros((PACK - 3 * OUT, 128), F32)], axis=0
        ).astype(BF16)
    parts = [
        remote(
            part_out.at[(z + k) % CHIPS], part_in.at[k], part_send.at[k], part_recv.at[k], {"exp": along(k)}
        )
        for k in FAR
    ]
    total = part_out[z].astype(F32)
    for k, copy in reversed(list(zip(FAR, parts))):
        copy.wait_recv()
        total = total + part_in[k].astype(F32)
    for i in range(3):
        out[0, :, 128 * i : 128 * i + 128] = total[OUT * i : OUT * (i + 1)]
    for copy in halos + psf_copies + [psf_pair, num_pair, t_pair] + num_copies + parts:
        copy.wait_send()

    @pl.when((p == 1) & (z < CHIPS - 1))
    def _():
        extra(z).wait_send()


def body(stamps, footprint, psf_anchor, psf_degree, psf_powers, psf_basis, flux, variance):
    ftab, wtab, pgt, pgw, ytab, xtab, taper = (jnp.asarray(t) for t in tables())
    vmem = pl.BlockSpec(memory_space=pltpu.VMEM)
    hbm = pl.BlockSpec(memory_space=pl.ANY)
    dma = pltpu.SemaphoreType.DMA
    return pl.pallas_call(
        kernel,
        out_shape=jax.ShapeDtypeStruct((1, OUT, CORE), F32),
        in_specs=[hbm] * 15,
        out_specs=vmem,
        scratch_shapes=[
            pltpu.SMEM((2, 4), jnp.int32),
            pltpu.SMEM((2, 2), jnp.int32),
            pltpu.SMEM((2,), jnp.int32),
            pltpu.SMEM((2, 2, NBASIS), jnp.int32),
            pltpu.SMEM((2,), F32),
            pltpu.SMEM((2,), F32),
            pltpu.VMEM((NBASIS, 2, PS * PS), F32),
            pltpu.VMEM(pgt.shape, BF16),
            pltpu.VMEM(taper.shape, F32),
            pltpu.VMEM((2, 2, CORE, 128), BF16),
            pltpu.VMEM((2, 2, ROWS, 2 * TILE), F32),
            pltpu.VMEM((2, 2 * HALO, CORE), BF16),
            pltpu.VMEM((CORE, 128), BF16),
            pltpu.VMEM((CORE, 128), BF16),
            pltpu.VMEM((TILE, 128), BF16),
            pltpu.VMEM((TILE, 128), BF16),
            pltpu.VMEM((2, TILE, TILE), BF16),
            pltpu.VMEM(ftab.shape, BF16),
            pltpu.VMEM(wtab.shape, BF16),
            pltpu.VMEM(pgw.shape, BF16),
            pltpu.VMEM(ytab.shape, BF16),
            pltpu.VMEM(xtab.shape[1:], BF16),
            pltpu.VMEM((PS + BLK, 128), BF16),
            pltpu.VMEM((PS + BLK, 128), BF16),
            pltpu.VMEM((CHIPS, PS + BLK, 128), BF16),
            pltpu.VMEM((2, ROWS, TILE), BF16),
            pltpu.VMEM((2, ROWS, TILE), BF16),
            pltpu.VMEM((2, ROWS, TILE), F32),
            pltpu.VMEM((2, ROWS, TILE), BF16),
            pltpu.VMEM((CHIPS, 2, BLK, TILE), BF16),
            pltpu.VMEM((CHIPS - 1, 2, BLK, TILE), BF16),
            pltpu.VMEM((2, BLK, TILE), F32),
            pltpu.VMEM((4 * BLK, CORE), BF16),
            pltpu.VMEM((4 * BLK, CORE), BF16),
            pltpu.VMEM((CHIPS, PACK, 128), BF16),
            pltpu.VMEM((CHIPS, PACK, 128), BF16),
            dma((17,)),
            dma((8,)),
            dma((8,)),
            dma((3,)),
            dma((3,)),
            dma((CHIPS,)),
            dma((CHIPS,)),
            dma((CHIPS,)),
            dma((CHIPS,)),
            dma,
            dma((CHIPS - 1,)),
            dma((CHIPS,)),
            dma((CHIPS,)),
        ],
        compiler_params=pltpu.CompilerParams(
            collective_id=0, has_side_effects=True, vmem_limit_bytes=64 * 1024 * 1024 - 65536
        ),
    )(
        footprint, psf_anchor, psf_degree, psf_powers.transpose(0, 2, 1), flux, variance,
        psf_basis.transpose(1, 0, 2), pgt, taper,
        stamps, ftab, wtab, pgw, ytab, xtab,
    )


def solution(mesh):
    in_specs = (
        P("exp", "trow", "tcol"),
        P("exp", None),
        P("exp", None),
        P("exp"),
        P("exp", None, None),
        P("exp", None, None),
        P("exp"),
        P("exp"),
    )
    out_specs = P("trow", "exp", "tcol")
    return jax.shard_map(body, mesh=mesh, in_specs=in_specs, out_specs=out_specs, check_vma=False)
```

```python
import functools
import math

import jax
import jax.numpy as jnp
import ml_dtypes
import numpy as np
from jax import lax
from jax.experimental import pallas as pl
from jax.experimental.pallas import tpu as pltpu
from jax.sharding import PartitionSpec as P

TILE = 512
HALO = 64
PS = 32
NBASIS = 10
CORE = 384
CHIPS = 8
SIDE = TILE // 2
LANES = 128
FAR = (4, 3, 5, 2, 6, 1, 7)
BLK = 16
HALF = CHIPS * BLK
ROWS = HALF + BLK
OUT = CORE // (2 * CHIPS)
PACK = 80
MESH = pl.DeviceIdType.MESH
F32 = jnp.float32
BF16 = jnp.bfloat16


def angles(a, b):
    return (a[:, None] * b[None, :] % TILE) * (2.0 * math.pi / TILE)


@functools.cache
def tables():
    freq = np.arange(TILE)
    pixel = (freq + HALO) % TILE
    offset = np.arange(PS) - PS // 2
    scale = 1.0 / math.sqrt(TILE)

    def bf(x):
        return np.asarray(x, np.float32).astype(ml_dtypes.bfloat16)

    rows = [np.arange(HALF * q, HALF * q + ROWS) for q in range(2)]
    live = [(u <= TILE // 2)[:, None] for u in rows]
    ftab = np.stack(
        [
            np.concatenate([np.cos(angles(u, pixel)) * k, -np.sin(angles(u, pixel)) * k]) * scale
            for u, k in zip(rows, live)
        ]
    )
    cos, sin = np.cos(angles(pixel, freq[:SIDE])), -np.sin(angles(pixel, freq[:SIDE]))
    sin[:, 0] = np.cos(angles(pixel, freq[SIDE : SIDE + 1]))[:, 0]
    wtab = np.concatenate([cos[:, :LANES], sin[:, :LANES], cos[:, LANES:], sin[:, LANES:]], 1) * scale
    pgt = np.stack(
        [np.concatenate([np.cos(angles(u, offset)) * k, -np.sin(angles(u, offset)) * k]) for u, k in zip(rows, live)]
    )
    minus = np.concatenate([freq[SIDE : SIDE + 1], freq[:SIDE:-1]])
    order = np.concatenate([freq[:LANES], minus[:LANES], freq[LANES:SIDE], minus[LANES:]])
    cos, sin = np.cos(angles(offset, order)), np.sin(angles(offset, order))
    cos, sin = np.tile(cos, (4, 1)), np.tile(sin, (4, 1))
    pgw = np.block([[cos, -sin], [sin, cos]])
    core = np.arange(CORE) + HALO
    ytab = np.concatenate([np.cos(angles(freq[:SIDE], core)), np.sin(angles(freq[:SIDE], core))]) * scale
    ytab[SIDE] = np.cos(angles(freq[SIDE : SIDE + 1], core))[0] * scale
    xtab = np.zeros((2 * CHIPS, 2, CHIPS * OUT, 4 * BLK))
    for z in range(CHIPS):
        for p in range(2):
            x = np.concatenate([OUT * (2 * t + p) + np.arange(OUT) for t in range(CHIPS)]) + HALO
            for side in range(2):
                q = p ^ side
                u = np.concatenate([q * HALF + BLK * z + np.arange(BLK), TILE // 2 + np.arange(BLK)])
                count = np.where((u == 0) | (u == TILE // 2), 1.0, 2.0)
                count[BLK:] = 0.0
                if z == CHIPS - 1 and q == 1:
                    count[BLK] = 1.0
                xtab[2 * z + p, side, :, : 2 * BLK] = np.cos(angles(x, u)) * scale * count
                xtab[2 * z + p, side, :, 2 * BLK :] = -np.sin(angles(x, u)) * scale * count
    edge = np.arange(HALO)
    dist = np.concatenate([HALO - 1 - edge, edge])
    line = np.sin(0.5 * math.pi * (dist + 0.5) / HALO) ** 2
    taper = np.stack([np.tile(line[:, None], (1, 128)), np.tile(line[None, :], (128, 1))]).astype(np.float32)
    return bf(ftab), bf(wtab), bf(pgt), bf(pgw), bf(ytab), bf(xtab), taper


def monomial(value, power):
    return jnp.where(
        power == 0,
        1.0,
        jnp.where(power == 1, value, jnp.where(power == 2, value * value, value * value * value)),
    )


def dot(a, b):
    return jnp.dot(a, b, preferred_element_type=F32)


def kernel(
    foot_h, anchor_h, degree_h, powers_h, flux_h, variance_h, basis_h, pgt_h, taper_h, stamps, ftab_h, wtab_h, pgw_h,
    ytab_h, xtab_h,
    out,
    foot, anchor, degree, powers, flux, variance, basis, pgt, taper, strip, otf_all, rowh, first, last, right, left, ap, ftab, wtab, pgw, ytab, xtab,
    psf_own, psf_sib, psf_all, num_sib_out, num_sib_in, num_own, num_out, num_in, ex_out, ex_in, ex_sum,
    t_own, t_sib, part_out,
    load_sem, halo_send, halo_recv, sib_send, sib_recv, psf_send, psf_recv, num_send, num_recv,
    ex_send, ex_recv, part_send, part_recv,
):
    group = lax.axis_index("exp")
    r = lax.axis_index("trow")
    c = lax.axis_index("tcol")
    z = group // 2
    p = group % 2
    sib = {"exp": group + 1 - 2 * p}

    def along(k):
        return 2 * ((z + k) % CHIPS) + p

    def near(dr, dc):
        return {"trow": (r + dr + 4) % 4, "tcol": (c + dc + 4) % 4}

    around = [(-1, -1), (-1, 1), (0, -1), (-1, 0), (1, 0), (0, 1), (1, -1), (1, 1)]
    inside = [(r + dr >= 0) & (r + dr < 4) & (c + dc >= 0) & (c + dc < 4) for dr, dc in around]
    barrier = pltpu.get_barrier_semaphore()
    for at, there in zip(around, inside):

        @pl.when(there)
        def _():
            pl.semaphore_signal(barrier, inc=1, device_id=near(*at), device_id_type=MESH)

    for k in FAR:
        pl.semaphore_signal(barrier, inc=1, device_id={"exp": along(k)}, device_id_type=MESH)
    pl.semaphore_signal(barrier, inc=1, device_id=sib, device_id_type=MESH)
    loads = []
    for i, (src, dst) in enumerate(
        [
            (stamps.at[:, :, pl.ds(0, 128)], strip.at[0]), (stamps.at[:, :, pl.ds(CORE - 128, 128)], strip.at[1]),
            (foot_h, foot), (anchor_h, anchor), (degree_h, degree), (powers_h, powers),
            (flux_h, flux), (variance_h, variance), (basis_h, basis), (pgt_h, pgt), (pgw_h, pgw),
            (stamps, ap.at[:, pl.ds(0, CORE), pl.ds(0, CORE)]), (taper_h, taper), (ftab_h, ftab), (wtab_h, wtab),
            (ytab_h, ytab), (xtab_h.at[group], xtab),
        ]
    ):
        load = pltpu.make_async_copy(src, dst, load_sem.at[i])
        load.start()
        loads.append(load)

    def describe(src, dst, send, recv, where):
        return pltpu.make_async_remote_copy(
            src_ref=src, dst_ref=dst, send_sem=send, recv_sem=recv, device_id=where, device_id_type=MESH
        )

    def remote(*args):
        copy = describe(*args)
        copy.start()
        return copy

    def others(first_chips):
        place = jnp.where(z > 4, 2 * (z - 4) - 1, jnp.where(z == 0, CHIPS - 1, 2 * (4 - z))) if first_chips else z
        for i in range(CHIPS - 1):
            m = i + (i >= place).astype(jnp.int32)
            chip = jnp.where(m % 2 == 1, 4 + (m + 1) // 2, 4 - m // 2) if first_chips else m
            yield (chip - z + 2 * CHIPS) % CHIPS

    loads[0].wait()
    loads[1].wait()
    low = lax.broadcasted_iota(jnp.int32, (CORE, 128), 1) < HALO
    first[...] = jnp.where(low, strip[0, 0].astype(F32), pltpu.roll(strip[0, 1].astype(F32), HALO, 1)).astype(BF16)
    last[...] = jnp.where(low, pltpu.roll(strip[1, 0].astype(F32), HALO, 1), strip[1, 1].astype(F32)).astype(BF16)
    pl.semaphore_wait(barrier, sum(there.astype(jnp.int32) for there in inside) + CHIPS)
    top, low_rows = pl.ds(0, HALO), pl.ds(CORE - HALO, HALO)
    at_next, at_prev = pl.ds(CORE, HALO), pl.ds(CORE + HALO, HALO)
    pieces = [
        (first.at[top, :], right.at[at_next, :]),
        (last.at[top, :], left.at[at_next, :]),
        (first, right.at[pl.ds(0, CORE), :]),
        (stamps.at[:, top, :], rowh.at[:, pl.ds(0, HALO), :]),
        (stamps.at[:, low_rows, :], rowh.at[:, pl.ds(HALO, HALO), :]),
        (last, left.at[pl.ds(0, CORE), :]),
        (first.at[low_rows, :], right.at[at_prev, :]),
        (last.at[low_rows, :], left.at[at_prev, :]),
    ]
    halos = [
        describe(src, dst, halo_send.at[i], halo_recv.at[i], near(*around[i])) for i, (src, dst) in enumerate(pieces)
    ]
    for i in (0, 1, 6, 7, 2, 5, 3, 4):
        pl.when(inside[i])(halos[i].start)
    for i, (_, dst) in enumerate(pieces):

        @pl.when(jnp.logical_not(inside[7 - i]))
        def _():
            dst[...] = jnp.zeros(dst.shape, BF16)

    for load in loads[2:9]:
        load.wait()

    lane32 = lax.broadcasted_iota(jnp.int32, (PS, 128), 1)
    row32 = lax.broadcasted_iota(jnp.int32, (PS, 128), 0)
    slot32 = lane32 // PS
    fold = jnp.where(
        lax.broadcasted_iota(jnp.int32, (128, 128), 0) % PS == lax.broadcasted_iota(jnp.int32, (128, 128), 1) % PS,
        1.0,
        0.0,
    ).astype(BF16)
    lane16 = lax.broadcasted_iota(jnp.int32, (BLK, 128), 1) // PS
    row16 = lax.broadcasted_iota(jnp.int32, (BLK, 128), 0)
    psf = jnp.zeros((PS, 128), F32)
    wrow = jnp.zeros((BLK, 128), F32)
    wnum = []
    for e in range(2):
        ux = (c * CORE + CORE // 2 - anchor[e, 1]).astype(F32) / (2.0 * CORE)
        uy = (r * CORE + CORE // 2 - anchor[e, 0]).astype(F32) / (2.0 * CORE)
        flat = jnp.zeros((1, PS * PS), F32)
        for k in range(NBASIS):
            px, qy = powers[e, 0, k], powers[e, 1, k]
            term = jnp.where(px + qy <= degree[e], monomial(ux, px) * monomial(uy, qy), 0.0)
            flat = flat + term * basis[k, e : e + 1, :]
        spread = jnp.zeros((PS, 128), F32)
        for t in range(PS * PS // 128):
            spread = jnp.where(
                (row32 // 4 == t) & (slot32 == row32 % 4),
                jnp.broadcast_to(flat[:, 128 * t : 128 * t + 128], (PS, 128)),
                spread,
            )
        mine = 2 * p + e
        psf = jnp.where(slot32 == mine, dot(spread.astype(BF16), fold), psf)
        active = (foot[e, 0] <= r) & (r < foot[e, 1]) & (foot[e, 2] <= c) & (c < foot[e, 3])
        gain = jnp.where(active, flux[e], 0.0)
        wnum.append(jnp.full((8, 128), gain, F32) / jnp.full((8, 128), variance[e], F32))
        wden = jnp.full((BLK, 128), gain * flux[e], F32) / jnp.full((BLK, 128), variance[e], F32)
        wrow = jnp.where(lane16 == mine, wden, wrow)
    high = wrow.astype(BF16).astype(F32)
    rest = wrow - high
    mid = rest.astype(BF16).astype(F32)
    wrow = jnp.where(row16 == 0, high, jnp.where(row16 == 1, mid, jnp.where(row16 == 2, rest - mid, 0.0)))
    psf_own[0:PS, :] = psf.astype(BF16)
    psf_own[PS : PS + BLK, :] = wrow.astype(BF16)
    psf_pair = remote(psf_own, psf_sib, sib_send.at[0], sib_recv.at[0], sib)


    loads[9].wait()
    loads[10].wait()
    stamp = psf_own[0:PS, :]
    lane_r = lax.broadcasted_iota(jnp.int32, (2 * ROWS, 128), 1) // PS
    for side in range(2):
        lift = dot(pgt[1 - p if side == 0 else p], stamp)
        for e in range(2):
            one = jnp.where(lane_r == 2 * p + e, lift, 0.0).astype(BF16)
            otf_all[side, e] = dot(jnp.concatenate([one[:ROWS], one[ROWS:]], axis=1), pgw[...])
        if side == 0:
            psf_pair.wait_recv()
            psf_all[0] = (psf_own[...].astype(F32) + psf_sib[...].astype(F32)).astype(BF16)
            psf_copies = [
                remote(psf_all.at[0], psf_all.at[k], psf_send.at[k], psf_recv.at[k], {"exp": along(k)}) for k in FAR
            ]

    for load in loads[11:15]:
        load.wait()
    for i, copy in enumerate(halos):
        pl.when(inside[7 - i])(copy.wait_recv)
    cover = []
    for e in range(2):
        cover.append(
            [
                jnp.where((foot[e, lo] <= at) & (at < foot[e, lo + 1]), 1.0, 0.0)
                for lo, at in ((0, r + 1), (0, r - 1), (2, c + 1), (2, c - 1))
            ]
        )
    lane_s = lax.broadcasted_iota(jnp.int32, (TILE, 128), 1) < HALO
    line_r = taper[0]
    line_c = taper[1]
    right_v, left_v = right[...].astype(F32), left[...].astype(F32)
    right_t, left_t = pltpu.roll(right_v, HALO, 1), pltpu.roll(left_v, HALO, 1)
    for e in range(2):
        up, down, after, before = cover[e]
        wide = jnp.concatenate([line_r] * 3, axis=1)
        ap[e, CORE : CORE + HALO, 0:CORE] = (rowh[e, 0:HALO, :].astype(F32) * (wide[0:HALO] * up)).astype(BF16)
        ap[e, CORE + HALO : TILE, 0:CORE] = (rowh[e, HALO:, :].astype(F32) * (wide[HALO:] * down)).astype(BF16)
        side = jnp.where(lane_s, right_v, left_t) if e == 0 else jnp.where(lane_s, right_t, left_v)
        keep = jnp.where(lane_s[0:128], after, before) * line_c
        for t in range(3):
            ap[e, 128 * t : 128 * t + 128, CORE:TILE] = (side[128 * t : 128 * t + 128] * keep).astype(BF16)
        corner = side[CORE:TILE]
        taper2 = line_r * line_c * jnp.where(lane_s[0:128], after, before)
        ap[e, CORE : CORE + HALO, CORE:TILE] = (corner[0:HALO] * (taper2[0:HALO] * up)).astype(BF16)
        ap[e, CORE + HALO : TILE, CORE:TILE] = (corner[HALO:] * (taper2[HALO:] * down)).astype(BF16)

    lane0 = lax.broadcasted_iota(jnp.int32, (ROWS, LANES), 1) == 0

    def halves(q):
        return [dot(ftab[q], ap[e]).astype(BF16) for e in range(2)]

    def numerator(half, side, chunk):
        cols = slice(SIDE * chunk, SIDE * chunk + SIDE)
        total_re = total_im = None
        for e in range(2):
            prod = dot(half[e], wtab[:, cols])
            re_cos, re_sin = prod[:ROWS, :LANES], prod[:ROWS, LANES:]
            im_cos, im_sin = prod[ROWS:, :LANES], prod[ROWS:, LANES:]
            if chunk == 0:
                plus = [re_cos - jnp.where(lane0, 0.0, im_sin), im_cos + jnp.where(lane0, 0.0, re_sin)]
                minus = [jnp.where(lane0, re_sin, re_cos + im_sin), jnp.where(lane0, im_sin, im_cos - re_sin)]
            else:
                plus = [re_cos - im_sin, im_cos + re_sin]
                minus = [re_cos + im_sin, im_cos - re_sin]
            spec_re, spec_im = (jnp.concatenate(pair, axis=1) for pair in zip(plus, minus))
            otf_re = otf_all[side, e, :, cols]
            otf_im = otf_all[side, e, :, TILE + SIDE * chunk : TILE + SIDE * chunk + SIDE]
            w = wnum[e][0:1, 0:1]
            part_re = w * (otf_re * spec_re + otf_im * spec_im)
            part_im = w * (otf_re * spec_im - otf_im * spec_re)
            total_re = part_re if e == 0 else total_re + part_re
            total_im = part_im if e == 0 else total_im + part_im
        return total_re, total_im

    def num_copy(chunk, k):
        return describe(
            num_out.at[chunk, :, pl.ds(pl.multiple_of(BLK * ((z + k) % CHIPS), BLK), BLK), :],
            num_in.at[chunk, k],
            num_send.at[chunk, k],
            num_recv.at[chunk, k],
            {"exp": along(k)},
        )

    half = halves(1 - p)
    num_pairs = []
    for chunk in range(2):
        for i, part in enumerate(numerator(half, 0, chunk)):
            num_sib_out[chunk, i] = part.astype(BF16)
        num_pairs.append(
            remote(num_sib_out.at[chunk], num_sib_in.at[chunk], sib_send.at[1 + chunk], sib_recv.at[1 + chunk], sib)
        )
    half = halves(p)
    num_copies = []
    for chunk in range(2):
        parts = numerator(half, 1, chunk)
        num_pairs[chunk].wait_recv()
        for i, part in enumerate(parts):
            part = part + num_sib_in[chunk, i].astype(F32)
            num_own[i, :, SIDE * chunk : SIDE * chunk + SIDE] = part
            num_out[chunk, i] = part[:HALF].astype(BF16)
            ex_out[i, :, SIDE * chunk : SIDE * chunk + SIDE] = part[HALF:].astype(BF16)
        for k in others(True):
            num_copy(chunk, k).start()
        num_copies += [num_copy(chunk, k) for k in FAR]

    def extra(at):
        return pltpu.make_async_remote_copy(
            src_ref=ex_out,
            dst_ref=ex_in.at[at],
            send_sem=ex_send,
            recv_sem=ex_recv.at[at],
            device_id={"exp": 2 * CHIPS - 1},
            device_id_type=MESH,
        )

    @pl.when((p == 1) & (z < CHIPS - 1))
    def _():
        extra(z).start()

    for copy in psf_copies:
        copy.wait_recv()
    start = pl.multiple_of(BLK * z, BLK)
    pgz = jnp.concatenate(
        [
            pgt[p, pl.ds(start, BLK), :],
            pgt[p, HALF:ROWS, :],
            pgt[p, pl.ds(pl.multiple_of(start + ROWS, BLK), BLK), :],
            pgt[p, ROWS + HALF :, :],
        ],
        axis=0,
    )
    lane_d = lax.broadcasted_iota(jnp.int32, (4 * BLK, 128), 1) // PS

    def add_den(g, den):
        lift = dot(pgz, psf_all[g, 0:PS, :])
        weights = jnp.sum(psf_all[g, PS : PS + BLK, :].astype(F32), axis=0, keepdims=True)
        ones = [jnp.where(lane_d == t, lift, 0.0).astype(BF16) for t in range(4)]
        lhs = jnp.concatenate(
            [jnp.concatenate([one[: 2 * BLK], one[2 * BLK :]], axis=1) for one in ones], axis=0
        )
        otf = dot(lhs, pgw[...])
        power = otf[:, :TILE] * otf[:, :TILE] + otf[:, TILE:] * otf[:, TILE:]
        for t in range(4):
            den = den + weights[:, PS * t : PS * t + 1] * power[2 * BLK * t : 2 * BLK * (t + 1)]
        return den

    den = lax.fori_loop(0, CHIPS, add_den, jnp.zeros((2 * BLK, TILE), F32))

    ex_sum[...] = jnp.zeros_like(ex_sum)

    @pl.when(group == 2 * CHIPS - 1)
    def _():
        for t in range(CHIPS - 1):
            extra(t).wait_recv()
        total = num_own[:, HALF:ROWS, :]
        for t in range(CHIPS - 1):
            total = total + ex_in[t].astype(F32)
        ex_sum[...] = total

    sums = num_own[:, pl.ds(start, BLK), :]
    for i in reversed(range(len(FAR))):
        num_copies[i].wait_recv()
        num_copies[len(FAR) + i].wait_recv()
        k = FAR[i]
        sums = sums + jnp.concatenate([num_in[0, k], num_in[1, k]], axis=2).astype(F32)
    norm = lax.rsqrt(den + 1.0)
    s_re = jnp.concatenate([sums[0], ex_sum[0]], axis=0) * norm
    s_im = jnp.concatenate([sums[1], ex_sum[1]], axis=0) * norm
    loads[15].wait()
    loads[16].wait()
    lane0 = lax.broadcasted_iota(jnp.int32, (2 * BLK, SIDE), 1) == 0
    (re_p, re_m), (im_p, im_m) = (
        [jnp.concatenate([x[:, at : at + LANES], x[:, SIDE + at : SIDE + at + LANES]], axis=1) for at in (0, LANES)]
        for x in (s_re, s_im)
    )
    top_rows = [jnp.where(lane0, re_p, re_p + re_m), jnp.where(lane0, re_m, im_m - im_p)]
    low_rows = [jnp.where(lane0, im_p, im_p + im_m), jnp.where(lane0, im_m, re_p - re_m)]
    folded = jnp.concatenate([jnp.concatenate(top_rows, axis=1), jnp.concatenate(low_rows, axis=1)], axis=0)
    t_own[...] = dot(folded.astype(BF16), ytab[...]).astype(BF16)
    t_pair = remote(t_own, t_sib, sib_send.at[3], sib_recv.at[3], sib)
    image = dot(xtab[0], t_own[...])
    t_pair.wait_recv()
    image = image + dot(xtab[1], t_sib[...])
    for t in range(CHIPS):
        block = image[OUT * t : OUT * (t + 1)]
        part_out[t] = jnp.concatenate(
            [block[:, 128 * i : 128 * i + 128] for i in range(3)] + [jnp.zeros((PACK - 3 * OUT, 128), F32)], axis=0
        ).astype(BF16)
    def part_copy(k):
        return describe(
            part_out.at[(z + k) % CHIPS], out.at[k], part_send.at[k], part_recv.at[k], {"exp": along(k)}
        )

    for k in others(False):
        part_copy(k).start()
    parts = [part_copy(k) for k in FAR]
    mine = pltpu.make_async_copy(part_out.at[z], out.at[0], load_sem.at[0])
    mine.start()
    mine.wait()
    for copy in parts:
        copy.wait_recv()
    for i, copy in enumerate(halos):
        pl.when(inside[i])(copy.wait_send)
    for copy in psf_copies + num_pairs + [psf_pair, t_pair] + num_copies + parts:
        copy.wait_send()

    @pl.when((p == 1) & (z < CHIPS - 1))
    def _():
        extra(z).wait_send()


def finish(parts, out):
    total = jnp.sum(parts[...].astype(F32), axis=0)
    for i in range(3):
        out[0, :, LANES * i : LANES * (i + 1)] = total[OUT * i : OUT * (i + 1)]


def body(stamps, footprint, psf_anchor, psf_degree, psf_powers, psf_basis, flux, variance):
    ftab, wtab, pgt, pgw, ytab, xtab, taper = (jnp.asarray(t) for t in tables())
    vmem = pl.BlockSpec(memory_space=pltpu.VMEM)
    hbm = pl.BlockSpec(memory_space=pl.ANY)
    dma = pltpu.SemaphoreType.DMA
    parts = pl.pallas_call(
        kernel,
        out_shape=jax.ShapeDtypeStruct((CHIPS, PACK, 128), BF16),
        in_specs=[hbm] * 15,
        out_specs=hbm,
        scratch_shapes=[
            pltpu.SMEM((2, 4), jnp.int32),
            pltpu.SMEM((2, 2), jnp.int32),
            pltpu.SMEM((2,), jnp.int32),
            pltpu.SMEM((2, 2, NBASIS), jnp.int32),
            pltpu.SMEM((2,), F32),
            pltpu.SMEM((2,), F32),
            pltpu.VMEM((NBASIS, 2, PS * PS), F32),
            pltpu.VMEM(pgt.shape, BF16),
            pltpu.VMEM(taper.shape, F32),
            pltpu.VMEM((2, 2, CORE, 128), BF16),
            pltpu.VMEM((2, 2, ROWS, 2 * TILE), F32),
            pltpu.VMEM((2, 2 * HALO, CORE), BF16),
            pltpu.VMEM((CORE, 128), BF16),
            pltpu.VMEM((CORE, 128), BF16),
            pltpu.VMEM((TILE, 128), BF16),
            pltpu.VMEM((TILE, 128), BF16),
            pltpu.VMEM((2, TILE, TILE), BF16),
            pltpu.VMEM(ftab.shape, BF16),
            pltpu.VMEM(wtab.shape, BF16),
            pltpu.VMEM(pgw.shape, BF16),
            pltpu.VMEM(ytab.shape, BF16),
            pltpu.VMEM(xtab.shape[1:], BF16),
            pltpu.VMEM((PS + BLK, 128), BF16),
            pltpu.VMEM((PS + BLK, 128), BF16),
            pltpu.VMEM((CHIPS, PS + BLK, 128), BF16),
            pltpu.VMEM((2, 2, ROWS, SIDE), BF16),
            pltpu.VMEM((2, 2, ROWS, SIDE), BF16),
            pltpu.VMEM((2, ROWS, TILE), F32),
            pltpu.VMEM((2, 2, HALF, SIDE), BF16),
            pltpu.VMEM((2, CHIPS, 2, BLK, SIDE), BF16),
            pltpu.VMEM((2, BLK, TILE), BF16),
            pltpu.VMEM((CHIPS - 1, 2, BLK, TILE), BF16),
            pltpu.VMEM((2, BLK, TILE), F32),
            pltpu.VMEM((4 * BLK, CORE), BF16),
            pltpu.VMEM((4 * BLK, CORE), BF16),
            pltpu.VMEM((CHIPS, PACK, 128), BF16),
            dma((17,)),
            dma((8,)),
            dma((8,)),
            dma((4,)),
            dma((4,)),
            dma((CHIPS,)),
            dma((CHIPS,)),
            dma((2, CHIPS)),
            dma((2, CHIPS)),
            dma,
            dma((CHIPS - 1,)),
            dma((CHIPS,)),
            dma((CHIPS,)),
        ],
        compiler_params=pltpu.CompilerParams(
            collective_id=0, has_side_effects=True, vmem_limit_bytes=64 * 1024 * 1024 - 65536
        ),
    )(
        footprint, psf_anchor, psf_degree, psf_powers.transpose(0, 2, 1), flux, variance,
        psf_basis.transpose(1, 0, 2), pgt, taper,
        stamps, ftab, wtab, pgw, ytab, xtab,
    )
    return pl.pallas_call(
        finish, out_shape=jax.ShapeDtypeStruct((1, OUT, CORE), F32), in_specs=[vmem], out_specs=vmem
    )(parts)


def solution(mesh):
    in_specs = (
        P("exp", "trow", "tcol"),
        P("exp", None),
        P("exp", None),
        P("exp"),
        P("exp", None, None),
        P("exp", None, None),
        P("exp"),
        P("exp"),
    )
    out_specs = P("trow", "exp", "tcol")
    return jax.shard_map(body, mesh=mesh, in_specs=in_specs, out_specs=out_specs, check_vma=False)
```

```python
import functools
import math

import jax
import jax.numpy as jnp
import ml_dtypes
import numpy as np
from jax import lax
from jax.experimental import pallas as pl
from jax.experimental.pallas import tpu as pltpu
from jax.sharding import PartitionSpec as P

TILE = 512
HALO = 64
PS = 32
NBASIS = 10
CORE = 384
CHIPS = 8
SIDE = TILE // 2
LANES = 128
FAR = (4, 3, 5, 2, 6, 1, 7)
NUM_ORDER = (3, 2, 1, 4, 0, 5, 6, 7)
PART_ORDER = (0, 1, 2, 3, 4, 5, 6, 7)
BLK = 16
HALF = CHIPS * BLK
ROWS = HALF + BLK
OUT = CORE // (2 * CHIPS)
PACK = 80
MESH = pl.DeviceIdType.MESH
F32 = jnp.float32
BF16 = jnp.bfloat16


def angles(a, b):
    return (a[:, None] * b[None, :] % TILE) * (2.0 * math.pi / TILE)


@functools.cache
def tables():
    freq = np.arange(TILE)
    pixel = (freq + HALO) % TILE
    offset = np.arange(PS) - PS // 2
    scale = 1.0 / math.sqrt(TILE)

    def bf(x):
        return np.asarray(x, np.float32).astype(ml_dtypes.bfloat16)

    rows = [np.arange(HALF * q, HALF * q + ROWS) for q in range(2)]
    live = [(u <= TILE // 2)[:, None] for u in rows]
    ftab = np.stack(
        [
            np.concatenate([np.cos(angles(u, pixel)) * k, -np.sin(angles(u, pixel)) * k]) * scale
            for u, k in zip(rows, live)
        ]
    )
    cos, sin = np.cos(angles(pixel, freq[:SIDE])), -np.sin(angles(pixel, freq[:SIDE]))
    sin[:, 0] = np.cos(angles(pixel, freq[SIDE : SIDE + 1]))[:, 0]
    wtab = np.concatenate([cos[:, :LANES], sin[:, :LANES], cos[:, LANES:], sin[:, LANES:]], 1) * scale
    pgt = np.stack(
        [np.concatenate([np.cos(angles(u, offset)) * k, -np.sin(angles(u, offset)) * k]) for u, k in zip(rows, live)]
    )
    minus = np.concatenate([freq[SIDE : SIDE + 1], freq[:SIDE:-1]])
    order = np.concatenate([freq[:LANES], minus[:LANES], freq[LANES:SIDE], minus[LANES:]])
    cos, sin = np.cos(angles(offset, order)), np.sin(angles(offset, order))
    cos, sin = np.tile(cos, (4, 1)), np.tile(sin, (4, 1))
    pgw = np.block([[cos, -sin], [sin, cos]])
    core = np.arange(CORE) + HALO
    ytab = np.concatenate([np.cos(angles(freq[:SIDE], core)), np.sin(angles(freq[:SIDE], core))]) * scale
    ytab[SIDE] = np.cos(angles(freq[SIDE : SIDE + 1], core))[0] * scale
    xtab = np.zeros((2 * CHIPS, 2, CHIPS * OUT, 4 * BLK))
    for z in range(CHIPS):
        for p in range(2):
            x = np.concatenate([OUT * (2 * t + p) + np.arange(OUT) for t in range(CHIPS)]) + HALO
            for side in range(2):
                q = p ^ side
                u = np.concatenate([q * HALF + BLK * z + np.arange(BLK), TILE // 2 + np.arange(BLK)])
                count = np.where((u == 0) | (u == TILE // 2), 1.0, 2.0)
                count[BLK:] = 0.0
                if z == CHIPS - 1 and q == 1:
                    count[BLK] = 1.0
                xtab[2 * z + p, side, :, : 2 * BLK] = np.cos(angles(x, u)) * scale * count
                xtab[2 * z + p, side, :, 2 * BLK :] = -np.sin(angles(x, u)) * scale * count
    edge = np.arange(HALO)
    dist = np.concatenate([HALO - 1 - edge, edge])
    line = np.sin(0.5 * math.pi * (dist + 0.5) / HALO) ** 2
    taper = np.stack([np.tile(line[:, None], (1, 128)), np.tile(line[None, :], (128, 1))]).astype(np.float32)
    return bf(ftab), bf(wtab), bf(pgt), bf(pgw), bf(ytab), bf(xtab), taper


def monomial(value, power):
    return jnp.where(
        power == 0,
        1.0,
        jnp.where(power == 1, value, jnp.where(power == 2, value * value, value * value * value)),
    )


def dot(a, b):
    return jnp.dot(a, b, preferred_element_type=F32)


def kernel(
    foot_h, anchor_h, degree_h, powers_h, flux_h, variance_h, basis_h, pgt_h, taper_h, stamps, ftab_h, wtab_h, pgw_h,
    ytab_h, xtab_h,
    out,
    foot, anchor, degree, powers, flux, variance, basis, pgt, taper, strip, otf_all, num_first, rowh, cols, cols_in, corners,
    corners_in, ap, ftab, wtab, pgw, ytab, xtab,
    psf_own, psf_sib, psf_all, num_sib_out, num_sib_in, num_own, num_out, num_in, ex_out, ex_in, ex_sum,
    t_own, t_sib, part_out,
    load_sem, halo_send, halo_recv, sib_send, sib_recv, psf_send, psf_recv, num_send, num_recv,
    ex_send, ex_recv, part_send, part_recv, ready,
):
    group = lax.axis_index("exp")
    r = lax.axis_index("trow")
    c = lax.axis_index("tcol")
    z = group // 2
    p = group % 2
    sib = {"exp": group + 1 - 2 * p}

    def along(k):
        return 2 * ((z + k) % CHIPS) + p

    def near(dr, dc):
        return {"trow": (r + dr + 4) % 4, "tcol": (c + dc + 4) % 4}

    around = [(-1, -1), (-1, 1), (0, -1), (-1, 0), (1, 0), (0, 1), (1, -1), (1, 1)]
    inside = [(r + dr >= 0) & (r + dr < 4) & (c + dc >= 0) & (c + dc < 4) for dr, dc in around]
    barrier = pltpu.get_barrier_semaphore()
    for at, there in zip(around, inside):

        @pl.when(there)
        def _():
            pl.semaphore_signal(barrier, inc=1, device_id=near(*at), device_id_type=MESH)

    for k in FAR:

        @pl.when((z + k) % CHIPS > z)
        def _():
            pl.semaphore_signal(barrier, inc=1, device_id={"exp": along(k)}, device_id_type=MESH)

    pl.semaphore_signal(barrier, inc=1, device_id=sib, device_id_type=MESH)
    loads = []
    for i, (src, dst) in enumerate(
        [
            (stamps.at[:, :, pl.ds(0, 128)], strip.at[0]), (stamps.at[:, :, pl.ds(CORE - 128, 128)], strip.at[1]),
            (foot_h, foot), (anchor_h, anchor), (degree_h, degree), (powers_h, powers),
            (flux_h, flux), (variance_h, variance), (basis_h, basis), (pgt_h, pgt), (pgw_h, pgw),
            (stamps, ap.at[:, pl.ds(0, CORE), pl.ds(0, CORE)]), (taper_h, taper), (ftab_h, ftab), (wtab_h, wtab),
            (ytab_h, ytab), (xtab_h.at[group], xtab),
        ]
    ):
        load = pltpu.make_async_copy(src, dst, load_sem.at[i])
        load.start()
        loads.append(load)

    def describe(src, dst, send, recv, where):
        return pltpu.make_async_remote_copy(
            src_ref=src, dst_ref=dst, send_sem=send, recv_sem=recv, device_id=where, device_id_type=MESH
        )

    def remote(*args):
        copy = describe(*args)
        copy.start()
        return copy

    def to_others(chips, copy):
        for chip in chips:
            pl.when(z != chip)(lambda chip=chip: copy((chip - z + CHIPS) % CHIPS).start())

    loads[0].wait()
    loads[1].wait()
    low = lax.broadcasted_iota(jnp.int32, (CORE // 2, 128), 1) < HALO
    turned = [[pltpu.roll(strip[side, e].astype(F32), HALO, 1) for e in range(2)] for side in range(2)]
    for e in range(2):
        cols[0, e] = jnp.where(low, strip[0, e, : CORE // 2].astype(F32), turned[0][e][CORE // 2 :]).astype(BF16)
        cols[1, e] = jnp.where(low, turned[1][e][: CORE // 2], strip[1, e, CORE // 2 :].astype(F32)).astype(BF16)
    for i, rows in enumerate((slice(0, HALO), slice(CORE - HALO, CORE))):
        corners[i, 0] = jnp.where(low[:HALO], strip[0, 0, rows].astype(F32), turned[0][1][rows]).astype(BF16)
        corners[i, 1] = jnp.where(low[:HALO], turned[1][0][rows], strip[1, 1, rows].astype(F32)).astype(BF16)
    pl.semaphore_wait(barrier, sum(there.astype(jnp.int32) for there in inside) + 1 + z)
    pieces = [
        (0, corners.at[0, 0], corners_in.at[0, 0]),
        (1, corners.at[0, 1], corners_in.at[0, 1]),
        (6, corners.at[1, 0], corners_in.at[1, 0]),
        (7, corners.at[1, 1], corners_in.at[1, 1]),
    ]
    for e in range(2):
        pieces += [
            (2, cols.at[0, e], cols_in.at[0, e]),
            (5, cols.at[1, e], cols_in.at[1, e]),
            (3, stamps.at[e, pl.ds(0, HALO), :], rowh.at[e, pl.ds(0, HALO), :]),
            (4, stamps.at[e, pl.ds(CORE - HALO, HALO), :], rowh.at[e, pl.ds(HALO, HALO), :]),
        ]
    halos = [
        (i, describe(src, dst, halo_send.at[n], halo_recv.at[n], near(*around[i])))
        for n, (i, src, dst) in enumerate(pieces)
    ]
    for i, copy in halos:
        pl.when(inside[i])(copy.start)
    for k in FAR:

        @pl.when((z + k) % CHIPS < z)
        def _():
            pl.semaphore_signal(ready.at[CHIPS - k], inc=1, device_id={"exp": along(k)}, device_id_type=MESH)

    for i, _, dst in pieces:

        @pl.when(jnp.logical_not(inside[7 - i]))
        def _():
            dst[...] = jnp.zeros(dst.shape, BF16)

    for load in loads[2:9]:
        load.wait()

    lane32 = lax.broadcasted_iota(jnp.int32, (PS, 128), 1)
    row32 = lax.broadcasted_iota(jnp.int32, (PS, 128), 0)
    slot32 = lane32 // PS
    fold = jnp.where(
        lax.broadcasted_iota(jnp.int32, (128, 128), 0) % PS == lax.broadcasted_iota(jnp.int32, (128, 128), 1) % PS,
        1.0,
        0.0,
    ).astype(BF16)
    lane16 = lax.broadcasted_iota(jnp.int32, (BLK, 128), 1) // PS
    row16 = lax.broadcasted_iota(jnp.int32, (BLK, 128), 0)
    psf = jnp.zeros((PS, 128), F32)
    wrow = jnp.zeros((BLK, 128), F32)
    wnum = []
    for e in range(2):
        ux = (c * CORE + CORE // 2 - anchor[e, 1]).astype(F32) / (2.0 * CORE)
        uy = (r * CORE + CORE // 2 - anchor[e, 0]).astype(F32) / (2.0 * CORE)
        flat = jnp.zeros((1, PS * PS), F32)
        for k in range(NBASIS):
            px, qy = powers[e, 0, k], powers[e, 1, k]
            term = jnp.where(px + qy <= degree[e], monomial(ux, px) * monomial(uy, qy), 0.0)
            flat = flat + term * basis[k, e : e + 1, :]
        spread = jnp.zeros((PS, 128), F32)
        for t in range(PS * PS // 128):
            spread = jnp.where(
                (row32 // 4 == t) & (slot32 == row32 % 4),
                jnp.broadcast_to(flat[:, 128 * t : 128 * t + 128], (PS, 128)),
                spread,
            )
        mine = 2 * p + e
        psf = jnp.where(slot32 == mine, dot(spread.astype(BF16), fold), psf)
        active = (foot[e, 0] <= r) & (r < foot[e, 1]) & (foot[e, 2] <= c) & (c < foot[e, 3])
        gain = jnp.where(active, flux[e], 0.0)
        wnum.append(jnp.full((8, 128), gain, F32) / jnp.full((8, 128), variance[e], F32))
        wden = jnp.full((BLK, 128), gain * flux[e], F32) / jnp.full((BLK, 128), variance[e], F32)
        wrow = jnp.where(lane16 == mine, wden, wrow)
    high = wrow.astype(BF16).astype(F32)
    rest = wrow - high
    mid = rest.astype(BF16).astype(F32)
    wrow = jnp.where(row16 == 0, high, jnp.where(row16 == 1, mid, jnp.where(row16 == 2, rest - mid, 0.0)))
    psf_own[0:PS, :] = psf.astype(BF16)
    psf_own[PS : PS + BLK, :] = wrow.astype(BF16)
    psf_pair = remote(psf_own, psf_sib, sib_send.at[0], sib_recv.at[0], sib)


    loads[9].wait()
    loads[10].wait()
    stamp = psf_own[0:PS, :]
    lane_r = lax.broadcasted_iota(jnp.int32, (2 * ROWS, 128), 1) // PS
    for side in range(2):
        lift = dot(pgt[1 - p if side == 0 else p], stamp)
        for e in range(2):
            one = jnp.where(lane_r == 2 * p + e, lift, 0.0).astype(BF16)
            otf_all[side, e] = dot(jnp.concatenate([one[:ROWS], one[ROWS:]], axis=1), pgw[...])

    for load in loads[11:15]:
        load.wait()
    lane_s = lax.broadcasted_iota(jnp.int32, (CORE, 128), 1) < HALO
    line_r = taper[0]
    line_c = taper[1]
    wide = jnp.concatenate([line_r] * 3, axis=1)

    def apodize(e):
        for i, copy in halos[4 + 4 * e : 8 + 4 * e]:
            pl.when(inside[7 - i])(copy.wait_recv)
        up, down, after, before = [
            jnp.where((foot[e, lo] <= at) & (at < foot[e, lo + 1]), 1.0, 0.0)
            for lo, at in ((0, r + 1), (0, r - 1), (2, c + 1), (2, c - 1))
        ]
        ap[e, CORE : CORE + HALO, 0:CORE] = (rowh[e, 0:HALO, :].astype(F32) * (wide[0:HALO] * up)).astype(BF16)
        ap[e, CORE + HALO : TILE, 0:CORE] = (rowh[e, HALO:, :].astype(F32) * (wide[HALO:] * down)).astype(BF16)
        right, left = cols_in[0, e].astype(F32), cols_in[1, e].astype(F32)
        side = jnp.concatenate(
            [jnp.where(low, right, pltpu.roll(left, HALO, 1)), jnp.where(low, pltpu.roll(right, HALO, 1), left)], axis=0
        )
        keep = jnp.where(lane_s, after, before)
        ap[e, 0:CORE, CORE:TILE] = (side * (jnp.concatenate([line_c] * 3, axis=0) * keep)).astype(BF16)
        for i, rows in enumerate((slice(0, HALO), slice(HALO, 2 * HALO))):
            right, left = corners_in[i, 0].astype(F32), corners_in[i, 1].astype(F32)
            if e == 0:
                corner = jnp.where(low[:HALO], right, pltpu.roll(left, HALO, 1))
            else:
                corner = jnp.where(low[:HALO], pltpu.roll(right, HALO, 1), left)
            taper2 = line_r[rows] * line_c[rows] * keep[:HALO] * (up if i == 0 else down)
            ap[e, CORE + HALO * i : CORE + HALO * (i + 1), CORE:TILE] = (corner * taper2).astype(BF16)

    lane0 = lax.broadcasted_iota(jnp.int32, (ROWS, LANES), 1) == 0

    def halved(q, e):
        return dot(ftab[q], ap[e]).astype(BF16)

    def numerator(half, side, chunk, e):
        cols = slice(SIDE * chunk, SIDE * chunk + SIDE)
        prod = dot(half, wtab[:, cols])
        re_cos, re_sin = prod[:ROWS, :LANES], prod[:ROWS, LANES:]
        im_cos, im_sin = prod[ROWS:, :LANES], prod[ROWS:, LANES:]
        if chunk == 0:
            plus = [re_cos - jnp.where(lane0, 0.0, im_sin), im_cos + jnp.where(lane0, 0.0, re_sin)]
            minus = [jnp.where(lane0, re_sin, re_cos + im_sin), jnp.where(lane0, im_sin, im_cos - re_sin)]
        else:
            plus = [re_cos - im_sin, im_cos + re_sin]
            minus = [re_cos + im_sin, im_cos - re_sin]
        spec_re, spec_im = (jnp.concatenate(pair, axis=1) for pair in zip(plus, minus))
        otf_re = otf_all[side, e, :, cols]
        otf_im = otf_all[side, e, :, TILE + SIDE * chunk : TILE + SIDE * chunk + SIDE]
        w = wnum[e][0:1, 0:1]
        return w * (otf_re * spec_re + otf_im * spec_im), w * (otf_re * spec_im - otf_im * spec_re)

    def num_copy(chunk, k):
        return describe(
            num_out.at[chunk, :, pl.ds(pl.multiple_of(BLK * ((z + k) % CHIPS), BLK), BLK), :],
            num_in.at[chunk, k],
            num_send.at[chunk, k],
            num_recv.at[chunk, k],
            {"exp": along(k)},
        )

    psf_pair.wait_recv()
    psf_all[0] = (psf_own[...].astype(F32) + psf_sib[...].astype(F32)).astype(BF16)
    psf_copies = [
        describe(psf_all.at[0], psf_all.at[k], psf_send.at[k], psf_recv.at[k], {"exp": along(k)}) for k in FAR
    ]
    for k, copy in zip(FAR, psf_copies):
        pl.when((z + k) % CHIPS < z)(copy.start)
    for i, copy in halos[:4]:
        pl.when(inside[7 - i])(copy.wait_recv)
    apodize(0)
    half = halved(1 - p, 0)
    for chunk in range(2):
        for i, part in enumerate(numerator(half, 0, chunk, 0)):
            num_first[chunk, i] = part
    apodize(1)
    half = halved(1 - p, 1)
    num_pairs = []
    for chunk in range(2):
        for i, part in enumerate(numerator(half, 0, chunk, 1)):
            num_sib_out[chunk, i] = (num_first[chunk, i] + part).astype(BF16)
        num_pairs.append(
            remote(num_sib_out.at[chunk], num_sib_in.at[chunk], sib_send.at[1 + chunk], sib_recv.at[1 + chunk], sib)
        )
    for k, copy in zip(FAR, psf_copies):

        @pl.when((z + k) % CHIPS > z)
        def _():
            pl.semaphore_wait(ready.at[k], 1)
            copy.start()

    half = [halved(p, e) for e in range(2)]
    num_copies = []
    for chunk in range(2):
        parts = [a + b for a, b in zip(*(numerator(half[e], 1, chunk, e) for e in range(2)))]
        num_pairs[chunk].wait_recv()
        for i, part in enumerate(parts):
            part = part + num_sib_in[chunk, i].astype(F32)
            num_own[i, :, SIDE * chunk : SIDE * chunk + SIDE] = part
            num_out[chunk, i] = part[:HALF].astype(BF16)
            ex_out[i, :, SIDE * chunk : SIDE * chunk + SIDE] = part[HALF:].astype(BF16)
        to_others(NUM_ORDER, functools.partial(num_copy, chunk))
        num_copies += [num_copy(chunk, k) for k in FAR]

    def extra(at):
        return pltpu.make_async_remote_copy(
            src_ref=ex_out,
            dst_ref=ex_in.at[at],
            send_sem=ex_send,
            recv_sem=ex_recv.at[at],
            device_id={"exp": 2 * CHIPS - 1},
            device_id_type=MESH,
        )

    @pl.when((p == 1) & (z < CHIPS - 1))
    def _():
        extra(z).start()

    for copy in psf_copies:
        copy.wait_recv()
    start = pl.multiple_of(BLK * z, BLK)
    pgz = jnp.concatenate(
        [
            pgt[p, pl.ds(start, BLK), :],
            pgt[p, HALF:ROWS, :],
            pgt[p, pl.ds(pl.multiple_of(start + ROWS, BLK), BLK), :],
            pgt[p, ROWS + HALF :, :],
        ],
        axis=0,
    )
    lane_d = lax.broadcasted_iota(jnp.int32, (4 * BLK, 128), 1) // PS

    def add_den(g, den):
        lift = dot(pgz, psf_all[g, 0:PS, :])
        weights = jnp.sum(psf_all[g, PS : PS + BLK, :].astype(F32), axis=0, keepdims=True)
        ones = [jnp.where(lane_d == t, lift, 0.0).astype(BF16) for t in range(4)]
        lhs = jnp.concatenate(
            [jnp.concatenate([one[: 2 * BLK], one[2 * BLK :]], axis=1) for one in ones], axis=0
        )
        otf = dot(lhs, pgw[...])
        power = otf[:, :TILE] * otf[:, :TILE] + otf[:, TILE:] * otf[:, TILE:]
        for t in range(4):
            den = den + weights[:, PS * t : PS * t + 1] * power[2 * BLK * t : 2 * BLK * (t + 1)]
        return den

    den = lax.fori_loop(0, CHIPS, add_den, jnp.zeros((2 * BLK, TILE), F32))

    ex_sum[...] = jnp.zeros_like(ex_sum)

    @pl.when(group == 2 * CHIPS - 1)
    def _():
        for t in range(CHIPS - 1):
            extra(t).wait_recv()
        total = num_own[:, HALF:ROWS, :]
        for t in range(CHIPS - 1):
            total = total + ex_in[t].astype(F32)
        ex_sum[...] = total

    sums = num_own[:, pl.ds(start, BLK), :]
    for i in reversed(range(len(FAR))):
        num_copies[i].wait_recv()
        num_copies[len(FAR) + i].wait_recv()
        k = FAR[i]
        sums = sums + jnp.concatenate([num_in[0, k], num_in[1, k]], axis=2).astype(F32)
    norm = lax.rsqrt(den + 1.0)
    s_re = jnp.concatenate([sums[0], ex_sum[0]], axis=0) * norm
    s_im = jnp.concatenate([sums[1], ex_sum[1]], axis=0) * norm
    loads[15].wait()
    loads[16].wait()
    lane0 = lax.broadcasted_iota(jnp.int32, (2 * BLK, SIDE), 1) == 0
    (re_p, re_m), (im_p, im_m) = (
        [jnp.concatenate([x[:, at : at + LANES], x[:, SIDE + at : SIDE + at + LANES]], axis=1) for at in (0, LANES)]
        for x in (s_re, s_im)
    )
    top_rows = [jnp.where(lane0, re_p, re_p + re_m), jnp.where(lane0, re_m, im_m - im_p)]
    low_rows = [jnp.where(lane0, im_p, im_p + im_m), jnp.where(lane0, im_m, re_p - re_m)]
    folded = jnp.concatenate([jnp.concatenate(top_rows, axis=1), jnp.concatenate(low_rows, axis=1)], axis=0)
    t_own[...] = dot(folded.astype(BF16), ytab[...]).astype(BF16)
    t_pair = remote(t_own, t_sib, sib_send.at[3], sib_recv.at[3], sib)
    image = dot(xtab[0], t_own[...])
    t_pair.wait_recv()
    image = image + dot(xtab[1], t_sib[...])
    for t in range(CHIPS):
        block = image[OUT * t : OUT * (t + 1)]
        part_out[t] = jnp.concatenate(
            [block[:, 128 * i : 128 * i + 128] for i in range(3)] + [jnp.zeros((PACK - 3 * OUT, 128), F32)], axis=0
        ).astype(BF16)
    def part_copy(k):
        return describe(
            part_out.at[(z + k) % CHIPS], out.at[k], part_send.at[k], part_recv.at[k], {"exp": along(k)}
        )

    to_others(PART_ORDER, part_copy)
    parts = [part_copy(k) for k in FAR]
    mine = pltpu.make_async_copy(part_out.at[z], out.at[0], load_sem.at[0])
    mine.start()
    mine.wait()
    for copy in parts:
        copy.wait_recv()
    for i, copy in halos:
        pl.when(inside[i])(copy.wait_send)
    for copy in psf_copies + num_pairs + [psf_pair, t_pair] + num_copies + parts:
        copy.wait_send()

    @pl.when((p == 1) & (z < CHIPS - 1))
    def _():
        extra(z).wait_send()


def finish(parts, out):
    total = jnp.sum(parts[...].astype(F32), axis=0)
    for i in range(3):
        out[0, :, LANES * i : LANES * (i + 1)] = total[OUT * i : OUT * (i + 1)]


def body(stamps, footprint, psf_anchor, psf_degree, psf_powers, psf_basis, flux, variance):
    ftab, wtab, pgt, pgw, ytab, xtab, taper = (jnp.asarray(t) for t in tables())
    vmem = pl.BlockSpec(memory_space=pltpu.VMEM)
    hbm = pl.BlockSpec(memory_space=pl.ANY)
    dma = pltpu.SemaphoreType.DMA
    parts = pl.pallas_call(
        kernel,
        out_shape=pltpu.VMEM((CHIPS, PACK, 128), BF16),
        in_specs=[hbm] * 15,
        out_specs=hbm,
        scratch_shapes=[
            pltpu.SMEM((2, 4), jnp.int32),
            pltpu.SMEM((2, 2), jnp.int32),
            pltpu.SMEM((2,), jnp.int32),
            pltpu.SMEM((2, 2, NBASIS), jnp.int32),
            pltpu.SMEM((2,), F32),
            pltpu.SMEM((2,), F32),
            pltpu.VMEM((NBASIS, 2, PS * PS), F32),
            pltpu.VMEM(pgt.shape, BF16),
            pltpu.VMEM(taper.shape, F32),
            pltpu.VMEM((2, 2, CORE, 128), BF16),
            pltpu.VMEM((2, 2, ROWS, 2 * TILE), F32),
            pltpu.VMEM((2, 2, ROWS, SIDE), F32),
            pltpu.VMEM((2, 2 * HALO, CORE), BF16),
            pltpu.VMEM((2, 2, CORE // 2, 128), BF16),
            pltpu.VMEM((2, 2, CORE // 2, 128), BF16),
            pltpu.VMEM((2, 2, HALO, 128), BF16),
            pltpu.VMEM((2, 2, HALO, 128), BF16),
            pltpu.VMEM((2, TILE, TILE), BF16),
            pltpu.VMEM(ftab.shape, BF16),
            pltpu.VMEM(wtab.shape, BF16),
            pltpu.VMEM(pgw.shape, BF16),
            pltpu.VMEM(ytab.shape, BF16),
            pltpu.VMEM(xtab.shape[1:], BF16),
            pltpu.VMEM((PS + BLK, 128), BF16),
            pltpu.VMEM((PS + BLK, 128), BF16),
            pltpu.VMEM((CHIPS, PS + BLK, 128), BF16),
            pltpu.VMEM((2, 2, ROWS, SIDE), BF16),
            pltpu.VMEM((2, 2, ROWS, SIDE), BF16),
            pltpu.VMEM((2, ROWS, TILE), F32),
            pltpu.VMEM((2, 2, HALF, SIDE), BF16),
            pltpu.VMEM((2, CHIPS, 2, BLK, SIDE), BF16),
            pltpu.VMEM((2, BLK, TILE), BF16),
            pltpu.VMEM((CHIPS - 1, 2, BLK, TILE), BF16),
            pltpu.VMEM((2, BLK, TILE), F32),
            pltpu.VMEM((4 * BLK, CORE), BF16),
            pltpu.VMEM((4 * BLK, CORE), BF16),
            pltpu.VMEM((CHIPS, PACK, 128), BF16),
            dma((17,)),
            dma((12,)),
            dma((12,)),
            dma((4,)),
            dma((4,)),
            dma((CHIPS,)),
            dma((CHIPS,)),
            dma((2, CHIPS)),
            dma((2, CHIPS)),
            dma,
            dma((CHIPS - 1,)),
            dma((CHIPS,)),
            dma((CHIPS,)),
            pltpu.SemaphoreType.REGULAR((CHIPS,)),
        ],
        compiler_params=pltpu.CompilerParams(
            collective_id=0, has_side_effects=True, vmem_limit_bytes=64 * 1024 * 1024 - 512 * 1024
        ),
    )(
        footprint, psf_anchor, psf_degree, psf_powers.transpose(0, 2, 1), flux, variance,
        psf_basis.transpose(1, 0, 2), pgt, taper,
        stamps, ftab, wtab, pgw, ytab, xtab,
    )
    parts = pltpu.with_memory_space_constraint(parts, pltpu.VMEM)
    return pl.pallas_call(
        finish, out_shape=jax.ShapeDtypeStruct((1, OUT, CORE), F32), in_specs=[vmem], out_specs=vmem
    )(parts)


def solution(mesh):
    in_specs = (
        P("exp", "trow", "tcol"),
        P("exp", None),
        P("exp", None),
        P("exp"),
        P("exp", None, None),
        P("exp", None, None),
        P("exp"),
        P("exp"),
    )
    out_specs = P("trow", "exp", "tcol")
    return jax.shard_map(body, mesh=mesh, in_specs=in_specs, out_specs=out_specs, check_vma=False)
```

```python
import functools
import math

import jax
import jax.numpy as jnp
import ml_dtypes
import numpy as np
from jax import lax
from jax.experimental import pallas as pl
from jax.experimental.pallas import tpu as pltpu
from jax.sharding import PartitionSpec as P

TILE = 512
HALO = 64
PS = 32
NBASIS = 10
CORE = 384
CHIPS = 8
SIDE = TILE // 2
LANES = 128
FAR = (4, 3, 5, 2, 6, 1, 7)
NUM_ORDER = (3, 2, 1, 4, 0, 5, 6, 7)
PART_ORDER = (0, 1, 2, 3, 4, 5, 6, 7)
BLK = 16
HALF = CHIPS * BLK
ROWS = HALF + BLK
OUT = CORE // (2 * CHIPS)
PACK = 80
MESH = pl.DeviceIdType.MESH
F32 = jnp.float32
BF16 = jnp.bfloat16


def angles(a, b):
    return (a[:, None] * b[None, :] % TILE) * (2.0 * math.pi / TILE)


@functools.cache
def tables():
    freq = np.arange(TILE)
    pixel = (freq + HALO) % TILE
    offset = np.arange(PS) - PS // 2
    scale = 1.0 / math.sqrt(TILE)

    def bf(x):
        return np.asarray(x, np.float32).astype(ml_dtypes.bfloat16)

    rows = [np.arange(HALF * q, HALF * q + ROWS) for q in range(2)]
    live = [(u <= TILE // 2)[:, None] for u in rows]
    ftab = np.stack(
        [
            np.concatenate([np.cos(angles(u, pixel)) * k, -np.sin(angles(u, pixel)) * k]) * scale
            for u, k in zip(rows, live)
        ]
    )
    cos, sin = np.cos(angles(pixel, freq[:SIDE])), -np.sin(angles(pixel, freq[:SIDE]))
    sin[:, 0] = np.cos(angles(pixel, freq[SIDE : SIDE + 1]))[:, 0]
    wtab = np.concatenate([cos[:, :LANES], sin[:, :LANES], cos[:, LANES:], sin[:, LANES:]], 1) * scale
    pgt = np.stack(
        [np.concatenate([np.cos(angles(u, offset)) * k, -np.sin(angles(u, offset)) * k]) for u, k in zip(rows, live)]
    )
    minus = np.concatenate([freq[SIDE : SIDE + 1], freq[:SIDE:-1]])
    order = np.concatenate([freq[:LANES], minus[:LANES], freq[LANES:SIDE], minus[LANES:]])
    cos, sin = np.cos(angles(offset, order)), np.sin(angles(offset, order))
    cos, sin = np.tile(cos, (4, 1)), np.tile(sin, (4, 1))
    pgw = np.block([[cos, -sin], [sin, cos]])
    core = np.arange(CORE) + HALO
    cos, sin = np.cos(angles(freq[:SIDE], core)), np.sin(angles(freq[:SIDE], core))
    sin[0] = np.cos(angles(freq[SIDE : SIDE + 1], core))[0]
    ytab = np.concatenate([cos[:LANES], sin[:LANES], cos[LANES:], sin[LANES:]]) * scale
    xtab = np.zeros((2 * CHIPS, 2, CHIPS * OUT, 4 * BLK))
    for z in range(CHIPS):
        for p in range(2):
            x = np.concatenate([OUT * (2 * t + p) + np.arange(OUT) for t in range(CHIPS)]) + HALO
            for side in range(2):
                q = p ^ side
                u = np.concatenate([q * HALF + BLK * z + np.arange(BLK), TILE // 2 + np.arange(BLK)])
                count = np.where((u == 0) | (u == TILE // 2), 1.0, 2.0)
                count[BLK:] = 0.0
                if z == CHIPS - 1 and q == 1:
                    count[BLK] = 1.0
                xtab[2 * z + p, side, :, : 2 * BLK] = np.cos(angles(x, u)) * scale * count
                xtab[2 * z + p, side, :, 2 * BLK :] = -np.sin(angles(x, u)) * scale * count
    edge = np.arange(HALO)
    dist = np.concatenate([HALO - 1 - edge, edge])
    line = np.sin(0.5 * math.pi * (dist + 0.5) / HALO) ** 2
    taper = np.stack([np.tile(line[:, None], (1, 128)), np.tile(line[None, :], (128, 1))]).astype(np.float32)
    return bf(ftab), bf(wtab), bf(pgt), bf(pgw), bf(ytab), bf(xtab), taper


def monomial(value, power):
    return jnp.where(
        power == 0,
        1.0,
        jnp.where(power == 1, value, jnp.where(power == 2, value * value, value * value * value)),
    )


def dot(a, b):
    return jnp.dot(a, b, preferred_element_type=F32)


def kernel(
    foot_h, anchor_h, degree_h, powers_h, flux_h, variance_h, basis_h, pgt_h, taper_h, stamps, ftab_h, wtab_h, pgw_h,
    ytab_h, xtab_h,
    out,
    foot, anchor, degree, powers, flux, variance, basis, pgt, taper, strip, otf_all, num_first, rowh, cols, cols_in, corners,
    corners_in, ap, ftab, wtab, pgw, ytab, xtab,
    psf_own, psf_sib, psf_all, num_sib_out, num_sib_in, num_own, num_out, num_in, ex_out, ex_in, ex_sum,
    t_own, t_sib, part_out,
    load_sem, halo_send, halo_recv, sib_send, sib_recv, psf_send, psf_recv, num_send, num_recv,
    ex_send, ex_recv, part_send, part_recv, ready,
):
    group = lax.axis_index("exp")
    r = lax.axis_index("trow")
    c = lax.axis_index("tcol")
    z = group // 2
    p = group % 2
    sib = {"exp": group + 1 - 2 * p}

    def along(k):
        return 2 * ((z + k) % CHIPS) + p

    def near(dr, dc):
        return {"trow": (r + dr + 4) % 4, "tcol": (c + dc + 4) % 4}

    around = [(-1, -1), (-1, 1), (0, -1), (-1, 0), (1, 0), (0, 1), (1, -1), (1, 1)]
    inside = [(r + dr >= 0) & (r + dr < 4) & (c + dc >= 0) & (c + dc < 4) for dr, dc in around]
    barrier = pltpu.get_barrier_semaphore()
    for at, there in zip(around, inside):

        @pl.when(there)
        def _():
            pl.semaphore_signal(barrier, inc=1, device_id=near(*at), device_id_type=MESH)

    for k in FAR:

        @pl.when((z + k) % CHIPS > z)
        def _():
            pl.semaphore_signal(barrier, inc=1, device_id={"exp": along(k)}, device_id_type=MESH)

    pl.semaphore_signal(barrier, inc=1, device_id=sib, device_id_type=MESH)
    loads = []
    for i, (src, dst) in enumerate(
        [
            (stamps.at[:, :, pl.ds(0, 128)], strip.at[0]), (stamps.at[:, :, pl.ds(CORE - 128, 128)], strip.at[1]),
            (foot_h, foot), (anchor_h, anchor), (degree_h, degree), (powers_h, powers),
            (flux_h, flux), (variance_h, variance), (basis_h, basis), (pgt_h, pgt), (pgw_h, pgw),
            (stamps, ap.at[:, pl.ds(0, CORE), pl.ds(0, CORE)]), (taper_h, taper), (ftab_h, ftab), (wtab_h, wtab),
            (ytab_h, ytab), (xtab_h.at[group], xtab),
        ]
    ):
        load = pltpu.make_async_copy(src, dst, load_sem.at[i])
        load.start()
        loads.append(load)

    def describe(src, dst, send, recv, where):
        return pltpu.make_async_remote_copy(
            src_ref=src, dst_ref=dst, send_sem=send, recv_sem=recv, device_id=where, device_id_type=MESH
        )

    def remote(*args):
        copy = describe(*args)
        copy.start()
        return copy

    def to_others(chips, copy):
        for chip in chips:
            pl.when(z != chip)(lambda chip=chip: copy((chip - z + CHIPS) % CHIPS).start())

    loads[0].wait()
    loads[1].wait()
    low = lax.broadcasted_iota(jnp.int32, (CORE // 2, 128), 1) < HALO
    turned = [[pltpu.roll(strip[side, e].astype(F32), HALO, 1) for e in range(2)] for side in range(2)]
    for e in range(2):
        cols[0, e] = jnp.where(low, strip[0, e, : CORE // 2].astype(F32), turned[0][e][CORE // 2 :]).astype(BF16)
        cols[1, e] = jnp.where(low, turned[1][e][: CORE // 2], strip[1, e, CORE // 2 :].astype(F32)).astype(BF16)
    for i, rows in enumerate((slice(0, HALO), slice(CORE - HALO, CORE))):
        corners[i, 0] = jnp.where(low[:HALO], strip[0, 0, rows].astype(F32), turned[0][1][rows]).astype(BF16)
        corners[i, 1] = jnp.where(low[:HALO], turned[1][0][rows], strip[1, 1, rows].astype(F32)).astype(BF16)
    pl.semaphore_wait(barrier, sum(there.astype(jnp.int32) for there in inside) + 1 + z)
    pieces = [
        (0, corners.at[0, 0], corners_in.at[0, 0]),
        (1, corners.at[0, 1], corners_in.at[0, 1]),
        (6, corners.at[1, 0], corners_in.at[1, 0]),
        (7, corners.at[1, 1], corners_in.at[1, 1]),
    ]
    for e in range(2):
        pieces += [
            (2, cols.at[0, e], cols_in.at[0, e]),
            (5, cols.at[1, e], cols_in.at[1, e]),
            (3, stamps.at[e, pl.ds(0, HALO), :], rowh.at[e, pl.ds(0, HALO), :]),
            (4, stamps.at[e, pl.ds(CORE - HALO, HALO), :], rowh.at[e, pl.ds(HALO, HALO), :]),
        ]
    halos = [
        (i, describe(src, dst, halo_send.at[n], halo_recv.at[n], near(*around[i])))
        for n, (i, src, dst) in enumerate(pieces)
    ]
    for i, copy in halos:
        pl.when(inside[i])(copy.start)
    for k in FAR:

        @pl.when((z + k) % CHIPS < z)
        def _():
            pl.semaphore_signal(ready.at[CHIPS - k], inc=1, device_id={"exp": along(k)}, device_id_type=MESH)

    for i, _, dst in pieces:

        @pl.when(jnp.logical_not(inside[7 - i]))
        def _():
            dst[...] = jnp.zeros(dst.shape, BF16)

    for load in loads[2:9]:
        load.wait()

    lane32 = lax.broadcasted_iota(jnp.int32, (PS, 128), 1)
    row32 = lax.broadcasted_iota(jnp.int32, (PS, 128), 0)
    slot32 = lane32 // PS
    fold = jnp.where(
        lax.broadcasted_iota(jnp.int32, (128, 128), 0) % PS == lax.broadcasted_iota(jnp.int32, (128, 128), 1) % PS,
        1.0,
        0.0,
    ).astype(BF16)
    lane16 = lax.broadcasted_iota(jnp.int32, (BLK, 128), 1) // PS
    row16 = lax.broadcasted_iota(jnp.int32, (BLK, 128), 0)
    psf = jnp.zeros((PS, 128), F32)
    wrow = jnp.zeros((BLK, 128), F32)
    wnum = []
    for e in range(2):
        ux = (c * CORE + CORE // 2 - anchor[e, 1]).astype(F32) / (2.0 * CORE)
        uy = (r * CORE + CORE // 2 - anchor[e, 0]).astype(F32) / (2.0 * CORE)
        flat = jnp.zeros((1, PS * PS), F32)
        for k in range(NBASIS):
            px, qy = powers[e, 0, k], powers[e, 1, k]
            term = jnp.where(px + qy <= degree[e], monomial(ux, px) * monomial(uy, qy), 0.0)
            flat = flat + term * basis[k, e : e + 1, :]
        spread = jnp.zeros((PS, 128), F32)
        for t in range(PS * PS // 128):
            spread = jnp.where(
                (row32 // 4 == t) & (slot32 == row32 % 4),
                jnp.broadcast_to(flat[:, 128 * t : 128 * t + 128], (PS, 128)),
                spread,
            )
        mine = 2 * p + e
        psf = jnp.where(slot32 == mine, dot(spread.astype(BF16), fold), psf)
        active = (foot[e, 0] <= r) & (r < foot[e, 1]) & (foot[e, 2] <= c) & (c < foot[e, 3])
        gain = jnp.where(active, flux[e], 0.0)
        wnum.append(jnp.full((8, 128), gain, F32) / jnp.full((8, 128), variance[e], F32))
        wden = jnp.full((BLK, 128), gain * flux[e], F32) / jnp.full((BLK, 128), variance[e], F32)
        wrow = jnp.where(lane16 == mine, wden, wrow)
    high = wrow.astype(BF16).astype(F32)
    rest = wrow - high
    mid = rest.astype(BF16).astype(F32)
    wrow = jnp.where(row16 == 0, high, jnp.where(row16 == 1, mid, jnp.where(row16 == 2, rest - mid, 0.0)))
    psf_own[0:PS, :] = psf.astype(BF16)
    psf_own[PS : PS + BLK, :] = wrow.astype(BF16)
    psf_pair = remote(psf_own, psf_sib, sib_send.at[0], sib_recv.at[0], sib)


    loads[9].wait()
    loads[10].wait()
    stamp = psf_own[0:PS, :]
    lane_r = lax.broadcasted_iota(jnp.int32, (2 * ROWS, 128), 1) // PS
    for side in range(2):
        lift = dot(pgt[1 - p if side == 0 else p], stamp)
        for e in range(2):
            one = jnp.where(lane_r == 2 * p + e, lift, 0.0).astype(BF16)
            otf_all[side, e] = dot(jnp.concatenate([one[:ROWS], one[ROWS:]], axis=1), pgw[...])

    for load in loads[11:15]:
        load.wait()
    lane_s = lax.broadcasted_iota(jnp.int32, (CORE, 128), 1) < HALO
    line_r = taper[0]
    line_c = taper[1]
    wide = jnp.concatenate([line_r] * 3, axis=1)

    def apodize(e):
        for i, copy in halos[4 + 4 * e : 8 + 4 * e]:
            pl.when(inside[7 - i])(copy.wait_recv)
        up, down, after, before = [
            jnp.where((foot[e, lo] <= at) & (at < foot[e, lo + 1]), 1.0, 0.0)
            for lo, at in ((0, r + 1), (0, r - 1), (2, c + 1), (2, c - 1))
        ]
        ap[e, CORE : CORE + HALO, 0:CORE] = (rowh[e, 0:HALO, :].astype(F32) * (wide[0:HALO] * up)).astype(BF16)
        ap[e, CORE + HALO : TILE, 0:CORE] = (rowh[e, HALO:, :].astype(F32) * (wide[HALO:] * down)).astype(BF16)
        right, left = cols_in[0, e].astype(F32), cols_in[1, e].astype(F32)
        side = jnp.concatenate(
            [jnp.where(low, right, pltpu.roll(left, HALO, 1)), jnp.where(low, pltpu.roll(right, HALO, 1), left)], axis=0
        )
        keep = jnp.where(lane_s, after, before)
        ap[e, 0:CORE, CORE:TILE] = (side * (jnp.concatenate([line_c] * 3, axis=0) * keep)).astype(BF16)
        for i, rows in enumerate((slice(0, HALO), slice(HALO, 2 * HALO))):
            right, left = corners_in[i, 0].astype(F32), corners_in[i, 1].astype(F32)
            if e == 0:
                corner = jnp.where(low[:HALO], right, pltpu.roll(left, HALO, 1))
            else:
                corner = jnp.where(low[:HALO], pltpu.roll(right, HALO, 1), left)
            taper2 = line_r[rows] * line_c[rows] * keep[:HALO] * (up if i == 0 else down)
            ap[e, CORE + HALO * i : CORE + HALO * (i + 1), CORE:TILE] = (corner * taper2).astype(BF16)

    lane0 = lax.broadcasted_iota(jnp.int32, (ROWS, LANES), 1) == 0

    def halved(q, e):
        return dot(ftab[q], ap[e]).astype(BF16)

    def numerator(half, side, chunk, e):
        cols = slice(SIDE * chunk, SIDE * chunk + SIDE)
        prod = dot(half, wtab[:, cols])
        re_cos, re_sin = prod[:ROWS, :LANES], prod[:ROWS, LANES:]
        im_cos, im_sin = prod[ROWS:, :LANES], prod[ROWS:, LANES:]
        if chunk == 0:
            plus = [re_cos - jnp.where(lane0, 0.0, im_sin), im_cos + jnp.where(lane0, 0.0, re_sin)]
            minus = [jnp.where(lane0, re_sin, re_cos + im_sin), jnp.where(lane0, im_sin, im_cos - re_sin)]
        else:
            plus = [re_cos - im_sin, im_cos + re_sin]
            minus = [re_cos + im_sin, im_cos - re_sin]
        spec_re, spec_im = (jnp.concatenate(pair, axis=1) for pair in zip(plus, minus))
        otf_re = otf_all[side, e, :, cols]
        otf_im = otf_all[side, e, :, TILE + SIDE * chunk : TILE + SIDE * chunk + SIDE]
        w = wnum[e][0:1, 0:1]
        return w * (otf_re * spec_re + otf_im * spec_im), w * (otf_re * spec_im - otf_im * spec_re)

    def num_copy(chunk, k):
        return describe(
            num_out.at[chunk, :, pl.ds(pl.multiple_of(BLK * ((z + k) % CHIPS), BLK), BLK), :],
            num_in.at[chunk, k],
            num_send.at[chunk, k],
            num_recv.at[chunk, k],
            {"exp": along(k)},
        )

    psf_pair.wait_recv()
    psf_all[0] = (psf_own[...].astype(F32) + psf_sib[...].astype(F32)).astype(BF16)
    psf_copies = [
        describe(psf_all.at[0], psf_all.at[k], psf_send.at[k], psf_recv.at[k], {"exp": along(k)}) for k in FAR
    ]
    for k, copy in zip(FAR, psf_copies):
        pl.when((z + k) % CHIPS < z)(copy.start)
    for i, copy in halos[:4]:
        pl.when(inside[7 - i])(copy.wait_recv)
    apodize(0)
    half = halved(1 - p, 0)
    for chunk in range(2):
        for i, part in enumerate(numerator(half, 0, chunk, 0)):
            num_first[chunk, i] = part
    apodize(1)
    half = halved(1 - p, 1)
    num_pairs = []
    for chunk in range(2):
        for i, part in enumerate(numerator(half, 0, chunk, 1)):
            num_sib_out[chunk, i] = (num_first[chunk, i] + part).astype(BF16)
        num_pairs.append(
            remote(num_sib_out.at[chunk], num_sib_in.at[chunk], sib_send.at[1 + chunk], sib_recv.at[1 + chunk], sib)
        )
    for k, copy in zip(FAR, psf_copies):

        @pl.when((z + k) % CHIPS > z)
        def _():
            pl.semaphore_wait(ready.at[k], 1)
            copy.start()

    half = [halved(p, e) for e in range(2)]
    num_copies = []
    row8 = lax.broadcasted_iota(jnp.int32, (8, LANES), 0)
    nyquist = jnp.zeros((8, LANES), F32)
    for chunk in range(2):
        parts = [a + b for a, b in zip(*(numerator(half[e], 1, chunk, e) for e in range(2)))]
        num_pairs[chunk].wait_recv()
        for i, part in enumerate(parts):
            part = part + num_sib_in[chunk, i].astype(F32)
            num_own[i, :, SIDE * chunk : SIDE * chunk + SIDE] = part
            num_out[chunk, i] = part[:HALF].astype(BF16)
            for j in range(2):
                nyquist = jnp.where(
                    row8 == 4 * i + 2 * chunk + j,
                    jnp.broadcast_to(part[HALF : HALF + 1, LANES * j : LANES * (j + 1)], row8.shape),
                    nyquist,
                )
        to_others(NUM_ORDER, functools.partial(num_copy, chunk))
        num_copies += [num_copy(chunk, k) for k in FAR]

    def extra(at):
        return pltpu.make_async_remote_copy(
            src_ref=ex_out,
            dst_ref=ex_in.at[at],
            send_sem=ex_send,
            recv_sem=ex_recv.at[at],
            device_id={"exp": 2 * CHIPS - 1},
            device_id_type=MESH,
        )

    ex_out[...] = jnp.concatenate([nyquist, jnp.zeros_like(nyquist)], axis=0).astype(BF16)

    @pl.when((p == 1) & (z < CHIPS - 1))
    def _():
        extra(z).start()

    for copy in psf_copies:
        copy.wait_recv()
    start = pl.multiple_of(BLK * z, BLK)
    pgz = jnp.concatenate(
        [
            pgt[p, pl.ds(start, BLK), :],
            pgt[p, HALF:ROWS, :],
            pgt[p, pl.ds(pl.multiple_of(start + ROWS, BLK), BLK), :],
            pgt[p, ROWS + HALF :, :],
        ],
        axis=0,
    )
    lane_d = lax.broadcasted_iota(jnp.int32, (4 * BLK, 128), 1) // PS

    def add_den(g, den):
        lift = dot(pgz, psf_all[g, 0:PS, :])
        weights = jnp.sum(psf_all[g, PS : PS + BLK, :].astype(F32), axis=0, keepdims=True)
        ones = [jnp.where(lane_d == t, lift, 0.0).astype(BF16) for t in range(4)]
        lhs = jnp.concatenate(
            [jnp.concatenate([one[: 2 * BLK], one[2 * BLK :]], axis=1) for one in ones], axis=0
        )
        otf = dot(lhs, pgw[...])
        power = otf[:, :TILE] * otf[:, :TILE] + otf[:, TILE:] * otf[:, TILE:]
        for t in range(4):
            den = den + weights[:, PS * t : PS * t + 1] * power[2 * BLK * t : 2 * BLK * (t + 1)]
        return den

    den = lax.fori_loop(0, CHIPS, add_den, jnp.zeros((2 * BLK, TILE), F32))

    ex_sum[...] = jnp.zeros_like(ex_sum)

    @pl.when(group == 2 * CHIPS - 1)
    def _():
        for t in range(CHIPS - 1):
            extra(t).wait_recv()
        total = nyquist
        for t in range(CHIPS - 1):
            total = total + ex_in[t].astype(F32)[:8]
        for i in range(8):
            ex_sum[i // 4, 0:1, LANES * (i % 4) : LANES * (i % 4 + 1)] = total[i : i + 1]

    norm = lax.rsqrt(den + 1.0)
    loads[15].wait()
    loads[16].wait()
    lane0 = lax.broadcasted_iota(jnp.int32, (2 * BLK, LANES), 1) == 0
    t_all = None
    for chunk in range(2):
        cols = slice(SIDE * chunk, SIDE * chunk + SIDE)
        sums = num_own[:, pl.ds(start, BLK), cols]
        for k, copy in zip(FAR, num_copies[len(FAR) * chunk :]):
            copy.wait_recv()
            sums = sums + num_in[chunk, k].astype(F32)
        s_re, s_im = (jnp.concatenate([sums[i], ex_sum[i, :, cols]], axis=0) * norm[:, cols] for i in range(2))
        (re_p, re_m), (im_p, im_m) = ((x[:, :LANES], x[:, LANES:]) for x in (s_re, s_im))
        even, odd = [re_p + re_m, im_p + im_m], [im_m - im_p, re_p - re_m]
        if chunk == 0:
            even = [jnp.where(lane0, a, b) for a, b in zip((re_p, im_p), even)]
            odd = [jnp.where(lane0, a, b) for a, b in zip((re_m, im_m), odd)]
        folded = jnp.concatenate([jnp.concatenate(pair, axis=1) for pair in zip(even, odd)], axis=0)
        part = dot(folded.astype(BF16), ytab[cols, :])
        t_all = part if chunk == 0 else t_all + part
    t_own[...] = t_all.astype(BF16)
    t_pair = remote(t_own, t_sib, sib_send.at[3], sib_recv.at[3], sib)
    image = dot(xtab[0], t_own[...])
    t_pair.wait_recv()
    image = image + dot(xtab[1], t_sib[...])
    for t in range(CHIPS):
        block = image[OUT * t : OUT * (t + 1)]
        part_out[t] = jnp.concatenate(
            [block[:, 128 * i : 128 * i + 128] for i in range(3)] + [jnp.zeros((PACK - 3 * OUT, 128), F32)], axis=0
        ).astype(BF16)
    def part_copy(k):
        return describe(
            part_out.at[(z + k) % CHIPS], out.at[k], part_send.at[k], part_recv.at[k], {"exp": along(k)}
        )

    to_others(PART_ORDER, part_copy)
    parts = [part_copy(k) for k in FAR]
    mine = pltpu.make_async_copy(part_out.at[z], out.at[0], load_sem.at[0])
    mine.start()
    mine.wait()
    for copy in parts:
        copy.wait_recv()
    for i, copy in halos:
        pl.when(inside[i])(copy.wait_send)
    for copy in psf_copies + num_pairs + [psf_pair, t_pair] + num_copies + parts:
        copy.wait_send()

    @pl.when((p == 1) & (z < CHIPS - 1))
    def _():
        extra(z).wait_send()


def finish(parts, out):
    total = jnp.sum(parts[...].astype(F32), axis=0)
    for i in range(3):
        out[0, :, LANES * i : LANES * (i + 1)] = total[OUT * i : OUT * (i + 1)]


def body(stamps, footprint, psf_anchor, psf_degree, psf_powers, psf_basis, flux, variance):
    ftab, wtab, pgt, pgw, ytab, xtab, taper = (jnp.asarray(t) for t in tables())
    vmem = pl.BlockSpec(memory_space=pltpu.VMEM)
    hbm = pl.BlockSpec(memory_space=pl.ANY)
    dma = pltpu.SemaphoreType.DMA
    parts = pl.pallas_call(
        kernel,
        out_shape=pltpu.VMEM((CHIPS, PACK, 128), BF16),
        in_specs=[hbm] * 15,
        out_specs=hbm,
        scratch_shapes=[
            pltpu.SMEM((2, 4), jnp.int32),
            pltpu.SMEM((2, 2), jnp.int32),
            pltpu.SMEM((2,), jnp.int32),
            pltpu.SMEM((2, 2, NBASIS), jnp.int32),
            pltpu.SMEM((2,), F32),
            pltpu.SMEM((2,), F32),
            pltpu.VMEM((NBASIS, 2, PS * PS), F32),
            pltpu.VMEM(pgt.shape, BF16),
            pltpu.VMEM(taper.shape, F32),
            pltpu.VMEM((2, 2, CORE, 128), BF16),
            pltpu.VMEM((2, 2, ROWS, 2 * TILE), F32),
            pltpu.VMEM((2, 2, ROWS, SIDE), F32),
            pltpu.VMEM((2, 2 * HALO, CORE), BF16),
            pltpu.VMEM((2, 2, CORE // 2, 128), BF16),
            pltpu.VMEM((2, 2, CORE // 2, 128), BF16),
            pltpu.VMEM((2, 2, HALO, 128), BF16),
            pltpu.VMEM((2, 2, HALO, 128), BF16),
            pltpu.VMEM((2, TILE, TILE), BF16),
            pltpu.VMEM(ftab.shape, BF16),
            pltpu.VMEM(wtab.shape, BF16),
            pltpu.VMEM(pgw.shape, BF16),
            pltpu.VMEM(ytab.shape, BF16),
            pltpu.VMEM(xtab.shape[1:], BF16),
            pltpu.VMEM((PS + BLK, 128), BF16),
            pltpu.VMEM((PS + BLK, 128), BF16),
            pltpu.VMEM((CHIPS, PS + BLK, 128), BF16),
            pltpu.VMEM((2, 2, ROWS, SIDE), BF16),
            pltpu.VMEM((2, 2, ROWS, SIDE), BF16),
            pltpu.VMEM((2, ROWS, TILE), F32),
            pltpu.VMEM((2, 2, HALF, SIDE), BF16),
            pltpu.VMEM((2, CHIPS, 2, BLK, SIDE), BF16),
            pltpu.VMEM((BLK, LANES), BF16),
            pltpu.VMEM((CHIPS - 1, BLK, LANES), BF16),
            pltpu.VMEM((2, BLK, TILE), F32),
            pltpu.VMEM((4 * BLK, CORE), BF16),
            pltpu.VMEM((4 * BLK, CORE), BF16),
            pltpu.VMEM((CHIPS, PACK, 128), BF16),
            dma((17,)),
            dma((12,)),
            dma((12,)),
            dma((4,)),
            dma((4,)),
            dma((CHIPS,)),
            dma((CHIPS,)),
            dma((2, CHIPS)),
            dma((2, CHIPS)),
            dma,
            dma((CHIPS - 1,)),
            dma((CHIPS,)),
            dma((CHIPS,)),
            pltpu.SemaphoreType.REGULAR((CHIPS,)),
        ],
        compiler_params=pltpu.CompilerParams(
            collective_id=0, has_side_effects=True, vmem_limit_bytes=64 * 1024 * 1024 - 512 * 1024
        ),
    )(
        footprint, psf_anchor, psf_degree, psf_powers.transpose(0, 2, 1), flux, variance,
        psf_basis.transpose(1, 0, 2), pgt, taper,
        stamps, ftab, wtab, pgw, ytab, xtab,
    )
    parts = pltpu.with_memory_space_constraint(parts, pltpu.VMEM)
    return pl.pallas_call(
        finish, out_shape=jax.ShapeDtypeStruct((1, OUT, CORE), F32), in_specs=[vmem], out_specs=vmem
    )(parts)


def solution(mesh):
    in_specs = (
        P("exp", "trow", "tcol"),
        P("exp", None),
        P("exp", None),
        P("exp"),
        P("exp", None, None),
        P("exp", None, None),
        P("exp"),
        P("exp"),
    )
    out_specs = P("trow", "exp", "tcol")
    return jax.shard_map(body, mesh=mesh, in_specs=in_specs, out_specs=out_specs, check_vma=False)
```

```python
import functools
import math

import jax
import jax.numpy as jnp
import ml_dtypes
import numpy as np
from jax import lax
from jax.experimental import pallas as pl
from jax.experimental.pallas import tpu as pltpu
from jax.sharding import PartitionSpec as P

TILE = 512
HALO = 64
PS = 32
NBASIS = 10
CORE = 384
CHIPS = 8
SIDE = TILE // 2
LANES = 128
FAR = (4, 3, 5, 2, 6, 1, 7)
NUM_ORDER = (3, 2, 1, 4, 0, 5, 6, 7)
PART_ORDER = (0, 1, 2, 3, 4, 5, 6, 7)
BLK = 16
HALF = CHIPS * BLK
ROWS = HALF + BLK
OUT = CORE // (2 * CHIPS)
PACK = 80
MESH = pl.DeviceIdType.MESH
F32 = jnp.float32
BF16 = jnp.bfloat16


def angles(a, b):
    return (a[:, None] * b[None, :] % TILE) * (2.0 * math.pi / TILE)


@functools.cache
def tables():
    freq = np.arange(TILE)
    pixel = (freq + HALO) % TILE
    offset = np.arange(PS) - PS // 2
    scale = 1.0 / math.sqrt(TILE)

    def bf(x):
        return np.asarray(x, np.float32).astype(ml_dtypes.bfloat16)

    rows = [np.arange(HALF * q, HALF * q + ROWS) for q in range(2)]
    live = [(u <= TILE // 2)[:, None] for u in rows]
    ftab = np.stack(
        [
            np.concatenate([np.cos(angles(u, pixel)) * k, -np.sin(angles(u, pixel)) * k]) * scale
            for u, k in zip(rows, live)
        ]
    )
    cos, sin = np.cos(angles(pixel, freq[:SIDE])), -np.sin(angles(pixel, freq[:SIDE]))
    sin[:, 0] = np.cos(angles(pixel, freq[SIDE : SIDE + 1]))[:, 0]
    wtab = np.concatenate([cos[:, :LANES], sin[:, :LANES], cos[:, LANES:], sin[:, LANES:]], 1) * scale
    pgt = np.stack(
        [np.concatenate([np.cos(angles(u, offset)) * k, -np.sin(angles(u, offset)) * k]) for u, k in zip(rows, live)]
    )
    minus = np.concatenate([freq[SIDE : SIDE + 1], freq[:SIDE:-1]])
    order = np.concatenate([freq[:LANES], minus[:LANES], freq[LANES:SIDE], minus[LANES:]])
    cos, sin = np.cos(angles(offset, order)), np.sin(angles(offset, order))
    cos, sin = np.tile(cos, (4, 1)), np.tile(sin, (4, 1))
    pgw = np.block([[cos, -sin], [sin, cos]])
    core = np.arange(CORE) + HALO
    cos, sin = np.cos(angles(freq[:SIDE], core)), np.sin(angles(freq[:SIDE], core))
    sin[0] = np.cos(angles(freq[SIDE : SIDE + 1], core))[0]
    ytab = np.concatenate([cos[:LANES], sin[:LANES], cos[LANES:], sin[LANES:]]) * scale
    xtab = np.zeros((2 * CHIPS, 2, CHIPS * OUT, 4 * BLK))
    for z in range(CHIPS):
        for p in range(2):
            x = np.concatenate([OUT * (2 * t + p) + np.arange(OUT) for t in range(CHIPS)]) + HALO
            for side in range(2):
                q = p ^ side
                u = np.concatenate([q * HALF + BLK * z + np.arange(BLK), TILE // 2 + np.arange(BLK)])
                count = np.where((u == 0) | (u == TILE // 2), 1.0, 2.0)
                count[BLK:] = 0.0
                if z == CHIPS - 1 and q == 1:
                    count[BLK] = 1.0
                xtab[2 * z + p, side, :, : 2 * BLK] = np.cos(angles(x, u)) * scale * count
                xtab[2 * z + p, side, :, 2 * BLK :] = -np.sin(angles(x, u)) * scale * count
    edge = np.arange(HALO)
    dist = np.concatenate([HALO - 1 - edge, edge])
    line = np.sin(0.5 * math.pi * (dist + 0.5) / HALO) ** 2
    taper = np.stack([np.tile(line[:, None], (1, 128)), np.tile(line[None, :], (128, 1))]).astype(np.float32)
    return bf(ftab), bf(wtab), bf(pgt), bf(pgw), bf(ytab), bf(xtab), taper


def monomial(value, power):
    return jnp.where(
        power == 0,
        1.0,
        jnp.where(power == 1, value, jnp.where(power == 2, value * value, value * value * value)),
    )


def dot(a, b):
    return jnp.dot(a, b, preferred_element_type=F32)


def kernel(
    foot_h, anchor_h, degree_h, powers_h, flux_h, variance_h, basis_h, pgt_h, taper_h, stamps, ftab_h, wtab_h, pgw_h,
    ytab_h, xtab_h,
    out,
    foot, anchor, degree, powers, flux, variance, basis, pgt, taper, strip, otf_all, num_first, rowh, cols, cols_in, corners,
    corners_in, ap, ftab, wtab, pgw, ytab, xtab,
    psf_own, psf_sib, psf_all, num_sib_out, num_sib_in, num_own, num_out, num_in, ex_out, ex_in, ex_sum,
    t_own, t_sib, part_out,
    load_sem, halo_send, halo_recv, sib_send, sib_recv, psf_send, psf_recv, num_send, num_recv,
    ex_send, ex_recv, part_send, part_recv, ready,
):
    group = lax.axis_index("exp")
    r = lax.axis_index("trow")
    c = lax.axis_index("tcol")
    z = group // 2
    p = group % 2
    sib = {"exp": group + 1 - 2 * p}

    def along(k):
        return 2 * ((z + k) % CHIPS) + p

    def near(dr, dc):
        return {"trow": (r + dr + 4) % 4, "tcol": (c + dc + 4) % 4}

    around = [(-1, -1), (-1, 1), (0, -1), (-1, 0), (1, 0), (0, 1), (1, -1), (1, 1)]
    inside = [(r + dr >= 0) & (r + dr < 4) & (c + dc >= 0) & (c + dc < 4) for dr, dc in around]
    barrier = pltpu.get_barrier_semaphore()
    for at, there in zip(around, inside):

        @pl.when(there)
        def _():
            pl.semaphore_signal(barrier, inc=1, device_id=near(*at), device_id_type=MESH)

    for k in FAR:

        @pl.when((z + k) % CHIPS > z)
        def _():
            pl.semaphore_signal(barrier, inc=1, device_id={"exp": along(k)}, device_id_type=MESH)

    pl.semaphore_signal(barrier, inc=1, device_id=sib, device_id_type=MESH)
    loads = []
    for i, (src, dst) in enumerate(
        [
            (stamps.at[:, :, pl.ds(0, 128)], strip.at[0]), (stamps.at[:, :, pl.ds(CORE - 128, 128)], strip.at[1]),
            (foot_h, foot), (anchor_h, anchor), (degree_h, degree), (powers_h, powers),
            (flux_h, flux), (variance_h, variance), (basis_h, basis), (pgt_h, pgt), (pgw_h, pgw),
            (stamps, ap.at[:, pl.ds(0, CORE), pl.ds(0, CORE)]), (taper_h, taper), (ftab_h, ftab), (wtab_h, wtab),
            (ytab_h, ytab), (xtab_h.at[group], xtab),
        ]
    ):
        load = pltpu.make_async_copy(src, dst, load_sem.at[i])
        load.start()
        loads.append(load)

    def describe(src, dst, send, recv, where):
        return pltpu.make_async_remote_copy(
            src_ref=src, dst_ref=dst, send_sem=send, recv_sem=recv, device_id=where, device_id_type=MESH
        )

    def remote(*args):
        copy = describe(*args)
        copy.start()
        return copy

    def to_others(chips, copy):
        for chip in chips:
            pl.when(z != chip)(lambda chip=chip: copy((chip - z + CHIPS) % CHIPS).start())

    loads[0].wait()
    loads[1].wait()
    low = lax.broadcasted_iota(jnp.int32, (CORE // 2, 128), 1) < HALO
    turned = [[pltpu.roll(strip[side, e].astype(F32), HALO, 1) for e in range(2)] for side in range(2)]
    for e in range(2):
        cols[0, e] = jnp.where(low, strip[0, e, : CORE // 2].astype(F32), turned[0][e][CORE // 2 :]).astype(BF16)
        cols[1, e] = jnp.where(low, turned[1][e][: CORE // 2], strip[1, e, CORE // 2 :].astype(F32)).astype(BF16)
    for i, rows in enumerate((slice(0, HALO), slice(CORE - HALO, CORE))):
        corners[i, 0] = jnp.where(low[:HALO], strip[0, 0, rows].astype(F32), turned[0][1][rows]).astype(BF16)
        corners[i, 1] = jnp.where(low[:HALO], turned[1][0][rows], strip[1, 1, rows].astype(F32)).astype(BF16)
    pl.semaphore_wait(barrier, sum(there.astype(jnp.int32) for there in inside) + 1 + z)
    pieces = [
        (0, corners.at[0, 0], corners_in.at[0, 0]),
        (1, corners.at[0, 1], corners_in.at[0, 1]),
        (6, corners.at[1, 0], corners_in.at[1, 0]),
        (7, corners.at[1, 1], corners_in.at[1, 1]),
    ]
    for e in range(2):
        pieces += [
            (2, cols.at[0, e], cols_in.at[0, e]),
            (5, cols.at[1, e], cols_in.at[1, e]),
            (3, stamps.at[e, pl.ds(0, HALO), :], rowh.at[e, pl.ds(0, HALO), :]),
            (4, stamps.at[e, pl.ds(CORE - HALO, HALO), :], rowh.at[e, pl.ds(HALO, HALO), :]),
        ]
    halos = [
        (i, describe(src, dst, halo_send.at[n], halo_recv.at[n], near(*around[i])))
        for n, (i, src, dst) in enumerate(pieces)
    ]
    for i, copy in halos:
        pl.when(inside[i])(copy.start)
    for k in FAR:

        @pl.when((z + k) % CHIPS < z)
        def _():
            pl.semaphore_signal(ready.at[CHIPS - k], inc=1, device_id={"exp": along(k)}, device_id_type=MESH)

    for i, _, dst in pieces:

        @pl.when(jnp.logical_not(inside[7 - i]))
        def _():
            dst[...] = jnp.zeros(dst.shape, BF16)

    for load in loads[2:9]:
        load.wait()

    lane32 = lax.broadcasted_iota(jnp.int32, (PS, 128), 1)
    row32 = lax.broadcasted_iota(jnp.int32, (PS, 128), 0)
    slot32 = lane32 // PS
    fold = jnp.where(
        lax.broadcasted_iota(jnp.int32, (128, 128), 0) % PS == lax.broadcasted_iota(jnp.int32, (128, 128), 1) % PS,
        1.0,
        0.0,
    ).astype(BF16)
    lane16 = lax.broadcasted_iota(jnp.int32, (BLK, 128), 1) // PS
    row16 = lax.broadcasted_iota(jnp.int32, (BLK, 128), 0)
    psf = jnp.zeros((PS, 128), F32)
    wrow = jnp.zeros((BLK, 128), F32)
    wnum = []
    for e in range(2):
        ux = (c * CORE + CORE // 2 - anchor[e, 1]).astype(F32) / (2.0 * CORE)
        uy = (r * CORE + CORE // 2 - anchor[e, 0]).astype(F32) / (2.0 * CORE)
        flat = jnp.zeros((1, PS * PS), F32)
        for k in range(NBASIS):
            px, qy = powers[e, 0, k], powers[e, 1, k]
            term = jnp.where(px + qy <= degree[e], monomial(ux, px) * monomial(uy, qy), 0.0)
            flat = flat + term * basis[k, e : e + 1, :]
        spread = jnp.zeros((PS, 128), F32)
        for t in range(PS * PS // 128):
            spread = jnp.where(
                (row32 // 4 == t) & (slot32 == row32 % 4),
                jnp.broadcast_to(flat[:, 128 * t : 128 * t + 128], (PS, 128)),
                spread,
            )
        mine = 2 * p + e
        psf = jnp.where(slot32 == mine, dot(spread.astype(BF16), fold), psf)
        active = (foot[e, 0] <= r) & (r < foot[e, 1]) & (foot[e, 2] <= c) & (c < foot[e, 3])
        gain = jnp.where(active, flux[e], 0.0)
        wnum.append(jnp.full((8, 128), gain, F32) / jnp.full((8, 128), variance[e], F32))
        wden = jnp.full((BLK, 128), gain * flux[e], F32) / jnp.full((BLK, 128), variance[e], F32)
        wrow = jnp.where(lane16 == mine, wden, wrow)
    high = wrow.astype(BF16).astype(F32)
    rest = wrow - high
    mid = rest.astype(BF16).astype(F32)
    wrow = jnp.where(row16 == 0, high, jnp.where(row16 == 1, mid, jnp.where(row16 == 2, rest - mid, 0.0)))
    psf_own[0:PS, :] = psf.astype(BF16)
    psf_own[PS : PS + BLK, :] = wrow.astype(BF16)
    psf_pair = remote(psf_own, psf_sib, sib_send.at[0], sib_recv.at[0], sib)


    loads[9].wait()
    loads[10].wait()
    stamp = psf_own[0:PS, :]
    lane_r = lax.broadcasted_iota(jnp.int32, (2 * ROWS, 128), 1) // PS
    for side in range(2):
        lift = dot(pgt[1 - p if side == 0 else p], stamp)
        for e in range(2):
            one = jnp.where(lane_r == 2 * p + e, lift, 0.0).astype(BF16)
            otf_all[side, e] = dot(jnp.concatenate([one[:ROWS], one[ROWS:]], axis=1), pgw[...])

    for load in loads[11:15]:
        load.wait()
    lane_s = lax.broadcasted_iota(jnp.int32, (CORE, 128), 1) < HALO
    line_r = taper[0]
    line_c = taper[1]
    wide = jnp.concatenate([line_r] * 3, axis=1)

    def apodize(e):
        for i, copy in halos[4 + 4 * e : 8 + 4 * e]:
            pl.when(inside[7 - i])(copy.wait_recv)
        up, down, after, before = [
            jnp.where((foot[e, lo] <= at) & (at < foot[e, lo + 1]), 1.0, 0.0)
            for lo, at in ((0, r + 1), (0, r - 1), (2, c + 1), (2, c - 1))
        ]
        ap[e, CORE : CORE + HALO, 0:CORE] = (rowh[e, 0:HALO, :].astype(F32) * (wide[0:HALO] * up)).astype(BF16)
        ap[e, CORE + HALO : TILE, 0:CORE] = (rowh[e, HALO:, :].astype(F32) * (wide[HALO:] * down)).astype(BF16)
        right, left = cols_in[0, e].astype(F32), cols_in[1, e].astype(F32)
        side = jnp.concatenate(
            [jnp.where(low, right, pltpu.roll(left, HALO, 1)), jnp.where(low, pltpu.roll(right, HALO, 1), left)], axis=0
        )
        keep = jnp.where(lane_s, after, before)
        ap[e, 0:CORE, CORE:TILE] = (side * (jnp.concatenate([line_c] * 3, axis=0) * keep)).astype(BF16)
        for i, rows in enumerate((slice(0, HALO), slice(HALO, 2 * HALO))):
            right, left = corners_in[i, 0].astype(F32), corners_in[i, 1].astype(F32)
            if e == 0:
                corner = jnp.where(low[:HALO], right, pltpu.roll(left, HALO, 1))
            else:
                corner = jnp.where(low[:HALO], pltpu.roll(right, HALO, 1), left)
            taper2 = line_r[rows] * line_c[rows] * keep[:HALO] * (up if i == 0 else down)
            ap[e, CORE + HALO * i : CORE + HALO * (i + 1), CORE:TILE] = (corner * taper2).astype(BF16)

    lane0 = lax.broadcasted_iota(jnp.int32, (ROWS, LANES), 1) == 0

    def halved(q, e):
        return dot(ftab[q], ap[e]).astype(BF16)

    def numerator(half, side, chunk, e):
        cols = slice(SIDE * chunk, SIDE * chunk + SIDE)
        prod = dot(half, wtab[:, cols])
        re_cos, re_sin = prod[:ROWS, :LANES], prod[:ROWS, LANES:]
        im_cos, im_sin = prod[ROWS:, :LANES], prod[ROWS:, LANES:]
        if chunk == 0:
            plus = [re_cos - jnp.where(lane0, 0.0, im_sin), im_cos + jnp.where(lane0, 0.0, re_sin)]
            minus = [jnp.where(lane0, re_sin, re_cos + im_sin), jnp.where(lane0, im_sin, im_cos - re_sin)]
        else:
            plus = [re_cos - im_sin, im_cos + re_sin]
            minus = [re_cos + im_sin, im_cos - re_sin]
        spec_re, spec_im = (jnp.concatenate(pair, axis=1) for pair in zip(plus, minus))
        otf_re = otf_all[side, e, :, cols]
        otf_im = otf_all[side, e, :, TILE + SIDE * chunk : TILE + SIDE * chunk + SIDE]
        w = wnum[e][0:1, 0:1]
        return w * (otf_re * spec_re + otf_im * spec_im), w * (otf_re * spec_im - otf_im * spec_re)

    def num_copy(chunk, k):
        return describe(
            num_out.at[chunk, :, pl.ds(pl.multiple_of(BLK * ((z + k) % CHIPS), BLK), BLK), :],
            num_in.at[chunk, k],
            num_send.at[chunk, k],
            num_recv.at[chunk, k],
            {"exp": along(k)},
        )

    psf_pair.wait_recv()
    psf_all[0] = (psf_own[...].astype(F32) + psf_sib[...].astype(F32)).astype(BF16)
    psf_copies = [
        describe(psf_all.at[0], psf_all.at[k], psf_send.at[k], psf_recv.at[k], {"exp": along(k)}) for k in FAR
    ]
    for k, copy in zip(FAR, psf_copies):
        pl.when((z + k) % CHIPS < z)(copy.start)
    for i, copy in halos[:4]:
        pl.when(inside[7 - i])(copy.wait_recv)
    apodize(0)
    half = halved(1 - p, 0)
    for chunk in range(2):
        for i, part in enumerate(numerator(half, 0, chunk, 0)):
            num_first[chunk, i] = part
    apodize(1)
    half = halved(1 - p, 1)
    num_pairs = []
    for chunk in range(2):
        for i, part in enumerate(numerator(half, 0, chunk, 1)):
            num_sib_out[chunk, i] = (num_first[chunk, i] + part).astype(BF16)
        num_pairs.append(
            remote(num_sib_out.at[chunk], num_sib_in.at[chunk], sib_send.at[1 + chunk], sib_recv.at[1 + chunk], sib)
        )
    for k, copy in zip(FAR, psf_copies):

        @pl.when((z + k) % CHIPS > z)
        def _():
            pl.semaphore_wait(ready.at[k], 1)
            copy.start()

    half = [halved(p, e) for e in range(2)]
    num_copies = []
    row8 = lax.broadcasted_iota(jnp.int32, (8, LANES), 0)
    nyquist = jnp.zeros((8, LANES), F32)
    for chunk in range(2):
        parts = [a + b for a, b in zip(*(numerator(half[e], 1, chunk, e) for e in range(2)))]
        num_pairs[chunk].wait_recv()
        for i, part in enumerate(parts):
            part = part + num_sib_in[chunk, i].astype(F32)
            num_own[i, :, SIDE * chunk : SIDE * chunk + SIDE] = part
            num_out[chunk, i] = part[:HALF].astype(BF16)
            for j in range(2):
                nyquist = jnp.where(
                    row8 == 4 * i + 2 * chunk + j,
                    jnp.broadcast_to(part[HALF : HALF + 1, LANES * j : LANES * (j + 1)], row8.shape),
                    nyquist,
                )
        to_others(NUM_ORDER, functools.partial(num_copy, chunk))
        num_copies += [num_copy(chunk, k) for k in FAR]

    def extra(at):
        return pltpu.make_async_remote_copy(
            src_ref=ex_out,
            dst_ref=ex_in.at[at],
            send_sem=ex_send,
            recv_sem=ex_recv.at[at],
            device_id={"exp": 2 * CHIPS - 1},
            device_id_type=MESH,
        )

    ex_out[...] = jnp.concatenate([nyquist, jnp.zeros_like(nyquist)], axis=0).astype(BF16)

    @pl.when((p == 1) & (z < CHIPS - 1))
    def _():
        extra(z).start()

    for copy in psf_copies:
        copy.wait_recv()
    start = pl.multiple_of(BLK * z, BLK)
    pgz = jnp.concatenate(
        [
            pgt[p, pl.ds(start, BLK), :],
            pgt[p, HALF:ROWS, :],
            pgt[p, pl.ds(pl.multiple_of(start + ROWS, BLK), BLK), :],
            pgt[p, ROWS + HALF :, :],
        ],
        axis=0,
    )
    lane_d = lax.broadcasted_iota(jnp.int32, (4 * BLK, 128), 1) // PS

    def add_den(g, den):
        lift = dot(pgz, psf_all[g, 0:PS, :])
        weights = jnp.sum(psf_all[g, PS : PS + BLK, :].astype(F32), axis=0, keepdims=True)
        ones = [jnp.where(lane_d == t, lift, 0.0).astype(BF16) for t in range(4)]
        lhs = jnp.concatenate(
            [jnp.concatenate([one[: 2 * BLK], one[2 * BLK :]], axis=1) for one in ones], axis=0
        )
        otf = dot(lhs, pgw[...])
        power = otf[:, :TILE] * otf[:, :TILE] + otf[:, TILE:] * otf[:, TILE:]
        for t in range(4):
            den = den + weights[:, PS * t : PS * t + 1] * power[2 * BLK * t : 2 * BLK * (t + 1)]
        return den

    den = lax.fori_loop(0, CHIPS, add_den, jnp.zeros((2 * BLK, TILE), F32))

    ex_sum[...] = jnp.zeros_like(ex_sum)

    @pl.when(group == 2 * CHIPS - 1)
    def _():
        for t in range(CHIPS - 1):
            extra(t).wait_recv()
        total = nyquist
        for t in range(CHIPS - 1):
            total = total + ex_in[t].astype(F32)[:8]
        for i in range(8):
            ex_sum[i // 4, 0:1, LANES * (i % 4) : LANES * (i % 4 + 1)] = total[i : i + 1]

    norm = lax.rsqrt(den + 1.0)
    loads[15].wait()
    loads[16].wait()
    lane0 = lax.broadcasted_iota(jnp.int32, (2 * BLK, LANES), 1) == 0
    t_all = None
    for chunk in range(2):
        cols = slice(SIDE * chunk, SIDE * chunk + SIDE)
        sums = num_own[:, pl.ds(start, BLK), cols]
        for k, copy in list(zip(FAR, num_copies[len(FAR) * chunk :]))[::-1]:
            copy.wait_recv()
            sums = sums + num_in[chunk, k].astype(F32)
        s_re, s_im = (jnp.concatenate([sums[i], ex_sum[i, :, cols]], axis=0) * norm[:, cols] for i in range(2))
        (re_p, re_m), (im_p, im_m) = ((x[:, :LANES], x[:, LANES:]) for x in (s_re, s_im))
        even, odd = [re_p + re_m, im_p + im_m], [im_m - im_p, re_p - re_m]
        if chunk == 0:
            even = [jnp.where(lane0, a, b) for a, b in zip((re_p, im_p), even)]
            odd = [jnp.where(lane0, a, b) for a, b in zip((re_m, im_m), odd)]
        folded = jnp.concatenate([jnp.concatenate(pair, axis=1) for pair in zip(even, odd)], axis=0)
        part = dot(folded.astype(BF16), ytab[cols, :])
        t_all = part if chunk == 0 else t_all + part
    t_own[...] = t_all.astype(BF16)
    t_pair = remote(t_own, t_sib, sib_send.at[3], sib_recv.at[3], sib)
    image = dot(xtab[0], t_own[...])
    t_pair.wait_recv()
    image = image + dot(xtab[1], t_sib[...])

    def part_copy(k):
        return describe(
            part_out.at[(z + k) % CHIPS], out.at[k], part_send.at[k], part_recv.at[k], {"exp": along(k)}
        )

    for t in PART_ORDER:
        block = image[OUT * t : OUT * (t + 1)]
        part_out[t] = jnp.concatenate(
            [block[:, LANES * i : LANES * (i + 1)] for i in range(3)] + [jnp.zeros((PACK - 3 * OUT, LANES), F32)], axis=0
        ).astype(BF16)
        to_others((t,), part_copy)
    parts = [part_copy(k) for k in FAR]
    mine = pltpu.make_async_copy(part_out.at[z], out.at[0], load_sem.at[0])
    mine.start()
    mine.wait()
    for i, copy in halos:
        pl.when(inside[i])(copy.wait_send)
    for copy in psf_copies + num_pairs + [psf_pair, t_pair] + num_copies:
        copy.wait_send()

    @pl.when((p == 1) & (z < CHIPS - 1))
    def _():
        extra(z).wait_send()

    for copy in parts:
        copy.wait_recv()
    for copy in parts:
        copy.wait_send()


def finish(parts, out):
    total = jnp.sum(parts[...].astype(F32), axis=0)
    for i in range(3):
        out[0, :, LANES * i : LANES * (i + 1)] = total[OUT * i : OUT * (i + 1)]


def body(stamps, footprint, psf_anchor, psf_degree, psf_powers, psf_basis, flux, variance):
    ftab, wtab, pgt, pgw, ytab, xtab, taper = (jnp.asarray(t) for t in tables())
    vmem = pl.BlockSpec(memory_space=pltpu.VMEM)
    hbm = pl.BlockSpec(memory_space=pl.ANY)
    dma = pltpu.SemaphoreType.DMA
    parts = pl.pallas_call(
        kernel,
        out_shape=pltpu.VMEM((CHIPS, PACK, 128), BF16),
        in_specs=[hbm] * 15,
        out_specs=hbm,
        scratch_shapes=[
            pltpu.SMEM((2, 4), jnp.int32),
            pltpu.SMEM((2, 2), jnp.int32),
            pltpu.SMEM((2,), jnp.int32),
            pltpu.SMEM((2, 2, NBASIS), jnp.int32),
            pltpu.SMEM((2,), F32),
            pltpu.SMEM((2,), F32),
            pltpu.VMEM((NBASIS, 2, PS * PS), F32),
            pltpu.VMEM(pgt.shape, BF16),
            pltpu.VMEM(taper.shape, F32),
            pltpu.VMEM((2, 2, CORE, 128), BF16),
            pltpu.VMEM((2, 2, ROWS, 2 * TILE), F32),
            pltpu.VMEM((2, 2, ROWS, SIDE), F32),
            pltpu.VMEM((2, 2 * HALO, CORE), BF16),
            pltpu.VMEM((2, 2, CORE // 2, 128), BF16),
            pltpu.VMEM((2, 2, CORE // 2, 128), BF16),
            pltpu.VMEM((2, 2, HALO, 128), BF16),
            pltpu.VMEM((2, 2, HALO, 128), BF16),
            pltpu.VMEM((2, TILE, TILE), BF16),
            pltpu.VMEM(ftab.shape, BF16),
            pltpu.VMEM(wtab.shape, BF16),
            pltpu.VMEM(pgw.shape, BF16),
            pltpu.VMEM(ytab.shape, BF16),
            pltpu.VMEM(xtab.shape[1:], BF16),
            pltpu.VMEM((PS + BLK, 128), BF16),
            pltpu.VMEM((PS + BLK, 128), BF16),
            pltpu.VMEM((CHIPS, PS + BLK, 128), BF16),
            pltpu.VMEM((2, 2, ROWS, SIDE), BF16),
            pltpu.VMEM((2, 2, ROWS, SIDE), BF16),
            pltpu.VMEM((2, ROWS, TILE), F32),
            pltpu.VMEM((2, 2, HALF, SIDE), BF16),
            pltpu.VMEM((2, CHIPS, 2, BLK, SIDE), BF16),
            pltpu.VMEM((BLK, LANES), BF16),
            pltpu.VMEM((CHIPS - 1, BLK, LANES), BF16),
            pltpu.VMEM((2, BLK, TILE), F32),
            pltpu.VMEM((4 * BLK, CORE), BF16),
            pltpu.VMEM((4 * BLK, CORE), BF16),
            pltpu.VMEM((CHIPS, PACK, 128), BF16),
            dma((17,)),
            dma((12,)),
            dma((12,)),
            dma((4,)),
            dma((4,)),
            dma((CHIPS,)),
            dma((CHIPS,)),
            dma((2, CHIPS)),
            dma((2, CHIPS)),
            dma,
            dma((CHIPS - 1,)),
            dma((CHIPS,)),
            dma((CHIPS,)),
            pltpu.SemaphoreType.REGULAR((CHIPS,)),
        ],
        compiler_params=pltpu.CompilerParams(
            collective_id=0, has_side_effects=True, vmem_limit_bytes=64 * 1024 * 1024 - 512 * 1024
        ),
    )(
        footprint, psf_anchor, psf_degree, psf_powers.transpose(0, 2, 1), flux, variance,
        psf_basis.transpose(1, 0, 2), pgt, taper,
        stamps, ftab, wtab, pgw, ytab, xtab,
    )
    parts = pltpu.with_memory_space_constraint(parts, pltpu.VMEM)
    return pl.pallas_call(
        finish, out_shape=jax.ShapeDtypeStruct((1, OUT, CORE), F32), in_specs=[vmem], out_specs=vmem
    )(parts)


def solution(mesh):
    in_specs = (
        P("exp", "trow", "tcol"),
        P("exp", None),
        P("exp", None),
        P("exp"),
        P("exp", None, None),
        P("exp", None, None),
        P("exp"),
        P("exp"),
    )
    out_specs = P("trow", "exp", "tcol")
    return jax.shard_map(body, mesh=mesh, in_specs=in_specs, out_specs=out_specs, check_vma=False)
```

```python
import functools
import math

import jax
import jax.numpy as jnp
import ml_dtypes
import numpy as np
from jax import lax
from jax.experimental import pallas as pl
from jax.experimental.pallas import tpu as pltpu
from jax.sharding import PartitionSpec as P

TILE = 512
HALO = 64
PS = 32
NBASIS = 10
CORE = 384
CHIPS = 8
SIDE = TILE // 2
LANES = 128
FAR = (4, 3, 5, 2, 6, 1, 7)
NUM_ORDER = (2, 1, 3, 4, 0, 5, 6, 7)
PART_ORDER = (0, 1, 2, 3, 4, 5, 6, 7)
BLK = 16
HALF = CHIPS * BLK
ROWS = HALF + BLK
OUT = CORE // (2 * CHIPS)
PACK = 80
MESH = pl.DeviceIdType.MESH
F32 = jnp.float32
BF16 = jnp.bfloat16


def angles(a, b):
    return (a[:, None] * b[None, :] % TILE) * (2.0 * math.pi / TILE)


@functools.cache
def tables():
    freq = np.arange(TILE)
    pixel = (freq + HALO) % TILE
    offset = np.arange(PS) - PS // 2
    scale = 1.0 / math.sqrt(TILE)

    def bf(x):
        return np.asarray(x, np.float32).astype(ml_dtypes.bfloat16)

    rows = [np.arange(HALF * q, HALF * q + ROWS) for q in range(2)]
    live = [(u <= TILE // 2)[:, None] for u in rows]
    ftab = np.stack(
        [
            np.concatenate([np.cos(angles(u, pixel)) * k, -np.sin(angles(u, pixel)) * k]) * scale
            for u, k in zip(rows, live)
        ]
    )
    cos, sin = np.cos(angles(pixel, freq[:SIDE])), -np.sin(angles(pixel, freq[:SIDE]))
    sin[:, 0] = np.cos(angles(pixel, freq[SIDE : SIDE + 1]))[:, 0]
    wtab = np.concatenate([cos[:, :LANES], sin[:, :LANES], cos[:, LANES:], sin[:, LANES:]], 1) * scale
    pgt = np.stack(
        [np.concatenate([np.cos(angles(u, offset)) * k, -np.sin(angles(u, offset)) * k]) for u, k in zip(rows, live)]
    )
    minus = np.concatenate([freq[SIDE : SIDE + 1], freq[:SIDE:-1]])
    order = np.concatenate([freq[:LANES], minus[:LANES], freq[LANES:SIDE], minus[LANES:]])
    cos, sin = np.cos(angles(offset, order)), np.sin(angles(offset, order))
    cos, sin = np.tile(cos, (4, 1)), np.tile(sin, (4, 1))
    pgw = np.block([[cos, -sin], [sin, cos]])
    core = np.arange(CORE) + HALO
    cos, sin = np.cos(angles(freq[:SIDE], core)), np.sin(angles(freq[:SIDE], core))
    sin[0] = np.cos(angles(freq[SIDE : SIDE + 1], core))[0]
    ytab = np.concatenate([cos[:LANES], sin[:LANES], cos[LANES:], sin[LANES:]]) * scale
    xtab = np.zeros((2 * CHIPS, 2, CHIPS * OUT, 4 * BLK))
    for z in range(CHIPS):
        for p in range(2):
            x = np.concatenate([OUT * (2 * t + p) + np.arange(OUT) for t in range(CHIPS)]) + HALO
            for side in range(2):
                q = p ^ side
                u = np.concatenate([q * HALF + BLK * z + np.arange(BLK), TILE // 2 + np.arange(BLK)])
                count = np.where((u == 0) | (u == TILE // 2), 1.0, 2.0)
                count[BLK:] = 0.0
                if z == CHIPS - 1 and q == 1:
                    count[BLK] = 1.0
                xtab[2 * z + p, side, :, : 2 * BLK] = np.cos(angles(x, u)) * scale * count
                xtab[2 * z + p, side, :, 2 * BLK :] = -np.sin(angles(x, u)) * scale * count
    edge = np.arange(HALO)
    dist = np.concatenate([HALO - 1 - edge, edge])
    line = np.sin(0.5 * math.pi * (dist + 0.5) / HALO) ** 2
    taper = np.stack([np.tile(line[:, None], (1, 128)), np.tile(line[None, :], (128, 1))]).astype(np.float32)
    return bf(ftab), bf(wtab), bf(pgt), bf(pgw), bf(ytab), bf(xtab), taper


def monomial(value, power):
    return jnp.where(
        power == 0,
        1.0,
        jnp.where(power == 1, value, jnp.where(power == 2, value * value, value * value * value)),
    )


def dot(a, b):
    return jnp.dot(a, b, preferred_element_type=F32)


def kernel(
    foot_h, anchor_h, degree_h, powers_h, flux_h, variance_h, basis_h, pgt_h, taper_h, stamps, ftab_h, wtab_h, pgw_h,
    ytab_h, xtab_h,
    out,
    foot, anchor, degree, powers, flux, variance, basis, pgt, taper, strip, otf_all, num_first, rowh, cols, cols_in, corners,
    corners_in, ap, ftab, wtab, pgw, ytab, xtab,
    psf_own, psf_sib, psf_all, num_sib_out, num_sib_in, num_own, num_out, num_in, ex_out, ex_in, ex_sum,
    t_own, t_sib, part_out,
    load_sem, halo_send, halo_recv, sib_send, sib_recv, psf_send, psf_recv, num_send, num_recv,
    ex_send, ex_recv, part_send, part_recv, ready,
):
    group = lax.axis_index("exp")
    r = lax.axis_index("trow")
    c = lax.axis_index("tcol")
    z = group // 2
    p = group % 2
    sib = {"exp": group + 1 - 2 * p}

    def along(k):
        return 2 * ((z + k) % CHIPS) + p

    def near(dr, dc):
        return {"trow": (r + dr + 4) % 4, "tcol": (c + dc + 4) % 4}

    around = [(-1, -1), (-1, 1), (0, -1), (-1, 0), (1, 0), (0, 1), (1, -1), (1, 1)]
    inside = [(r + dr >= 0) & (r + dr < 4) & (c + dc >= 0) & (c + dc < 4) for dr, dc in around]
    barrier = pltpu.get_barrier_semaphore()
    for at, there in zip(around, inside):

        @pl.when(there)
        def _():
            pl.semaphore_signal(barrier, inc=1, device_id=near(*at), device_id_type=MESH)

    for k in FAR:

        @pl.when((z + k) % CHIPS > z)
        def _():
            pl.semaphore_signal(barrier, inc=1, device_id={"exp": along(k)}, device_id_type=MESH)

    pl.semaphore_signal(barrier, inc=1, device_id=sib, device_id_type=MESH)
    loads = []
    for i, (src, dst) in enumerate(
        [
            (stamps.at[:, :, pl.ds(0, 128)], strip.at[0]), (stamps.at[:, :, pl.ds(CORE - 128, 128)], strip.at[1]),
            (foot_h, foot), (anchor_h, anchor), (degree_h, degree), (powers_h, powers),
            (flux_h, flux), (variance_h, variance), (basis_h, basis), (pgt_h, pgt), (pgw_h, pgw),
            (stamps, ap.at[:, pl.ds(0, CORE), pl.ds(0, CORE)]), (taper_h, taper), (ftab_h, ftab), (wtab_h, wtab),
            (ytab_h, ytab), (xtab_h.at[group], xtab),
        ]
    ):
        load = pltpu.make_async_copy(src, dst, load_sem.at[i])
        load.start()
        loads.append(load)

    def describe(src, dst, send, recv, where):
        return pltpu.make_async_remote_copy(
            src_ref=src, dst_ref=dst, send_sem=send, recv_sem=recv, device_id=where, device_id_type=MESH
        )

    def remote(*args):
        copy = describe(*args)
        copy.start()
        return copy

    def to_others(chips, copy):
        for chip in chips:
            pl.when(z != chip)(lambda chip=chip: copy((chip - z + CHIPS) % CHIPS).start())

    loads[0].wait()
    loads[1].wait()
    low = lax.broadcasted_iota(jnp.int32, (CORE // 2, 128), 1) < HALO
    turned = [[pltpu.roll(strip[side, e].astype(F32), HALO, 1) for e in range(2)] for side in range(2)]
    for e in range(2):
        cols[0, e] = jnp.where(low, strip[0, e, : CORE // 2].astype(F32), turned[0][e][CORE // 2 :]).astype(BF16)
        cols[1, e] = jnp.where(low, turned[1][e][: CORE // 2], strip[1, e, CORE // 2 :].astype(F32)).astype(BF16)
    for i, rows in enumerate((slice(0, HALO), slice(CORE - HALO, CORE))):
        corners[i, 0] = jnp.where(low[:HALO], strip[0, 0, rows].astype(F32), turned[0][1][rows]).astype(BF16)
        corners[i, 1] = jnp.where(low[:HALO], turned[1][0][rows], strip[1, 1, rows].astype(F32)).astype(BF16)
    pl.semaphore_wait(barrier, sum(there.astype(jnp.int32) for there in inside) + 1 + z)
    pieces = [
        (0, corners.at[0, 0], corners_in.at[0, 0]),
        (1, corners.at[0, 1], corners_in.at[0, 1]),
        (6, corners.at[1, 0], corners_in.at[1, 0]),
        (7, corners.at[1, 1], corners_in.at[1, 1]),
    ]
    for e in range(2):
        pieces += [
            (2, cols.at[0, e], cols_in.at[0, e]),
            (5, cols.at[1, e], cols_in.at[1, e]),
            (3, stamps.at[e, pl.ds(0, HALO), :], rowh.at[e, pl.ds(0, HALO), :]),
            (4, stamps.at[e, pl.ds(CORE - HALO, HALO), :], rowh.at[e, pl.ds(HALO, HALO), :]),
        ]
    halos = [
        (i, describe(src, dst, halo_send.at[n], halo_recv.at[n], near(*around[i])))
        for n, (i, src, dst) in enumerate(pieces)
    ]
    for i, copy in halos:
        pl.when(inside[i])(copy.start)
    for k in FAR:

        @pl.when((z + k) % CHIPS < z)
        def _():
            pl.semaphore_signal(ready.at[CHIPS - k], inc=1, device_id={"exp": along(k)}, device_id_type=MESH)

    for i, _, dst in pieces:

        @pl.when(jnp.logical_not(inside[7 - i]))
        def _():
            dst[...] = jnp.zeros(dst.shape, BF16)

    for load in loads[2:9]:
        load.wait()

    lane32 = lax.broadcasted_iota(jnp.int32, (PS, 128), 1)
    row32 = lax.broadcasted_iota(jnp.int32, (PS, 128), 0)
    slot32 = lane32 // PS
    fold = jnp.where(
        lax.broadcasted_iota(jnp.int32, (128, 128), 0) % PS == lax.broadcasted_iota(jnp.int32, (128, 128), 1) % PS,
        1.0,
        0.0,
    ).astype(BF16)
    lane16 = lax.broadcasted_iota(jnp.int32, (BLK, 128), 1) // PS
    row16 = lax.broadcasted_iota(jnp.int32, (BLK, 128), 0)
    psf = jnp.zeros((PS, 128), F32)
    wrow = jnp.zeros((BLK, 128), F32)
    wnum = []
    for e in range(2):
        ux = (c * CORE + CORE // 2 - anchor[e, 1]).astype(F32) / (2.0 * CORE)
        uy = (r * CORE + CORE // 2 - anchor[e, 0]).astype(F32) / (2.0 * CORE)
        flat = jnp.zeros((1, PS * PS), F32)
        for k in range(NBASIS):
            px, qy = powers[e, 0, k], powers[e, 1, k]
            term = jnp.where(px + qy <= degree[e], monomial(ux, px) * monomial(uy, qy), 0.0)
            flat = flat + term * basis[k, e : e + 1, :]
        spread = jnp.zeros((PS, 128), F32)
        for t in range(PS * PS // 128):
            spread = jnp.where(
                (row32 // 4 == t) & (slot32 == row32 % 4),
                jnp.broadcast_to(flat[:, 128 * t : 128 * t + 128], (PS, 128)),
                spread,
            )
        mine = 2 * p + e
        psf = jnp.where(slot32 == mine, dot(spread.astype(BF16), fold), psf)
        active = (foot[e, 0] <= r) & (r < foot[e, 1]) & (foot[e, 2] <= c) & (c < foot[e, 3])
        gain = jnp.where(active, flux[e], 0.0)
        wnum.append(jnp.full((8, 128), gain, F32) / jnp.full((8, 128), variance[e], F32))
        wden = jnp.full((BLK, 128), gain * flux[e], F32) / jnp.full((BLK, 128), variance[e], F32)
        wrow = jnp.where(lane16 == mine, wden, wrow)
    high = wrow.astype(BF16).astype(F32)
    rest = wrow - high
    mid = rest.astype(BF16).astype(F32)
    wrow = jnp.where(row16 == 0, high, jnp.where(row16 == 1, mid, jnp.where(row16 == 2, rest - mid, 0.0)))
    psf_own[0:PS, :] = psf.astype(BF16)
    psf_own[PS : PS + BLK, :] = wrow.astype(BF16)
    psf_pair = remote(psf_own, psf_sib, sib_send.at[0], sib_recv.at[0], sib)


    loads[9].wait()
    loads[10].wait()
    stamp = psf_own[0:PS, :]
    lane_r = lax.broadcasted_iota(jnp.int32, (2 * ROWS, 128), 1) // PS
    for side in range(2):
        lift = dot(pgt[1 - p if side == 0 else p], stamp)
        for e in range(2):
            one = jnp.where(lane_r == 2 * p + e, lift, 0.0).astype(BF16)
            otf_all[side, e] = dot(jnp.concatenate([one[:ROWS], one[ROWS:]], axis=1), pgw[...])

    for load in loads[11:15]:
        load.wait()
    lane_s = lax.broadcasted_iota(jnp.int32, (CORE, 128), 1) < HALO
    line_r = taper[0]
    line_c = taper[1]
    wide = jnp.concatenate([line_r] * 3, axis=1)

    def apodize(e):
        for i, copy in halos[4 + 4 * e : 8 + 4 * e]:
            pl.when(inside[7 - i])(copy.wait_recv)
        up, down, after, before = [
            jnp.where((foot[e, lo] <= at) & (at < foot[e, lo + 1]), 1.0, 0.0)
            for lo, at in ((0, r + 1), (0, r - 1), (2, c + 1), (2, c - 1))
        ]
        ap[e, CORE : CORE + HALO, 0:CORE] = (rowh[e, 0:HALO, :].astype(F32) * (wide[0:HALO] * up)).astype(BF16)
        ap[e, CORE + HALO : TILE, 0:CORE] = (rowh[e, HALO:, :].astype(F32) * (wide[HALO:] * down)).astype(BF16)
        right, left = cols_in[0, e].astype(F32), cols_in[1, e].astype(F32)
        side = jnp.concatenate(
            [jnp.where(low, right, pltpu.roll(left, HALO, 1)), jnp.where(low, pltpu.roll(right, HALO, 1), left)], axis=0
        )
        keep = jnp.where(lane_s, after, before)
        ap[e, 0:CORE, CORE:TILE] = (side * (jnp.concatenate([line_c] * 3, axis=0) * keep)).astype(BF16)
        for i, rows in enumerate((slice(0, HALO), slice(HALO, 2 * HALO))):
            right, left = corners_in[i, 0].astype(F32), corners_in[i, 1].astype(F32)
            if e == 0:
                corner = jnp.where(low[:HALO], right, pltpu.roll(left, HALO, 1))
            else:
                corner = jnp.where(low[:HALO], pltpu.roll(right, HALO, 1), left)
            taper2 = line_r[rows] * line_c[rows] * keep[:HALO] * (up if i == 0 else down)
            ap[e, CORE + HALO * i : CORE + HALO * (i + 1), CORE:TILE] = (corner * taper2).astype(BF16)

    lane0 = lax.broadcasted_iota(jnp.int32, (ROWS, LANES), 1) == 0

    def halved(q, e):
        return dot(ftab[q], ap[e]).astype(BF16)

    def numerator(half, side, chunk, e):
        cols = slice(SIDE * chunk, SIDE * chunk + SIDE)
        prod = dot(half, wtab[:, cols])
        re_cos, re_sin = prod[:ROWS, :LANES], prod[:ROWS, LANES:]
        im_cos, im_sin = prod[ROWS:, :LANES], prod[ROWS:, LANES:]
        if chunk == 0:
            plus = [re_cos - jnp.where(lane0, 0.0, im_sin), im_cos + jnp.where(lane0, 0.0, re_sin)]
            minus = [jnp.where(lane0, re_sin, re_cos + im_sin), jnp.where(lane0, im_sin, im_cos - re_sin)]
        else:
            plus = [re_cos - im_sin, im_cos + re_sin]
            minus = [re_cos + im_sin, im_cos - re_sin]
        spec_re, spec_im = (jnp.concatenate(pair, axis=1) for pair in zip(plus, minus))
        otf_re = otf_all[side, e, :, cols]
        otf_im = otf_all[side, e, :, TILE + SIDE * chunk : TILE + SIDE * chunk + SIDE]
        w = wnum[e][0:1, 0:1]
        return w * (otf_re * spec_re + otf_im * spec_im), w * (otf_re * spec_im - otf_im * spec_re)

    def num_copy(chunk, k):
        return describe(
            num_out.at[chunk, :, pl.ds(pl.multiple_of(BLK * ((z + k) % CHIPS), BLK), BLK), :],
            num_in.at[chunk, k],
            num_send.at[chunk, k],
            num_recv.at[chunk, k],
            {"exp": along(k)},
        )

    psf_pair.wait_recv()
    psf_all[0] = (psf_own[...].astype(F32) + psf_sib[...].astype(F32)).astype(BF16)
    psf_copies = [
        describe(psf_all.at[0], psf_all.at[k], psf_send.at[k], psf_recv.at[k], {"exp": along(k)}) for k in FAR
    ]
    for k, copy in zip(FAR, psf_copies):
        pl.when((z + k) % CHIPS < z)(copy.start)
    for i, copy in halos[:4]:
        pl.when(inside[7 - i])(copy.wait_recv)
    apodize(0)
    half = halved(1 - p, 0)
    for chunk in range(2):
        for i, part in enumerate(numerator(half, 0, chunk, 0)):
            num_first[chunk, i] = part
    apodize(1)
    half = halved(1 - p, 1)
    num_pairs = []
    for chunk in range(2):
        for i, part in enumerate(numerator(half, 0, chunk, 1)):
            num_sib_out[chunk, i] = (num_first[chunk, i] + part).astype(BF16)
        num_pairs.append(
            remote(num_sib_out.at[chunk], num_sib_in.at[chunk], sib_send.at[1 + chunk], sib_recv.at[1 + chunk], sib)
        )
    for k, copy in zip(FAR, psf_copies):

        @pl.when((z + k) % CHIPS > z)
        def _():
            pl.semaphore_wait(ready.at[k], 1)
            copy.start()

    half = [halved(p, e) for e in range(2)]
    num_copies = []
    row8 = lax.broadcasted_iota(jnp.int32, (8, LANES), 0)
    nyquist = jnp.zeros((8, LANES), F32)
    for chunk in range(2):
        parts = [a + b for a, b in zip(*(numerator(half[e], 1, chunk, e) for e in range(2)))]
        num_pairs[chunk].wait_recv()
        for i, part in enumerate(parts):
            part = part + num_sib_in[chunk, i].astype(F32)
            num_own[i, :, SIDE * chunk : SIDE * chunk + SIDE] = part
            num_out[chunk, i] = part[:HALF].astype(BF16)
            for j in range(2):
                nyquist = jnp.where(
                    row8 == 4 * i + 2 * chunk + j,
                    jnp.broadcast_to(part[HALF : HALF + 1, LANES * j : LANES * (j + 1)], row8.shape),
                    nyquist,
                )
        to_others(NUM_ORDER, functools.partial(num_copy, chunk))
        num_copies += [num_copy(chunk, k) for k in FAR]

    def extra(at):
        return pltpu.make_async_remote_copy(
            src_ref=ex_out,
            dst_ref=ex_in.at[at],
            send_sem=ex_send,
            recv_sem=ex_recv.at[at],
            device_id={"exp": 2 * CHIPS - 1},
            device_id_type=MESH,
        )

    ex_out[...] = jnp.concatenate([nyquist, jnp.zeros_like(nyquist)], axis=0).astype(BF16)

    @pl.when((p == 1) & (z < CHIPS - 1))
    def _():
        extra(z).start()

    for copy in psf_copies:
        copy.wait_recv()
    start = pl.multiple_of(BLK * z, BLK)
    pgz = jnp.concatenate(
        [
            pgt[p, pl.ds(start, BLK), :],
            pgt[p, HALF:ROWS, :],
            pgt[p, pl.ds(pl.multiple_of(start + ROWS, BLK), BLK), :],
            pgt[p, ROWS + HALF :, :],
        ],
        axis=0,
    )
    lane_d = lax.broadcasted_iota(jnp.int32, (4 * BLK, 128), 1) // PS

    def add_den(g, den):
        lift = dot(pgz, psf_all[g, 0:PS, :])
        weights = jnp.sum(psf_all[g, PS : PS + BLK, :].astype(F32), axis=0, keepdims=True)
        ones = [jnp.where(lane_d == t, lift, 0.0).astype(BF16) for t in range(4)]
        lhs = jnp.concatenate(
            [jnp.concatenate([one[: 2 * BLK], one[2 * BLK :]], axis=1) for one in ones], axis=0
        )
        otf = dot(lhs, pgw[...])
        power = otf[:, :TILE] * otf[:, :TILE] + otf[:, TILE:] * otf[:, TILE:]
        for t in range(4):
            den = den + weights[:, PS * t : PS * t + 1] * power[2 * BLK * t : 2 * BLK * (t + 1)]
        return den

    den = lax.fori_loop(0, CHIPS, add_den, jnp.zeros((2 * BLK, TILE), F32))

    ex_sum[...] = jnp.zeros_like(ex_sum)

    @pl.when(group == 2 * CHIPS - 1)
    def _():
        for t in range(CHIPS - 1):
            extra(t).wait_recv()
        total = nyquist
        for t in range(CHIPS - 1):
            total = total + ex_in[t].astype(F32)[:8]
        for i in range(8):
            ex_sum[i // 4, 0:1, LANES * (i % 4) : LANES * (i % 4 + 1)] = total[i : i + 1]

    norm = lax.rsqrt(den + 1.0)
    loads[15].wait()
    loads[16].wait()
    lane0 = lax.broadcasted_iota(jnp.int32, (2 * BLK, LANES), 1) == 0
    t_all = None
    for chunk in range(2):
        cols = slice(SIDE * chunk, SIDE * chunk + SIDE)
        sums = num_own[:, pl.ds(start, BLK), cols]
        for k, copy in list(zip(FAR, num_copies[len(FAR) * chunk :]))[::-1]:
            copy.wait_recv()
            sums = sums + num_in[chunk, k].astype(F32)
        s_re, s_im = (jnp.concatenate([sums[i], ex_sum[i, :, cols]], axis=0) * norm[:, cols] for i in range(2))
        (re_p, re_m), (im_p, im_m) = ((x[:, :LANES], x[:, LANES:]) for x in (s_re, s_im))
        even, odd = [re_p + re_m, im_p + im_m], [im_m - im_p, re_p - re_m]
        if chunk == 0:
            even = [jnp.where(lane0, a, b) for a, b in zip((re_p, im_p), even)]
            odd = [jnp.where(lane0, a, b) for a, b in zip((re_m, im_m), odd)]
        folded = jnp.concatenate([jnp.concatenate(pair, axis=1) for pair in zip(even, odd)], axis=0)
        part = dot(folded.astype(BF16), ytab[cols, :])
        t_all = part if chunk == 0 else t_all + part
    t_own[...] = t_all.astype(BF16)
    t_pair = remote(t_own, t_sib, sib_send.at[3], sib_recv.at[3], sib)
    image = dot(xtab[0], t_own[...])
    t_pair.wait_recv()
    image = image + dot(xtab[1], t_sib[...])

    def part_copy(k):
        return describe(
            part_out.at[(z + k) % CHIPS], out.at[k], part_send.at[k], part_recv.at[k], {"exp": along(k)}
        )

    for t in PART_ORDER:
        block = image[OUT * t : OUT * (t + 1)]
        part_out[t] = jnp.concatenate(
            [block[:, LANES * i : LANES * (i + 1)] for i in range(3)] + [jnp.zeros((PACK - 3 * OUT, LANES), F32)], axis=0
        ).astype(BF16)
        to_others((t,), part_copy)
    parts = [part_copy(k) for k in FAR]
    mine = pltpu.make_async_copy(part_out.at[z], out.at[0], load_sem.at[0])
    mine.start()
    mine.wait()
    for i, copy in halos:
        pl.when(inside[i])(copy.wait_send)
    for copy in psf_copies + num_pairs + [psf_pair, t_pair] + num_copies:
        copy.wait_send()

    @pl.when((p == 1) & (z < CHIPS - 1))
    def _():
        extra(z).wait_send()

    for copy in parts:
        copy.wait_recv()
    for copy in parts:
        copy.wait_send()


def finish(parts, out):
    total = jnp.sum(parts[...].astype(F32), axis=0)
    for i in range(3):
        out[0, :, LANES * i : LANES * (i + 1)] = total[OUT * i : OUT * (i + 1)]


def body(stamps, footprint, psf_anchor, psf_degree, psf_powers, psf_basis, flux, variance):
    ftab, wtab, pgt, pgw, ytab, xtab, taper = (jnp.asarray(t) for t in tables())
    vmem = pl.BlockSpec(memory_space=pltpu.VMEM)
    hbm = pl.BlockSpec(memory_space=pl.ANY)
    dma = pltpu.SemaphoreType.DMA
    parts = pl.pallas_call(
        kernel,
        out_shape=pltpu.VMEM((CHIPS, PACK, 128), BF16),
        in_specs=[hbm] * 15,
        out_specs=hbm,
        scratch_shapes=[
            pltpu.SMEM((2, 4), jnp.int32),
            pltpu.SMEM((2, 2), jnp.int32),
            pltpu.SMEM((2,), jnp.int32),
            pltpu.SMEM((2, 2, NBASIS), jnp.int32),
            pltpu.SMEM((2,), F32),
            pltpu.SMEM((2,), F32),
            pltpu.VMEM((NBASIS, 2, PS * PS), F32),
            pltpu.VMEM(pgt.shape, BF16),
            pltpu.VMEM(taper.shape, F32),
            pltpu.VMEM((2, 2, CORE, 128), BF16),
            pltpu.VMEM((2, 2, ROWS, 2 * TILE), F32),
            pltpu.VMEM((2, 2, ROWS, SIDE), F32),
            pltpu.VMEM((2, 2 * HALO, CORE), BF16),
            pltpu.VMEM((2, 2, CORE // 2, 128), BF16),
            pltpu.VMEM((2, 2, CORE // 2, 128), BF16),
            pltpu.VMEM((2, 2, HALO, 128), BF16),
            pltpu.VMEM((2, 2, HALO, 128), BF16),
            pltpu.VMEM((2, TILE, TILE), BF16),
            pltpu.VMEM(ftab.shape, BF16),
            pltpu.VMEM(wtab.shape, BF16),
            pltpu.VMEM(pgw.shape, BF16),
            pltpu.VMEM(ytab.shape, BF16),
            pltpu.VMEM(xtab.shape[1:], BF16),
            pltpu.VMEM((PS + BLK, 128), BF16),
            pltpu.VMEM((PS + BLK, 128), BF16),
            pltpu.VMEM((CHIPS, PS + BLK, 128), BF16),
            pltpu.VMEM((2, 2, ROWS, SIDE), BF16),
            pltpu.VMEM((2, 2, ROWS, SIDE), BF16),
            pltpu.VMEM((2, ROWS, TILE), F32),
            pltpu.VMEM((2, 2, HALF, SIDE), BF16),
            pltpu.VMEM((2, CHIPS, 2, BLK, SIDE), BF16),
            pltpu.VMEM((BLK, LANES), BF16),
            pltpu.VMEM((CHIPS - 1, BLK, LANES), BF16),
            pltpu.VMEM((2, BLK, TILE), F32),
            pltpu.VMEM((4 * BLK, CORE), BF16),
            pltpu.VMEM((4 * BLK, CORE), BF16),
            pltpu.VMEM((CHIPS, PACK, 128), BF16),
            dma((17,)),
            dma((12,)),
            dma((12,)),
            dma((4,)),
            dma((4,)),
            dma((CHIPS,)),
            dma((CHIPS,)),
            dma((2, CHIPS)),
            dma((2, CHIPS)),
            dma,
            dma((CHIPS - 1,)),
            dma((CHIPS,)),
            dma((CHIPS,)),
            pltpu.SemaphoreType.REGULAR((CHIPS,)),
        ],
        compiler_params=pltpu.CompilerParams(
            collective_id=0, has_side_effects=True, vmem_limit_bytes=64 * 1024 * 1024 - 512 * 1024
        ),
    )(
        footprint, psf_anchor, psf_degree, psf_powers.transpose(0, 2, 1), flux, variance,
        psf_basis.transpose(1, 0, 2), pgt, taper,
        stamps, ftab, wtab, pgw, ytab, xtab,
    )
    parts = pltpu.with_memory_space_constraint(parts, pltpu.VMEM)
    return pl.pallas_call(
        finish, out_shape=jax.ShapeDtypeStruct((1, OUT, CORE), F32), in_specs=[vmem], out_specs=vmem
    )(parts)


def solution(mesh):
    in_specs = (
        P("exp", "trow", "tcol"),
        P("exp", None),
        P("exp", None),
        P("exp"),
        P("exp", None, None),
        P("exp", None, None),
        P("exp"),
        P("exp"),
    )
    out_specs = P("trow", "exp", "tcol")
    return jax.shard_map(body, mesh=mesh, in_specs=in_specs, out_specs=out_specs, check_vma=False)
```
